32 devices in a mesh: fsdp: 32 (over z, y, x, core).
Axes of the slice: x: 2, y: 2, z: 4, core: 2. Of those that a mesh axis runs over, the one named last changes fastest.
Arguments:
- tokens: bfloat16 [6144, 2048], P('fsdp'), may hold values from -6 to 6
- segments: int32 [96, 64], P('fsdp'), may hold values from 0 to 2, never falling along the last dimension, each value on 1 to 48 neighbouring positions
- micro_live: int32 [32], P('fsdp'), may hold values from 2 to 3, as said below
- cotangent: bfloat16 [6144, 2048], P('fsdp'), may hold values from -6 to 6
- w_query: bfloat16 [2048, 2048], P('fsdp'), may hold values from -0.125 to 0.125
- key_weight: bfloat16 [2048, 1024], P('fsdp'), may hold values from -0.125 to 0.125
- value_weight: bfloat16 [2048, 1024], P('fsdp'), may hold values from -0.125 to 0.125
- w_output: bfloat16 [2048, 2048], P('fsdp'), may hold values from -0.5 to 0.5
- attn_gain: bfloat16 [2048], P('fsdp'), may hold values from 0.5 to 1.5
- query_norm_gain: bfloat16 [128], P('fsdp'), may hold values from 1.09375 to 1.6953125
- key_gain: bfloat16 [128], P('fsdp'), may hold values from 1.09375 to 1.6953125
- w_gate: bfloat16 [2048, 6144], P('fsdp'), may hold values from -0.125 to 0.125
- w_up: bfloat16 [2048, 6144], P('fsdp'), may hold values from -0.125 to 0.125
- w_down: bfloat16 [6144, 2048], P('fsdp'), may hold values from -0.109375 to 0.109375
- mlp_gain: bfloat16 [2048], P('fsdp'), may hold values from 0.5 to 1.5
Outputs:
- layer_out: bfloat16 [6144, 2048], P('fsdp')
- grad_tokens: bfloat16 [6144, 2048], P('fsdp')
- grad_query: float32 [2048, 2048], P('fsdp')
- grad_key: float32 [2048, 1024], P('fsdp')
- value_weight_gradient: float32 [2048, 1024], P('fsdp')
- grad_output: float32 [2048, 2048], P('fsdp')
- grad_attn_gain: float32 [2048], P('fsdp')
- grad_query_gain: float32 [128], P('fsdp')
- grad_key_gain: float32 [128], P('fsdp')
- grad_gate: float32 [2048, 6144], P('fsdp')
- grad_up: float32 [2048, 6144], P('fsdp')
- grad_down: float32 [6144, 2048], P('fsdp')
- grad_mlp_gain: float32 [2048], P('fsdp')
The draws below stay inside these ranges and needn't reach their ends.
Inputs may be any that keep to these rules, and one draw needn't show every extreme that they name: `segments`: within each micro-batch the ids start at 0 and never fall; a document has 1 to 48 rows. `micro_live`: exactly half of the devices have 3 live micro-batches, the others 2.
All inputs are finite; a program needn't handle non-finite values.
Results may differ from the reference program's by a relative error of at most 0.015.
Values may be sent and summed in bfloat16 or wider, within the bound.
A program may use at most 384 MiB of HBM per device.

```python
import math
import jax
import jax.numpy as jnp
import numpy as np
from jax import lax

MODEL_WIDTH = 2048
QUERY_HEADS = 16
KEY_VALUE_HEADS = 8
HEAD_SIZE = 128
FF = 6144
ROWS = 64
MSLOT = 3
MBATCH = 96
TOKENS = 6144
N_FSDP = 32


def device_order(key):
    return jax.random.permutation(key, N_FSDP)


def draw_micro_live(key, part):
    shuffled = device_order(key)
    return (MSLOT - 1 + (shuffled < N_FSDP // 2).astype(jnp.int32)).astype(jnp.int32)


def draw_tokens(key, part):
    key = jax.random.fold_in(key, 11)
    jitter_key = jax.random.fold_in(key, 0)
    return jnp.clip(jax.random.normal(jitter_key, (TOKENS, MODEL_WIDTH), jnp.float32), -6.0, 6.0).astype(jnp.bfloat16)


def draw_cotangent(key, part):
    key = jax.random.fold_in(key, 13)
    jitter_key = jax.random.fold_in(key, 0)
    return jnp.clip(jax.random.normal(jitter_key, (TOKENS, MODEL_WIDTH), jnp.float32), -6.0, 6.0).astype(jnp.bfloat16)


def block_scale(own_key, extent, cuts, low, largest):
    def one(dim, parts):
        steps = jax.random.uniform(jax.random.fold_in(jax.random.fold_in(own_key, 6), dim), (parts,), jnp.float32, low / len(cuts), largest / len(cuts))
        return jnp.repeat(jnp.exp(steps), extent[dim] // parts).reshape((-1,) + (1,) * (len(extent) - dim - 1))

    factor_of = one(*cuts[0])
    for cut in cuts[1:]:
        factor_of = factor_of * one(*cut)
    return factor_of


def profile(count, total, limit, slope):
    weights = [(1 << 20) // math.isqrt(rank ** slope) + 1 for rank in range(2, count + 1)]
    surplus, holding = total - limit - (count - 1), [1] * (count - 1)
    while surplus > 0:
        candidates = [i for i in range(count - 1) if holding[i] < limit]
        mass, left = sum([weights[i] for i in candidates]), surplus
        for i in candidates:
            more = min(limit - holding[i], max(1, left * weights[i] // mass), surplus)
            holding[i] = holding[i] + more
            surplus = surplus - more
    return np.array([limit] + holding)


def uneven(key, count, total, most, slope):
    if count == 2:
        one = jax.random.randint(key, (), max(1, total - most), min(most, total - 1) + 1)
        return jnp.stack([one, total - one])
    sizes = jnp.asarray(profile(count, total, most, slope), jnp.int32)
    couples = (count - 1) // 2
    donor, taker = sizes[1:1 + 2 * couples:2], sizes[2:2 + 2 * couples:2]
    room = jnp.minimum(donor - 1, most - taker)
    moved = jax.random.randint(jax.random.fold_in(key, 1), (couples,), 0, 1 << 20) % (room + 1)
    sizes = sizes.at[1:1 + 2 * couples:2].set(donor - moved).at[2:2 + 2 * couples:2].set(taker + moved)
    return sizes[jax.random.permutation(jax.random.fold_in(key, 2), count)]


def centred(stream_key, dims, spread, most, shards=(), held_as=jnp.bfloat16):
    result = spread * jax.random.normal(stream_key, dims, jnp.float32)
    if shards:
        result = result * block_scale(stream_key, dims, shards, -0.22, 0.18)
    return jnp.clip(result, -most, most).astype(held_as)


def setup_inputs(seed: int = 0) -> dict:
    seeds = jax.random.split(jax.random.key(seed), 16)
    return {
        "tokens": draw_tokens(jax.random.fold_in(seeds[15], 71), 0),
        "segments": jax.vmap(lambda own: jnp.searchsorted(jnp.cumsum(uneven(own, 3, ROWS, 3 * ROWS // 4, 0)), jnp.arange(ROWS), side="right"))(jax.random.split(seeds[1], MBATCH)).reshape((MBATCH, ROWS)).astype(jnp.int32),
        "micro_live": draw_micro_live(jax.random.fold_in(seeds[15], 71), 0),
        "cotangent": draw_cotangent(jax.random.fold_in(seeds[15], 71), 0),
        "w_query": centred(seeds[4], (MODEL_WIDTH, QUERY_HEADS * HEAD_SIZE), MODEL_WIDTH ** -0.5, 0.125, ((0, 32),)),
        "key_weight": centred(seeds[5], (MODEL_WIDTH, KEY_VALUE_HEADS * HEAD_SIZE), MODEL_WIDTH ** -0.5, 0.125, ((0, 32),)),
        "value_weight": centred(seeds[6], (MODEL_WIDTH, KEY_VALUE_HEADS * HEAD_SIZE), MODEL_WIDTH ** -0.5, 0.125, ((0, 32),)),
        "w_output": centred(seeds[7], (QUERY_HEADS * HEAD_SIZE, MODEL_WIDTH), (QUERY_HEADS * HEAD_SIZE // 16) ** -0.5, 0.5, ((0, 32),)),
        "attn_gain": jnp.clip(1.0 + 0.1 * jax.random.normal(seeds[8], (MODEL_WIDTH,), jnp.float32), 0.5, 1.5).astype(jnp.bfloat16),
        "query_norm_gain": jnp.clip(1.09375 + 0.6015625 * jax.random.uniform(seeds[9], (HEAD_SIZE,), jnp.float32) ** block_scale(seeds[9], (HEAD_SIZE,), ((0, 32),), -0.2, 0.2), 1.09375, 1.6953125).astype(jnp.bfloat16),
        "key_gain": jnp.clip(1.09375 + 0.6015625 * jax.random.uniform(seeds[10], (HEAD_SIZE,), jnp.float32) ** block_scale(seeds[10], (HEAD_SIZE,), ((0, 32),), -0.2, 0.2), 1.09375, 1.6953125).astype(jnp.bfloat16),
        "w_gate": centred(seeds[11], (MODEL_WIDTH, FF), MODEL_WIDTH ** -0.5, 0.125, ((0, 32),)),
        "w_up": centred(seeds[12], (MODEL_WIDTH, FF), MODEL_WIDTH ** -0.5, 0.125, ((0, 32),)),
        "w_down": centred(seeds[13], (FF, MODEL_WIDTH), (FF // 2) ** -0.5, 0.109375, ((0, 32),)),
        "mlp_gain": jnp.clip(1.0 + 0.1 * jax.random.normal(seeds[14], (MODEL_WIDTH,), jnp.float32), 0.5, 1.5).astype(jnp.bfloat16),
    }


epsilon = 1e-06
base_theta = 1000000.0
highest = lax.Precision.HIGHEST

@jax.custom_vjp
def lower_precision(v):
    return lax.optimization_barrier(v.astype(jnp.bfloat16)).astype(jnp.float32)

@jax.custom_vjp
def lower_precision_backward(v):
    return v

def low_keep(v):
    return (lower_precision(v), None)

def low_pass(kept, grad):
    return (grad,)

def back_keep(v):
    return (v, None)

def back_low(kept, grad):
    return (lower_precision(grad),)
lower_precision.defvjp(low_keep, low_pass)
lower_precision_backward.defvjp(back_keep, back_low)

def matrix_product(left, right):
    return jnp.dot(left, right, precision=highest, preferred_element_type=jnp.float32)

def root_mean_square_norm(values, gain):
    return values * lax.rsqrt(lax.optimization_barrier(jnp.mean(values * values, axis=-1, keepdims=True)) + epsilon) * gain

def doc_positions(segments):
    earlier = (segments[:, None, :] < segments[:, :, None]).astype(jnp.int32)
    starts = lax.optimization_barrier(jnp.sum(earlier, axis=2))
    token_positions = lax.broadcasted_iota(jnp.int32, segments.shape, 1)
    return (token_positions - starts).astype(jnp.float32)

def apply_rotation(values, token_positions):
    half = values.shape[-1] // 2
    freqs = base_theta ** (-jnp.arange(half, dtype=jnp.float32) * 2.0 / values.shape[-1])
    angles = token_positions[:, :, None, None] * freqs
    cosine = jnp.cos(angles)
    sine = jnp.sin(angles)
    first = values[..., :half]
    second = values[..., half:]
    return jnp.concatenate([first * cosine - second * sine, second * cosine + first * sine], axis=-1)

def allowed(segments):
    sequence_length = segments.shape[1]
    query_at = lax.broadcasted_iota(jnp.int32, (sequence_length, sequence_length), 0)
    key_at = lax.broadcasted_iota(jnp.int32, (sequence_length, sequence_length), 1)
    return (segments[:, :, None] == segments[:, None, :]) & (key_at <= query_at)[None]

def layer(inputs, segments, w_query, key_weight, value_weight, w_output, attn_gain, query_norm_gain, key_gain, w_gate, w_up, w_down, mlp_gain):
    item_count = inputs.shape[0]
    sequence_length = inputs.shape[1]
    query_group_count = QUERY_HEADS // KEY_VALUE_HEADS
    token_positions = doc_positions(segments)
    normalized_input = lower_precision(root_mean_square_norm(inputs, attn_gain)).reshape(item_count * sequence_length, MODEL_WIDTH)
    query_projected = lower_precision_backward(matrix_product(normalized_input, w_query)).reshape(item_count, sequence_length, QUERY_HEADS, HEAD_SIZE)
    key_projected = lower_precision_backward(matrix_product(normalized_input, key_weight)).reshape(item_count, sequence_length, KEY_VALUE_HEADS, HEAD_SIZE)
    value_rows = lower_precision(lower_precision_backward(matrix_product(normalized_input, value_weight))).reshape(item_count, sequence_length, KEY_VALUE_HEADS, HEAD_SIZE)
    query_rows = lower_precision(apply_rotation(root_mean_square_norm(query_projected, query_norm_gain), token_positions)).reshape(item_count, sequence_length, KEY_VALUE_HEADS, query_group_count, HEAD_SIZE)
    key = lower_precision(apply_rotation(root_mean_square_norm(key_projected, key_gain), token_positions))
    scores = lower_precision_backward(jnp.einsum('bikgd,bjkd->bkgij', query_rows, key, precision=highest) * HEAD_SIZE ** (-0.5))
    scores = jnp.where(allowed(segments)[:, None, None], scores, -1e+30)
    top = lax.optimization_barrier(jnp.max(scores, axis=-1, keepdims=True))
    expos = jnp.exp(scores - top)
    probs = lower_precision(expos / lax.optimization_barrier(jnp.sum(expos, axis=-1, keepdims=True)))
    context = jnp.einsum('bkgij,bjkd->bikgd', probs, value_rows, precision=highest)
    context = lower_precision(lower_precision_backward(context)).reshape(item_count * sequence_length, QUERY_HEADS * HEAD_SIZE)
    middle = inputs + lower_precision_backward(matrix_product(context, w_output)).reshape(item_count, sequence_length, MODEL_WIDTH)
    normed_two = lower_precision(root_mean_square_norm(middle, mlp_gain)).reshape(item_count * sequence_length, MODEL_WIDTH)
    gate = lower_precision_backward(matrix_product(normed_two, w_gate))
    up_part = lower_precision_backward(matrix_product(normed_two, w_up))
    act = lower_precision(jax.nn.silu(gate) * up_part)
    return middle + lower_precision_backward(matrix_product(act, w_down)).reshape(item_count, sequence_length, MODEL_WIDTH)

def reference(tokens, segments, micro_live, cotangent, w_query, key_weight, value_weight, w_output, attn_gain, query_norm_gain, key_gain, w_gate, w_up, w_down, mlp_gain):
    weights = tuple((weight.astype(jnp.float32) for weight in (w_query, key_weight, value_weight, w_output, attn_gain, query_norm_gain, key_gain, w_gate, w_up, w_down, mlp_gain)))
    slot_index = jnp.arange(MBATCH, dtype=jnp.int32)
    owner_index = (slot_index // MSLOT).astype(jnp.int32)
    live_flags = (slot_index % MSLOT < micro_live[owner_index]).astype(jnp.float32)
    group = math.gcd(MBATCH, 32)
    blocks = MBATCH // group
    inputs = tokens.astype(jnp.float32).reshape(blocks, group, ROWS, MODEL_WIDTH)
    seg_blocks = segments.reshape(blocks, group, ROWS)
    live_blocks = live_flags.reshape(blocks, group)
    step = jax.checkpoint(layer)

    def whole(values, *params):

        def scan_step(carry, pieces):
            return (carry, step(pieces[0], pieces[1], *params) * pieces[2][:, None, None])
        _, outputs = lax.scan(scan_step, None, (values, seg_blocks, live_blocks))
        return outputs
    outputs, pull = jax.vjp(whole, inputs, *weights)
    grads = pull(cotangent.astype(jnp.float32).reshape(inputs.shape))
    return (outputs.reshape(TOKENS, MODEL_WIDTH).astype(jnp.bfloat16), grads[0].reshape(TOKENS, MODEL_WIDTH).astype(jnp.bfloat16), grads[1], grads[2], grads[3], grads[4], grads[5], grads[6], grads[7], grads[8], grads[9], grads[10], grads[11])
```

```python
import functools

import jax
import jax.numpy as jnp
from jax import lax
from jax.experimental import pallas as pl
from jax.experimental.pallas import tpu as pltpu
from jax.sharding import PartitionSpec as P

QUERY_HEADS = 16
KEY_VALUE_HEADS = 8
HEAD_SIZE = 128
TEAM = 8
CHUNKS = 2

epsilon = 1e-06
base_theta = 1000000.0
MESH = pl.DeviceIdType.MESH
f32 = jnp.float32
bf16 = jnp.bfloat16


def root_mean_square_norm(values, gain):
    return values * lax.rsqrt(jnp.mean(values * values, axis=-1, keepdims=True) + epsilon) * gain


def doc_positions(segments):
    earlier = (segments[:, None, :] < segments[:, :, None]).astype(jnp.int32)
    starts = jnp.sum(earlier, axis=2)
    token_positions = lax.broadcasted_iota(jnp.int32, segments.shape, 1)
    return (token_positions - starts).astype(jnp.float32)


def rotation_tables(token_positions):
    half = HEAD_SIZE // 2
    freqs = base_theta ** (-jnp.arange(half, dtype=jnp.float32) * 2.0 / HEAD_SIZE)
    angles = token_positions[:, :, None, None] * freqs
    return jnp.cos(angles), jnp.sin(angles)


def apply_rotation(values, tables):
    cosine, sine = tables
    half = values.shape[-1] // 2
    first = values[..., :half]
    second = values[..., half:]
    return jnp.concatenate(
        [first * cosine - second * sine, second * cosine + first * sine], axis=-1
    )


def allowed(segments):
    sequence_length = segments.shape[1]
    query_at = lax.broadcasted_iota(jnp.int32, (sequence_length, sequence_length), 0)
    key_at = lax.broadcasted_iota(jnp.int32, (sequence_length, sequence_length), 1)
    return (segments[:, :, None] == segments[:, None, :]) & (key_at <= query_at)[None]


def dot_last(left, right):
    return lax.dot_general(
        left, right, (((1,), (1,)), ((), ())), preferred_element_type=jnp.float32
    )


def dot_first(left, right):
    return lax.dot_general(
        left, right, (((0,), (0,)), ((), ())), preferred_element_type=jnp.float32
    )


def simple_product(left, right):
    return jnp.dot(left, right, preferred_element_type=jnp.float32)


def flipped(index, mask):
    for bit in (1, 2, 4):
        if mask & bit:
            index = index + bit * (1 - 2 * lax.rem(lax.div(index, bit), 2))
    return index


def greet(me, masks, others=()):
    barrier = pltpu.get_barrier_semaphore()
    for mask in masks:
        pl.semaphore_signal(
            barrier, inc=1, device_id=(flipped(me, mask),), device_id_type=MESH
        )
    for other in others:
        pl.semaphore_signal(barrier, inc=1, device_id=(other,), device_id_type=MESH)
    pl.semaphore_wait(barrier, len(masks) + len(others))


def remote(source, target, send, receive, device):
    return pltpu.make_async_remote_copy(
        src_ref=source,
        dst_ref=target,
        send_sem=send,
        recv_sem=receive,
        device_id=(device,),
        device_id_type=MESH,
    )


def params(collective, limit=None):
    if limit is None:
        return pltpu.CompilerParams(collective_id=collective, has_side_effects=True)
    return pltpu.CompilerParams(
        collective_id=collective, has_side_effects=True, vmem_limit_bytes=limit
    )


def swap_kernel(x_ref, o_ref, send, receive, own):
    me = lax.axis_index("fsdp")
    place = lax.rem(me, TEAM)
    keep = pltpu.make_async_copy(x_ref.at[place], o_ref.at[place], own)
    keep.start()
    greet(me, range(1, TEAM))
    copies = []
    for mask in (6, 7, 2, 3, 4, 5, 1):
        copy = remote(
            x_ref.at[flipped(place, mask)],
            o_ref.at[place],
            send.at[mask - 1],
            receive.at[mask - 1],
            flipped(me, mask),
        )
        copy.start()
        copies.append(copy)
    for copy in copies:
        copy.wait()
    keep.wait()


def swap(x, collective):
    return pl.pallas_call(
        swap_kernel,
        out_shape=jax.ShapeDtypeStruct(x.shape, x.dtype),
        in_specs=[pl.BlockSpec(memory_space=pl.ANY)],
        out_specs=pl.BlockSpec(memory_space=pl.ANY),
        scratch_shapes=[
            pltpu.SemaphoreType.DMA((TEAM - 1,)),
            pltpu.SemaphoreType.DMA((TEAM - 1,)),
            pltpu.SemaphoreType.DMA,
        ],
        compiler_params=params(collective),
    )(x)


def gather_kernel(x_ref, o_ref, send, receive, own):
    me = lax.axis_index("fsdp")
    place = lax.rem(me, TEAM)
    rows = x_ref.shape[0]
    half = rows // 2
    keep = pltpu.make_async_copy(x_ref, o_ref.at[place], own)
    keep.start()
    greet(me, (1, 2, 4))

    def part(ref, which):
        return ref.at[pl.ds(which * half, half)]

    def begin(source, slot, which, mask, k):
        copy = remote(
            source, part(o_ref.at[slot], which), send.at[k], receive.at[k], flipped(me, mask)
        )
        copy.start()
        return copy

    def relay(slot, which, mask, k):
        return begin(part(o_ref.at[slot], which), slot, which, mask, k)

    by_x, by_y, by_both = flipped(place, 2), flipped(place, 4), flipped(place, 6)
    x0 = begin(part(x_ref, 0), place, 0, 2, 0)
    y1 = begin(part(x_ref, 1), place, 1, 4, 1)
    x1 = begin(part(x_ref, 1), place, 1, 2, 2)
    y0 = begin(part(x_ref, 0), place, 0, 4, 3)
    late = [begin(part(x_ref, 0), place, 0, 1, 6), begin(part(x_ref, 1), place, 1, 1, 7)]
    x0.wait_recv()
    d0 = relay(by_x, 0, 4, 4)
    y1.wait_recv()
    d1 = relay(by_y, 1, 2, 5)
    late.append(relay(by_x, 0, 1, 8))
    late.append(relay(by_y, 1, 1, 9))
    x1.wait_recv()
    late.append(relay(by_x, 1, 1, 10))
    y0.wait_recv()
    late.append(relay(by_y, 0, 1, 11))
    d0.wait_recv()
    late.append(relay(by_both, 0, 1, 12))
    d1.wait_recv()
    late.append(relay(by_both, 1, 1, 13))
    for copy in late:
        copy.wait_recv()
    for copy in (x0, y1, x1, y0, d0, d1, *late):
        copy.wait_send()
    keep.wait()


def gather(x, collective):
    rows, width = x.shape
    whole = pl.pallas_call(
        gather_kernel,
        out_shape=jax.ShapeDtypeStruct((TEAM, rows, width), x.dtype),
        in_specs=[pl.BlockSpec(memory_space=pl.ANY)],
        out_specs=pl.BlockSpec(memory_space=pl.ANY),
        scratch_shapes=[
            pltpu.SemaphoreType.DMA((14,)),
            pltpu.SemaphoreType.DMA((14,)),
            pltpu.SemaphoreType.DMA,
        ],
        compiler_params=params(collective),
    )(x)
    return whole.reshape(TEAM * rows, width)


def reduce_kernel(part, out, mix, from_core, from_x, from_y, send, receive):
    me = lax.axis_index("fsdp")
    place = lax.rem(me, TEAM)
    rows = out.shape[0]
    half = rows // 2
    step = 16
    targets = [flipped(place, mask) for mask in (6, 2, 4, 0)]
    greet(me, (1, 2, 4))

    across = []
    for j, target in enumerate(targets):
        copy = remote(
            part.at[flipped(target, 1)], from_core.at[j], send.at[j], receive.at[j], flipped(me, 1)
        )
        copy.start()
        across.append(copy)

    def combine(j):
        across[j].wait_recv()

        @pl.loop(0, rows // step)
        def _(i):
            at = pl.ds(i * step, step)
            mix[j, at, :] = (
                part[targets[j], at, :].astype(f32) + from_core[j, at, :].astype(f32)
            ).astype(bf16)

    def begin(j, which, ref, slot, mask, k):
        copy = remote(
            mix.at[j, pl.ds(which * half, half)],
            ref.at[slot],
            send.at[k],
            receive.at[k],
            flipped(me, mask),
        )
        copy.start()
        return copy

    def add_relayed(j, which, ref):
        @pl.loop(0, half // step)
        def _(i):
            at = pl.ds(which * half + i * step, step)
            mix[j, at, :] = (
                mix[j, at, :].astype(f32) + ref[0, pl.ds(i * step, step), :].astype(f32)
            ).astype(bf16)

    combine(0)
    d_x = begin(0, 0, from_x, 0, 2, 4)
    d_y = begin(0, 1, from_y, 0, 4, 5)
    combine(1)
    x_0 = begin(1, 0, from_x, 1, 2, 6)
    combine(2)
    y_1 = begin(2, 1, from_y, 1, 4, 7)
    d_x.wait_recv()
    add_relayed(2, 0, from_x)
    y_0 = begin(2, 0, from_y, 2, 4, 8)
    d_y.wait_recv()
    add_relayed(1, 1, from_y)
    x_1 = begin(1, 1, from_x, 2, 2, 9)
    across[3].wait_recv()

    @pl.loop(0, rows // step)
    def _(i):
        at = pl.ds(i * step, step)
        out[at, :] = part[place, at, :].astype(f32) + from_core[3, at, :].astype(f32)

    def finish(which, slot_x, slot_y):
        @pl.loop(0, half // step)
        def _(i):
            at = pl.ds(which * half + i * step, step)
            here = pl.ds(i * step, step)
            out[at, :] = out[at, :] + (
                from_x[slot_x, here, :].astype(f32) + from_y[slot_y, here, :].astype(f32)
            )

    x_0.wait_recv()
    y_0.wait_recv()
    finish(0, 1, 2)
    y_1.wait_recv()
    x_1.wait_recv()
    finish(1, 2, 1)
    for copy in (*across, d_x, d_y, x_0, x_1, y_0, y_1):
        copy.wait_send()


def reduce(part, collective):
    rows, width = part.shape[0] // TEAM, part.shape[1]
    vmem = pl.BlockSpec(memory_space=pltpu.VMEM)
    return pl.pallas_call(
        reduce_kernel,
        out_shape=jax.ShapeDtypeStruct((rows, width), f32),
        in_specs=[vmem],
        out_specs=vmem,
        scratch_shapes=[
            pltpu.VMEM((4, rows, width), bf16),
            pltpu.VMEM((4, rows, width), bf16),
            pltpu.VMEM((3, rows // 2, width), bf16),
            pltpu.VMEM((3, rows // 2, width), bf16),
            pltpu.SemaphoreType.DMA((10,)),
            pltpu.SemaphoreType.DMA((10,)),
        ],
        compiler_params=params(collective, 40 * 2**20),
    )(part.reshape(TEAM, rows, width))


def spread_kernel(planes, back, x_ref, o_ref, send, receive, own):
    me = lax.axis_index("fsdp")
    place = lax.rem(me, TEAM)
    team = me - place
    greet(me, range(1, TEAM))

    def route(k, at_heads):
        if at_heads:
            block = planes * place + k
            return lax.rem(block, TEAM), lax.div(block, TEAM)
        block = TEAM * k + place
        return lax.div(block, planes), lax.rem(block, planes)

    def copies(k):
        partner, there = route(k, back)
        over = remote(x_ref.at[k], o_ref.at[there], send.at[k], receive.at[there], team + partner)
        here = pltpu.make_async_copy(x_ref.at[k], o_ref.at[there], own.at[k])
        return partner, over, here

    def incoming(k):
        partner, _ = route(k, not back)
        return partner, remote(x_ref.at[k], o_ref.at[k], send.at[k], receive.at[k], team + partner)

    for k in range(planes):
        partner, over, here = copies(k)
        pl.when(partner != place)(over.start)
        pl.when(partner == place)(here.start)
    for k in range(planes):
        partner, over, here = copies(k)
        pl.when(partner != place)(over.wait_send)
        pl.when(partner == place)(here.wait)
        partner, arriving = incoming(k)
        pl.when(partner != place)(arriving.wait_recv)


def spread(x, planes, back, collective):
    rows = x.shape[0] // planes
    moved = pl.pallas_call(
        functools.partial(spread_kernel, planes, back),
        out_shape=jax.ShapeDtypeStruct((planes, rows, x.shape[1]), x.dtype),
        in_specs=[pl.BlockSpec(memory_space=pl.ANY)],
        out_specs=pl.BlockSpec(memory_space=pl.ANY),
        scratch_shapes=[
            pltpu.SemaphoreType.DMA((planes,)),
            pltpu.SemaphoreType.DMA((planes,)),
            pltpu.SemaphoreType.DMA((planes,)),
        ],
        compiler_params=params(collective),
    )(x.reshape(planes, rows, x.shape[1]))
    return moved.reshape(x.shape)


def open_kernel(
    planes,
    qkv_in,
    gate_up_in,
    output_in,
    tokens_in,
    small_in,
    qkv,
    gate_up,
    output_raw,
    output,
    tokens,
    small,
    send,
    receive,
    own,
):
    me = lax.axis_index("fsdp")
    place = lax.rem(me, TEAM)
    plane = lax.div(me, TEAM)
    team = me - place
    total_devices = planes * TEAM
    others = [lax.rem(me + TEAM * k, total_devices) for k in range(1, planes)]
    rows = tokens_in.shape[0]
    half = rows // 2
    counter = iter(range(10**6))
    chunks = gate_up_in.shape[0]

    keeps = []
    locals_ = iter(range(10**6))

    def keep(source, target):
        copy = pltpu.make_async_copy(source, target, own.at[next(locals_)])
        copy.start()
        return copy

    keep_qkv = keep(qkv_in.at[place], qkv.at[plane, place])
    keep_output = keep(output_in, output_raw.at[plane])
    keep_small = keep(small_in, small.at[me])
    keeps.append(keep(tokens_in, tokens.at[place]))
    for c in range(chunks):
        keeps.append(keep(gate_up_in.at[c, place], gate_up.at[c, place]))
    greet(me, range(1, TEAM), others)

    started = []

    def begin(source, target, device):
        k = next(counter)
        copy = remote(source, target, send.at[k], receive.at[k], device)
        copy.start()
        started.append(copy)
        return copy

    masks = (6, 7, 2, 3, 4, 5, 1)
    swaps = [
        begin(qkv_in.at[flipped(place, m)], qkv.at[plane, place], flipped(me, m)) for m in masks
    ]
    near = [begin(small_in, small.at[me], flipped(me, m)) for m in masks]

    def line(ref):
        up, down = [next(counter) for _ in range(planes - 1)], [
            next(counter) for _ in range(planes - 1)
        ]

        def passing(step, sign, ks, source):
            block = jnp.clip(source, 0, planes - 1)
            beyond = jnp.clip(plane + sign, 0, planes - 1) * TEAM + place
            return remote(
                ref.at[block], ref.at[block], send.at[ks[step]], receive.at[ks[step]], beyond
            )

        def goes(step, sign):
            source, onward = plane - sign * step, plane + sign
            return (
                (source >= 0) & (source <= planes - 1) & (onward >= 0) & (onward <= planes - 1)
            )

        def start(step):
            for sign, ks in ((1, up), (-1, down)):
                going = passing(step, sign, ks, plane - sign * step)
                pl.when(goes(step, sign))(going.start)

        def arrive(step):
            for sign, ks in ((1, up), (-1, down)):
                source = plane - sign * (step + 1)
                coming = passing(step, sign, ks, source)
                pl.when((source >= 0) & (source <= planes - 1))(coming.wait_recv)

        def sent(step):
            for sign, ks in ((1, up), (-1, down)):
                going = passing(step, sign, ks, plane - sign * step)
                pl.when(goes(step, sign))(going.wait_send)

        return start, arrive, sent

    qkv_start, qkv_arrive, qkv_sent = line(qkv)
    out_start, out_arrive, out_sent = line(output_raw)

    for copy in swaps:
        copy.wait_recv()
    keep_qkv.wait()
    keep_output.wait()
    qkv_start(0)
    out_start(0)

    def part(ref, which):
        return ref.at[pl.ds(which * half, half)]

    def relay(slot, which, mask):
        ref = part(tokens.at[slot], which)
        return begin(ref, ref, flipped(me, mask))

    def first(which, mask):
        return begin(part(tokens_in, which), part(tokens.at[place], which), flipped(me, mask))

    by_x, by_y, by_both = flipped(place, 2), flipped(place, 4), flipped(place, 6)
    x0, y1, x1, y0 = first(0, 2), first(1, 4), first(1, 2), first(0, 4)
    late = [first(0, 1), first(1, 1)]
    for copy in near:
        copy.wait_recv()
    keep_small.wait()
    slots = small.at[pl.ds(team, TEAM)]
    far = [begin(slots, slots, other) for other in others]
    x0.wait_recv()
    d0 = relay(by_x, 0, 4)
    y1.wait_recv()
    d1 = relay(by_y, 1, 2)
    late += [relay(by_x, 0, 1), relay(by_y, 1, 1)]
    gate_ups = [
        begin(gate_up_in.at[c, flipped(place, m)], gate_up.at[c, place], flipped(me, m))
        for c in range(chunks)
        for m in masks
    ]
    for step in range(planes - 1):
        qkv_arrive(step)
        if step < planes - 2:
            qkv_start(step + 1)
        out_arrive(step)
        if step < planes - 2:
            out_start(step + 1)
        if step == 0:
            x1.wait_recv()
            late.append(relay(by_x, 1, 1))
            y0.wait_recv()
            late.append(relay(by_y, 0, 1))
            d0.wait_recv()
            late.append(relay(by_both, 0, 1))
            d1.wait_recv()
            late.append(relay(by_both, 1, 1))

    spread_send = [next(counter) for _ in range(planes)]
    spread_receive = [next(counter) for _ in range(planes)]

    spread_own = [next(locals_) for _ in range(planes)]

    def outgoing(k):
        block = TEAM * k + place
        partner, there = lax.div(block, planes), lax.rem(block, planes)
        over = remote(
            output_raw.at[k],
            output.at[there],
            send.at[spread_send[k]],
            receive.at[spread_receive[0] + there],
            team + partner,
        )
        here = pltpu.make_async_copy(output_raw.at[k], output.at[there], own.at[spread_own[k]])
        return partner, over, here

    def incoming(k):
        partner = lax.rem(planes * place + k, TEAM)
        return partner, remote(
            output_raw.at[k],
            output.at[k],
            send.at[spread_send[k]],
            receive.at[spread_receive[k]],
            team + partner,
        )

    for k in range(planes):
        partner, over, here = outgoing(k)
        pl.when(partner != place)(over.start)
        pl.when(partner == place)(here.start)
    for copy in (*far, *gate_ups, *late):
        copy.wait_recv()
    for k in range(planes):
        partner, over, here = outgoing(k)
        pl.when(partner != place)(over.wait_send)
        pl.when(partner == place)(here.wait)
        partner, arriving = incoming(k)
        pl.when(partner != place)(arriving.wait_recv)
    for step in range(planes - 1):
        qkv_sent(step)
        out_sent(step)
    for copy in started:
        copy.wait_send()
    for copy in keeps:
        copy.wait()


def opening(qkv, gate_up, output, tokens, small, planes, collective):
    links = 7 + 7 + 4 * (planes - 1) + 14 + planes - 1 + 7 * gate_up.shape[0] + 2 * planes
    anywhere = pl.BlockSpec(memory_space=pl.ANY)
    like = jax.ShapeDtypeStruct
    return pl.pallas_call(
        functools.partial(open_kernel, planes),
        out_shape=(
            like((planes, *qkv.shape), bf16),
            like(gate_up.shape, bf16),
            like((planes, *output.shape), bf16),
            like((planes, *output.shape), bf16),
            like((TEAM, *tokens.shape), bf16),
            like((planes * TEAM, *small.shape), bf16),
        ),
        in_specs=[anywhere] * 5,
        out_specs=(anywhere,) * 6,
        scratch_shapes=[
            pltpu.SemaphoreType.DMA((links,)),
            pltpu.SemaphoreType.DMA((links,)),
            pltpu.SemaphoreType.DMA((4 + gate_up.shape[0] + planes,)),
        ],
        compiler_params=params(collective),
    )(qkv, gate_up, output, tokens, small)


def total_kernel(planes, x_ref, o_ref, near_in, mid, far_in, send, receive):
    me = lax.axis_index("fsdp")
    place = lax.rem(me, TEAM)
    plane = lax.div(me, TEAM)
    others = [lax.rem(me + TEAM * k, planes * TEAM) for k in range(1, planes)]
    greet(me, range(1, TEAM), others)
    near = []
    for mask in range(1, TEAM):
        copy = remote(
            x_ref.at[flipped(place, mask)],
            near_in.at[mask - 1],
            send.at[mask - 1],
            receive.at[mask - 1],
            flipped(me, mask),
        )
        copy.start()
        near.append(copy)
    for copy in near:
        copy.wait_recv()
    summed = x_ref[place]
    for mask in range(1, TEAM):
        summed = summed + near_in[mask - 1]
    mid[...] = summed
    far = []
    for k, other in enumerate(others):
        copy = remote(
            mid.at[lax.rem(plane + k + 1, planes)],
            far_in.at[k],
            send.at[TEAM - 1 + k],
            receive.at[TEAM - 1 + k],
            other,
        )
        copy.start()
        far.append(copy)
    for copy in far:
        copy.wait_recv()
    result = mid[plane]
    for k in range(planes - 1):
        result = result + far_in[k]
    o_ref[...] = result
    for copy in (*near, *far):
        copy.wait_send()


def total(x, planes, collective):
    links = TEAM - 1 + planes - 1
    block = x.shape[2:]
    vmem = pl.BlockSpec(memory_space=pltpu.VMEM)
    return pl.pallas_call(
        functools.partial(total_kernel, planes),
        out_shape=jax.ShapeDtypeStruct(block, x.dtype),
        in_specs=[vmem],
        out_specs=vmem,
        scratch_shapes=[
            pltpu.VMEM((TEAM - 1, planes, *block), x.dtype),
            pltpu.VMEM((planes, *block), x.dtype),
            pltpu.VMEM((planes - 1, *block), x.dtype),
            pltpu.SemaphoreType.DMA((links,)),
            pltpu.SemaphoreType.DMA((links,)),
        ],
        compiler_params=params(collective),
    )(x)


def padded(rows, height, width, dtype):
    rows = [jnp.pad(r, ((0, 0), (0, width - r.shape[1]))) for r in rows]
    block = jnp.concatenate(rows, axis=0).astype(dtype)
    return jnp.pad(block, ((0, height - block.shape[0]), (0, 0)))


def local(
    devices,
    tokens,
    segments,
    micro_live,
    cotangent,
    w_query,
    key_weight,
    value_weight,
    w_output,
    attn_gain,
    query_norm_gain,
    key_gain,
    w_gate,
    w_up,
    w_down,
    mlp_gain,
):
    planes = devices // TEAM
    lines = [[place + TEAM * k for k in range(planes)] for place in range(TEAM)]
    slots, sequence = segments.shape
    token_count, width = tokens.shape
    groups = QUERY_HEADS // KEY_VALUE_HEADS
    rows = w_query.shape[0]
    ff_rows = w_down.shape[0]
    ff_part = ff_rows // CHUNKS
    team_slots = TEAM * slots
    head_width = groups * HEAD_SIZE
    me = lax.axis_index("fsdp")
    plane = me // TEAM

    def gather_line(x):
        return lax.all_gather(x, "fsdp", axis=0, tiled=True, axis_index_groups=lines)

    def sum_line(x):
        return lax.psum_scatter(
            x, "fsdp", scatter_dimension=0, tiled=True, axis_index_groups=lines
        )

    slot_live = (lax.broadcasted_iota(jnp.int32, (slots, 1), 0) < micro_live[0]).astype(f32)
    row_live = jnp.broadcast_to(slot_live, (slots, sequence)).reshape(token_count, 1)

    qkv_send = jnp.concatenate(
        [
            w.reshape(rows, TEAM, w.shape[1] // TEAM).transpose(1, 0, 2)
            for w in (w_query, key_weight, value_weight)
        ],
        axis=2,
    )
    gate_up_send = jnp.concatenate(
        [
            w.reshape(rows, planes, TEAM, CHUNKS, ff_part)
            .transpose(3, 2, 0, 1, 4)
            .reshape(CHUNKS, TEAM, rows, planes * ff_part)
            for w in (w_gate, w_up)
        ],
        axis=3,
    )
    small_send = padded(
        [
            attn_gain[None],
            mlp_gain[None],
            query_norm_gain[None],
            key_gain[None],
            segments.astype(bf16),
        ],
        16,
        128,
        bf16,
    )
    qkv_weight, gate_up_slices, _, output_weight, team_tokens, small = opening(
        qkv_send, gate_up_send, w_output, tokens, small_send, planes, 1
    )
    qkv_weight = qkv_weight.reshape(width, -1)
    output_weight = output_weight.reshape(head_width, width)
    gate_up_weights = []
    down_weights = []
    for k in range(CHUNKS):
        gate_up_weights.append(gather_line(gate_up_slices[k].reshape(TEAM * rows, -1)))
        down_rows, _ = lax.optimization_barrier(
            (w_down[k * ff_part : (k + 1) * ff_part], gate_up_slices)
        )
        down_weights.append(gather_line(down_rows))

    norm_gain = small[:, 0, : attn_gain.shape[0]].reshape(width).astype(f32)
    mlp_norm_gain = small[:, 1, : mlp_gain.shape[0]].reshape(width).astype(f32)
    qgain = small[:, 2, : query_norm_gain.shape[0]].reshape(HEAD_SIZE).astype(f32)
    kgain = small[:, 3, : key_gain.shape[0]].reshape(HEAD_SIZE).astype(f32)
    team_small = lax.dynamic_slice_in_dim(small, plane * TEAM, TEAM, axis=0)
    team_segments = (
        team_small[:, 4 : 4 + slots, :sequence].reshape(team_slots, sequence).astype(jnp.int32)
    )
    tables = rotation_tables(doc_positions(team_segments))
    visible = allowed(team_segments)

    inputs = tokens.astype(f32)
    cot_b = cotangent * row_live.astype(bf16)
    team_normalized = root_mean_square_norm(
        team_tokens.reshape(TEAM * token_count, width).astype(f32), norm_gain
    ).astype(bf16)

    projected = simple_product(team_normalized, qkv_weight)

    def head_prep(query_projected, key_projected, gain_query, gain_key):
        query_heads = query_projected.reshape(team_slots, sequence, groups, HEAD_SIZE)
        key_heads = key_projected.reshape(team_slots, sequence, 1, HEAD_SIZE)
        return (
            apply_rotation(root_mean_square_norm(query_heads, gain_query), tables),
            apply_rotation(root_mean_square_norm(key_heads, gain_key), tables),
        )

    query_projected = projected[:, :head_width]
    key_projected = projected[:, head_width : head_width + HEAD_SIZE]
    value_b = projected[:, head_width + HEAD_SIZE :].astype(bf16)
    value_b = value_b.reshape(team_slots, sequence, HEAD_SIZE)
    query_rot, key_rot = head_prep(query_projected, key_projected, qgain, kgain)
    query_b = query_rot.astype(bf16)
    key_b = key_rot.astype(bf16).reshape(team_slots, sequence, HEAD_SIZE)
    scores = jnp.einsum(
        "bigd,bjd->bgij", query_b, key_b, preferred_element_type=f32
    ) * HEAD_SIZE ** (-0.5)
    scores = jnp.where(visible[:, None], scores, -1e30)
    top = jnp.max(scores, axis=-1, keepdims=True)
    expos = jnp.exp(scores - top)
    probs = expos / jnp.sum(expos, axis=-1, keepdims=True)
    probs_b = probs.astype(bf16)
    context = jnp.einsum("bgij,bjd->bigd", probs_b, value_b, preferred_element_type=f32)
    context_b = context.astype(bf16).reshape(team_slots * sequence, head_width)
    middle = inputs + reduce(simple_product(context_b, output_weight).astype(bf16), 5)

    normed_two = root_mean_square_norm(middle, mlp_norm_gain).astype(bf16)
    team_two = gather(normed_two, 3)
    late_cot, _ = lax.optimization_barrier((cot_b, team_two))
    team_cot = gather(late_cot, 3)
    out_part = 0.0
    grad_two_part = 0.0
    grad_gate_up = []
    grad_down = []
    units = planes * ff_part
    for k in range(CHUNKS):
        both = simple_product(team_two, gate_up_weights[k])
        gate, up = both[:, :units], both[:, units:]
        sigma = jax.nn.sigmoid(gate)
        silu_gate = gate * sigma
        act_b = (silu_gate * up).astype(bf16)
        grad_act = dot_last(team_cot, down_weights[k])
        grad_both = jnp.concatenate(
            [
                (grad_act * up * (sigma * (1.0 + gate * (1.0 - sigma)))).astype(bf16),
                (grad_act * silu_gate).astype(bf16),
            ],
            axis=1,
        )
        grad_gate_up.append(sum_line(dot_first(team_two, grad_both).astype(bf16)))
        grad_down.append(sum_line(dot_first(act_b, team_cot).astype(bf16)))
        out_part = out_part + simple_product(act_b, down_weights[k])
        grad_two_part = grad_two_part + dot_last(grad_both, gate_up_weights[k])

    grad_normed_two = reduce(grad_two_part.astype(bf16), 5)
    _, pull_two = jax.vjp(root_mean_square_norm, middle, mlp_norm_gain)
    middle_part, grad_mgain = pull_two(grad_normed_two)
    grad_middle = cot_b.astype(f32) + middle_part
    team_grad = gather(grad_middle.astype(bf16), 3)

    grad_output_part = spread(
        dot_first(context_b, team_grad).astype(bf16), planes, True, 6
    )
    grad_output = sum_line(grad_output_part)
    grad_context = dot_last(team_grad, output_weight).astype(bf16)
    grad_context = grad_context.reshape(team_slots, sequence, groups, HEAD_SIZE)
    grad_value = jnp.einsum(
        "bgij,bigd->bjd", probs_b, grad_context, preferred_element_type=f32
    )
    grad_probs = jnp.einsum(
        "bigd,bjd->bgij", grad_context, value_b, preferred_element_type=f32
    )
    inner = jnp.sum(probs * grad_probs, axis=-1, keepdims=True)
    grad_scores = (probs * (grad_probs - inner)).astype(bf16)
    grad_query_rot = jnp.einsum(
        "bgij,bjd->bigd", grad_scores, key_b, preferred_element_type=f32
    ) * HEAD_SIZE ** (-0.5)
    grad_key_rot = jnp.einsum(
        "bgij,bigd->bjd", grad_scores, query_b, preferred_element_type=f32
    ) * HEAD_SIZE ** (-0.5)
    _, pull_heads = jax.vjp(head_prep, query_projected, key_projected, qgain, kgain)
    grad_query_raw, grad_key_raw, grad_qgain, grad_kgain = pull_heads(
        (grad_query_rot, grad_key_rot.reshape(team_slots, sequence, 1, HEAD_SIZE))
    )
    grad_qkv = jnp.concatenate(
        [
            grad_query_raw.astype(bf16),
            grad_key_raw.astype(bf16),
            grad_value.reshape(team_slots * sequence, HEAD_SIZE).astype(bf16),
        ],
        axis=1,
    )
    grad_qkv_weight = sum_line(dot_first(team_normalized, grad_qkv).astype(bf16))
    grad_normed = reduce(dot_last(grad_qkv, qkv_weight).astype(bf16), 5)
    _, pull_one = jax.vjp(root_mean_square_norm, inputs, norm_gain)
    input_part, grad_again = pull_one(grad_normed)
    grad_tokens = (grad_middle + input_part).astype(bf16)
    layer_out = (row_live * (middle + reduce(out_part.astype(bf16), 5))).astype(bf16)

    def by_owner(vector):
        vector = vector.reshape(devices, -1)
        return jnp.pad(vector, ((0, 0), (0, 128 - vector.shape[1])))

    gains = jnp.stack(
        [by_owner(v) for v in (grad_again, grad_mgain, grad_qgain, grad_kgain)], axis=1
    )
    gains = jnp.pad(gains, ((0, 0), (0, 4), (0, 0)))
    gains = gains.reshape(planes, TEAM, 8, 128).transpose(1, 0, 2, 3)
    gains = total(gains, planes, 7)

    grad_gate_parts, grad_up_parts = [], []
    before = grad_down[0]
    for k in range(CHUNKS):
        summed, _, _ = lax.optimization_barrier((grad_gate_up[k], grad_down[k], before))
        back = swap(summed.reshape(TEAM, rows, 2 * units), 2)
        before = back
        back = back.astype(f32)
        back = back.reshape(TEAM, rows, 2, planes, ff_part).transpose(2, 1, 3, 0, 4)
        grad_gate_parts.append(back[0])
        grad_up_parts.append(back[1])
    grad_gate = jnp.stack(grad_gate_parts, axis=3).reshape(rows, -1)
    grad_up = jnp.stack(grad_up_parts, axis=3).reshape(rows, -1)
    grad_down_w = jnp.concatenate(grad_down, axis=0).astype(f32)
    grad_qkv_weight, grad_output, _ = lax.optimization_barrier(
        (grad_qkv_weight, grad_output, before)
    )
    grad_output = grad_output.astype(f32)
    qkv_back = swap(grad_qkv_weight.reshape(TEAM, rows, -1), 0).astype(f32)
    qkv_back = qkv_back.transpose(1, 0, 2)
    grad_query = qkv_back[:, :, :head_width].reshape(rows, -1)
    grad_key = qkv_back[:, :, head_width : head_width + HEAD_SIZE].reshape(rows, -1)
    grad_value_w = qkv_back[:, :, head_width + HEAD_SIZE :].reshape(rows, -1)
    return (
        layer_out,
        grad_tokens,
        grad_query,
        grad_key,
        grad_value_w,
        grad_output,
        gains[0, : attn_gain.shape[0]],
        gains[2, : query_norm_gain.shape[0]],
        gains[3, : key_gain.shape[0]],
        grad_gate,
        grad_up,
        grad_down_w,
        gains[1, : mlp_gain.shape[0]],
    )


def solution(mesh):
    by_rows, by_entry = P("fsdp", None), P("fsdp")
    return jax.shard_map(
        functools.partial(local, mesh.shape["fsdp"]),
        mesh=mesh,
        in_specs=(
            by_rows,
            by_rows,
            by_entry,
            by_rows,
            by_rows,
            by_rows,
            by_rows,
            by_rows,
            by_entry,
            by_entry,
            by_entry,
            by_rows,
            by_rows,
            by_rows,
            by_entry,
        ),
        out_specs=(
            by_rows,
            by_rows,
            by_rows,
            by_rows,
            by_rows,
            by_rows,
            by_entry,
            by_entry,
            by_entry,
            by_rows,
            by_rows,
            by_rows,
            by_entry,
        ),
        check_vma=False,
    )
```

```python
import functools

import jax
import jax.numpy as jnp
import numpy as np
from jax import lax
from jax.experimental import pallas as pl
from jax.experimental.pallas import tpu as pltpu
from jax.sharding import PartitionSpec as P

QUERY_HEADS = 16
KEY_VALUE_HEADS = 8
HEAD_SIZE = 128
TEAM = 8
STEP = 256

epsilon = 1e-06
base_theta = 1000000.0
MESH = pl.DeviceIdType.MESH
LIMIT = 60 * 2**20
f32 = jnp.float32
bf16 = jnp.bfloat16


def root_mean_square_norm(values, gain):
    return values * lax.rsqrt(jnp.mean(values * values, axis=-1, keepdims=True) + epsilon) * gain


def rotation_tables(positions):
    half = HEAD_SIZE // 2
    powers = -np.arange(half, dtype=np.float32) * np.float32(2.0) / np.float32(HEAD_SIZE)
    freqs = np.power(np.float32(base_theta), powers).astype(np.float32)
    angles = np.arange(positions, dtype=np.float32)[:, None] * freqs
    cosine, sine = np.cos(angles), np.sin(angles)
    rest = np.concatenate([cosine, cosine, -sine, sine], axis=1).astype(np.float32)
    parts = []
    for _ in range(3):
        parts.append(rest.astype(jnp.bfloat16))
        rest = rest - parts[-1].astype(np.float32)
    return np.concatenate(parts, axis=1)


def dot_last(left, right):
    return lax.dot_general(
        left, right, (((1,), (1,)), ((), ())), preferred_element_type=jnp.float32
    )


def dot_first(left, right):
    return lax.dot_general(
        left, right, (((0,), (0,)), ((), ())), preferred_element_type=jnp.float32
    )


def simple_product(left, right):
    return jnp.dot(left, right, preferred_element_type=jnp.float32)


def flipped(index, mask):
    for bit in (1, 2, 4):
        if mask & bit:
            index = index + bit * (1 - 2 * lax.rem(lax.div(index, bit), 2))
    return index


def greet(me, masks, others=(), owners=()):
    barrier = pltpu.get_barrier_semaphore()

    def signal(device):
        pl.semaphore_signal(barrier, inc=1, device_id=(device,), device_id_type=MESH)

    for mask in masks:
        signal(flipped(me, mask))
    for other in others:
        signal(other)
    peers = len(masks) + len(others)
    for owner in owners:
        pl.when(owner != me)(functools.partial(signal, owner))
        peers = peers + (owner != me).astype(jnp.int32)
    pl.semaphore_wait(barrier, peers)


def head_owner(me, planes):
    to = TEAM * lax.rem(me, planes) + lax.div(me, planes)
    back = planes * lax.rem(me, TEAM) + lax.div(me, TEAM)
    return to, back


def remote(source, target, send, receive, device):
    return pltpu.make_async_remote_copy(
        src_ref=source,
        dst_ref=target,
        send_sem=send,
        recv_sem=receive,
        device_id=(device,),
        device_id_type=MESH,
    )


def params(collective, limit=None):
    if limit is None:
        return pltpu.CompilerParams(collective_id=collective, has_side_effects=True)
    return pltpu.CompilerParams(
        collective_id=collective, has_side_effects=True, vmem_limit_bytes=limit
    )


class Gather:
    def __init__(self, begin, x, o, me):
        self.begin, self.x, self.o, self.me = begin, x, o, me
        self.place = lax.rem(me, TEAM)
        self.half = x.shape[0] // 2

    def part(self, ref, which):
        return ref.at[pl.ds(which * self.half, self.half)]

    def first(self, which, mask):
        target = self.part(self.o.at[self.place], which)
        return self.begin(self.part(self.x, which), target, flipped(self.me, mask))

    def relay(self, origin, which, mask):
        ref = self.part(self.o.at[flipped(self.place, origin)], which)
        return self.begin(ref, ref, flipped(self.me, mask))

    def start(self):
        self.x0, self.y1 = self.first(0, 2), self.first(1, 4)
        self.x1, self.y0 = self.first(1, 2), self.first(0, 4)
        self.late = [self.first(0, 1), self.first(1, 1)]

    def forward(self):
        self.x0.wait_recv()
        self.d0 = self.relay(2, 0, 4)
        self.y1.wait_recv()
        self.d1 = self.relay(4, 1, 2)
        self.late += [self.relay(2, 0, 1), self.relay(4, 1, 1)]

    def across(self):
        self.x1.wait_recv()
        self.late.append(self.relay(2, 1, 1))
        self.y0.wait_recv()
        self.late.append(self.relay(4, 0, 1))

    def diagonal(self):
        self.d0.wait_recv()
        self.late.append(self.relay(6, 0, 1))
        self.d1.wait_recv()
        self.late.append(self.relay(6, 1, 1))

    def arrive(self):
        for copy in self.late:
            copy.wait_recv()


class Sender:
    def __init__(self, send, receive):
        self.send, self.receive, self.count, self.started = send, receive, 0, []

    def take(self):
        self.count += 1
        return self.count - 1

    def __call__(self, source, target, device):
        k = self.take()
        copy = remote(source, target, self.send.at[k], self.receive.at[k], device)
        copy.start()
        self.started.append(copy)
        return copy

    def finish(self):
        for copy in self.started:
            copy.wait_send()


def gather_kernel(x_ref, o_ref, send, receive, own):
    me = lax.axis_index("fsdp")
    keep = pltpu.make_async_copy(x_ref, o_ref.at[lax.rem(me, TEAM)], own)
    keep.start()
    greet(me, (1, 2, 4))
    sender = Sender(send, receive)
    moves = Gather(sender, x_ref, o_ref, me)
    moves.start()
    moves.forward()
    moves.across()
    moves.diagonal()
    moves.arrive()
    sender.finish()
    keep.wait()


def gather(x, collective):
    rows, width = x.shape
    whole = pl.pallas_call(
        gather_kernel,
        out_shape=jax.ShapeDtypeStruct((TEAM, rows, width), x.dtype),
        in_specs=[pl.BlockSpec(memory_space=pltpu.VMEM)],
        out_specs=pl.BlockSpec(memory_space=pl.ANY),
        scratch_shapes=[
            pltpu.SemaphoreType.DMA((14,)),
            pltpu.SemaphoreType.DMA((14,)),
            pltpu.SemaphoreType.DMA,
        ],
        compiler_params=params(collective),
    )(x)
    return whole.reshape(TEAM * rows, width)


TILE = 512


def reduce_kernel(turned, cut, pairs, *refs):
    lefts, rights = refs[:pairs], refs[pairs : 2 * pairs]
    out, mix, from_core, from_x, from_y, *rest = refs[2 * pairs :]
    left_here, right_here = rest[:pairs], rest[pairs : 2 * pairs]
    send, receive, own = rest[2 * pairs :]
    me = lax.axis_index("fsdp")
    place = lax.rem(me, TEAM)
    core = lax.rem(place, 2)
    rows, width = out.shape
    half = rows // 2
    step = 16
    chips = [lax.div(flipped(place, mask), 2) for mask in (6, 2, 4, 0)]

    loads = []

    def load(source, target):
        copy = pltpu.make_async_copy(source, target, own.at[len(loads)])
        copy.start()
        loads.append(copy)

    for k, (right, here) in enumerate(zip(rights, right_here)):
        if cut:
            load(right.at[pl.ds(k * here.shape[0], here.shape[0])], here)
        else:
            load(right, here)
    for left, here in zip(lefts, left_here):
        load(left, here)

    def product(j):
        @pl.loop(0, width // TILE)
        def _(t):
            at = pl.ds(pl.multiple_of(t * TILE, TILE), TILE)
            value = 0.0
            for left, right in zip(left_here, right_here):
                both = left[pl.ds(2 * chips[j], 2)].reshape(2 * rows, left.shape[2])
                if turned:
                    value = value + dot_last(both, right[at, :])
                else:
                    value = value + simple_product(both, right[:, at])
            mix[j, :, :, at] = value.astype(bf16).reshape(2, rows, TILE)

    across = []

    def cross(j):
        copy = remote(
            mix.at[j, 1 - core], from_core.at[j], send.at[j], receive.at[j], flipped(me, 1)
        )
        copy.start()
        across.append(copy)

    def combine(j):
        across[j].wait_recv()

        @pl.loop(0, rows // step)
        def _(i):
            at = pl.ds(i * step, step)
            mix[j, core, at, :] = (
                mix[j, core, at, :].astype(f32) + from_core[j, at, :].astype(f32)
            ).astype(bf16)

    def begin(j, which, ref, slot, mask, k):
        copy = remote(
            mix.at[j, core, pl.ds(which * half, half)],
            ref.at[slot],
            send.at[k],
            receive.at[k],
            flipped(me, mask),
        )
        copy.start()
        return copy

    def add_relayed(j, which, ref):
        @pl.loop(0, half // step)
        def _(i):
            at = pl.ds(which * half + i * step, step)
            mix[j, core, at, :] = (
                mix[j, core, at, :].astype(f32) + ref[0, pl.ds(i * step, step), :].astype(f32)
            ).astype(bf16)

    greet(me, (1, 2, 4))
    for copy in loads:
        copy.wait()
    product(0)
    cross(0)
    product(1)
    combine(0)
    d_x = begin(0, 0, from_x, 0, 2, 4)
    d_y = begin(0, 1, from_y, 0, 4, 5)
    cross(1)
    product(2)
    cross(2)
    combine(1)
    x_0 = begin(1, 0, from_x, 1, 2, 6)
    combine(2)
    y_1 = begin(2, 1, from_y, 1, 4, 7)
    d_x.wait_recv()
    add_relayed(2, 0, from_x)
    y_0 = begin(2, 0, from_y, 2, 4, 8)
    d_y.wait_recv()
    add_relayed(1, 1, from_y)
    x_1 = begin(1, 1, from_x, 2, 2, 9)
    product(3)
    cross(3)
    across[3].wait_recv()

    def finish(which, slot_x, slot_y):
        @pl.loop(0, half // step)
        def _(i):
            at = pl.ds(which * half + i * step, step)
            here = pl.ds(i * step, step)
            out[at, :] = (mix[3, core, at, :].astype(f32) + from_core[3, at, :].astype(f32)) + (
                from_x[slot_x, here, :].astype(f32) + from_y[slot_y, here, :].astype(f32)
            )

    x_0.wait_recv()
    y_0.wait_recv()
    finish(0, 1, 2)
    y_1.wait_recv()
    x_1.wait_recv()
    finish(1, 2, 1)
    for copy in (*across, d_x, d_y, x_0, x_1, y_0, y_1):
        copy.wait_send()


def reduce(lefts, rights, turned, collective, cut=False):
    _, rows, _ = lefts[0].shape
    pairs = len(lefts)
    width = rights[0].shape[0] if turned else rights[0].shape[-1]
    depth = sum(left.shape[2] for left in lefts)
    anywhere = pl.BlockSpec(memory_space=pl.ANY)
    here = [(width, x.shape[2]) if turned else (x.shape[2], width) for x in lefts]
    loads = 2 * pairs
    return pl.pallas_call(
        functools.partial(reduce_kernel, turned, cut, pairs),
        out_shape=jax.ShapeDtypeStruct((rows, width), f32),
        in_specs=[anywhere] * (2 * pairs),
        out_specs=pl.BlockSpec(memory_space=pltpu.VMEM),
        scratch_shapes=[
            pltpu.VMEM((4, 2, rows, width), bf16),
            pltpu.VMEM((4, rows, width), bf16),
            pltpu.VMEM((3, rows // 2, width), bf16),
            pltpu.VMEM((3, rows // 2, width), bf16),
            *(pltpu.VMEM(x.shape, x.dtype) for x in lefts),
            *(pltpu.VMEM(shape, bf16) for shape in here),
            pltpu.SemaphoreType.DMA((10,)),
            pltpu.SemaphoreType.DMA((10,)),
            pltpu.SemaphoreType.DMA((loads,)),
        ],
        compiler_params=params(collective, LIMIT),
        cost_estimate=pl.CostEstimate(
            flops=2 * TEAM * rows * depth * width,
            bytes_accessed=2 * TEAM * rows * depth + 2 * depth * width + 4 * rows * width,
            transcendentals=0,
        ),
    )(*lefts, *rights)


class Line:
    def __init__(self, sender, ref, planes, me):
        self.sender, self.ref, self.planes = sender, ref, planes
        self.plane, self.place = lax.div(me, TEAM), lax.rem(me, TEAM)
        self.flows = [(sign, [sender.take() for _ in range(planes - 1)]) for sign in (1, -1)]

    def passing(self, step, sign, ks, source):
        block = jnp.clip(source, 0, self.planes - 1)
        beyond = jnp.clip(self.plane + sign, 0, self.planes - 1) * TEAM + self.place
        ref, k = self.ref.at[block], ks[step]
        return remote(ref, ref, self.sender.send.at[k], self.sender.receive.at[k], beyond)

    def goes(self, step, sign):
        source, onward = self.plane - sign * step, self.plane + sign
        last = self.planes - 1
        return (source >= 0) & (source <= last) & (onward >= 0) & (onward <= last)

    def start(self, step):
        for sign, ks in self.flows:
            going = self.passing(step, sign, ks, self.plane - sign * step)
            pl.when(self.goes(step, sign))(going.start)

    def arrive(self, step):
        for sign, ks in self.flows:
            source = self.plane - sign * (step + 1)
            coming = self.passing(step, sign, ks, source)
            pl.when((source >= 0) & (source <= self.planes - 1))(coming.wait_recv)

    def sent(self, step):
        for sign, ks in self.flows:
            going = self.passing(step, sign, ks, self.plane - sign * step)
            pl.when(self.goes(step, sign))(going.wait_send)


SWAP_ORDER = (6, 7, 2, 3, 4, 5, 1)


def open_kernel(planes, query_in, key_in, value_in, output_in, tokens_in, cot_in, *refs):
    smalls, refs = refs[:5], refs[5:]
    qkv, output, tokens, cot, *gain_refs, numbers = refs[:9]
    small_in, small, send, receive, own = refs[9:]
    slots, sequence = smalls[4].shape
    small_in[...] = jnp.zeros_like(small_in)
    for k, ref in enumerate(smalls):
        small_in[k : k + ref.shape[0], : ref.shape[1]] = ref[...].astype(f32)
    me = lax.axis_index("fsdp")
    place = lax.rem(me, TEAM)
    plane = lax.div(me, TEAM)
    team = me - place
    others = [lax.rem(me + TEAM * k, planes * TEAM) for k in range(1, planes)]
    sender = Sender(send, receive)
    keeps = []

    def keep(source, target):
        copy = pltpu.make_async_copy(source, target, own.at[len(keeps)])
        copy.start()
        keeps.append(copy)

    qkv_parts, at = [], 0
    for ref in (query_in, key_in, value_in):
        part = ref.shape[1] // TEAM
        qkv_parts.append((ref, part, qkv.at[plane, place, :, pl.ds(at, part)]))
        at += part

    def columns(ref, part, target):
        return ref.at[:, pl.ds(pl.multiple_of(target * part, part), part)]

    for ref, part, target in qkv_parts:
        keep(columns(ref, part, place), target)
    keep(small_in, small.at[me])
    keep(tokens_in, tokens.at[place])
    keep(cot_in, cot.at[place])
    to, back = head_owner(me, planes)
    greet(me, range(1, TEAM), others, (to, back))

    k = sender.take()
    over = remote(output_in, output.at[lax.rem(me, planes)], send.at[k], receive.at[k], to)
    home = remote(output_in, output.at[plane], send.at[k], receive.at[k], back)
    here = pltpu.make_async_copy(output_in, output.at[plane], own.at[len(keeps)])
    pl.when(to != me)(over.start)
    pl.when(to == me)(here.start)
    swaps = [
        sender(columns(ref, part, flipped(place, m)), target, flipped(me, m))
        for m in SWAP_ORDER
        for ref, part, target in qkv_parts
    ]
    near = [sender(small_in, small.at[me], flipped(me, m)) for m in SWAP_ORDER]
    qkv_line = Line(sender, qkv, planes, me)
    out_line = Line(sender, output, planes, me)
    rows_tokens = Gather(sender, tokens_in, tokens, me)
    rows_cot = Gather(sender, cot_in, cot, me)

    pl.when(to != me)(home.wait_recv)
    pl.when(to == me)(here.wait)
    out_line.start(0)
    for copy in swaps:
        copy.wait_recv()
    for copy in keeps[:3]:
        copy.wait()
    qkv_line.start(0)
    rows_tokens.start()
    rows_cot.start()
    rows_tokens.forward()
    out_line.arrive(0)
    if planes > 2:
        out_line.start(1)
    for copy in near:
        copy.wait_recv()
    keeps[3].wait()
    shared = small.at[pl.ds(team, TEAM)]
    far = [sender(shared, shared, other) for other in others]
    rows_tokens.across()
    for step in range(planes - 1):
        qkv_line.arrive(step)
        if step < planes - 2:
            qkv_line.start(step + 1)
            out_line.arrive(step + 1)
        if step < planes - 3:
            out_line.start(step + 2)
        if step == 0:
            rows_tokens.diagonal()
            rows_cot.forward()
        if step == 1:
            rows_cot.across()
            rows_cot.diagonal()
            for copy in far:
                copy.wait_recv()
            for k, ref in enumerate(gain_refs):
                part = smalls[k].shape[1]
                ref[...] = jnp.concatenate(
                    [small[i, k : k + 1, :part] for i in range(planes * TEAM)], axis=1
                )
            per_step = STEP // sequence
            for i in range(numbers.shape[0]):
                pieces = []
                for m in range(i * per_step, (i + 1) * per_step):
                    row = 4 + m % slots
                    pieces.append(small[team + m // slots, row : row + 1, :sequence] + 64.0 * m)
                numbers[i] = jnp.concatenate(pieces, axis=1)
    rows_tokens.arrive()
    rows_cot.arrive()
    pl.when(to != me)(over.wait_send)
    for step in range(planes - 1):
        qkv_line.sent(step)
        out_line.sent(step)
    sender.finish()
    for copy in keeps[4:]:
        copy.wait()


def opening(query, key, value, output, tokens, cot, smalls, planes, collective):
    links = 29 + 4 * (planes - 1) + 28 + planes - 1
    anywhere = pl.BlockSpec(memory_space=pl.ANY)
    vmem = pl.BlockSpec(memory_space=pltpu.VMEM)
    like = jax.ShapeDtypeStruct
    rows = query.shape[0]
    width = (query.shape[1] + key.shape[1] + value.shape[1]) // TEAM
    devices = planes * TEAM
    return pl.pallas_call(
        functools.partial(open_kernel, planes),
        out_shape=(
            like((planes, TEAM, rows, width), bf16),
            like((planes, *output.shape), bf16),
            like((TEAM, *tokens.shape), bf16),
            like((TEAM, *cot.shape), bf16),
            *(like((1, devices * x.shape[1]), f32) for x in smalls[:4]),
            like((TEAM * tokens.shape[0] // STEP, 1, STEP), f32),
        ),
        in_specs=[vmem] * 11,
        out_specs=(anywhere,) * 4 + (vmem,) * 5,
        scratch_shapes=[
            pltpu.VMEM((8, 128), f32),
            pltpu.VMEM((devices, 8, 128), f32),
            pltpu.SemaphoreType.DMA((links,)),
            pltpu.SemaphoreType.DMA((links,)),
            pltpu.SemaphoreType.DMA((7,)),
        ],
        compiler_params=params(collective, LIMIT),
    )(query, key, value, output, tokens, cot, *smalls)


def units_kernel(planes, parts, gate_in, up_in, *refs):
    gate_up, (sorted_units, send, receive, own) = refs[:parts], refs[parts:]
    me = lax.axis_index("fsdp")
    place = lax.rem(me, TEAM)
    greet(me, range(1, TEAM))
    sender = Sender(send, receive)
    block = gate_in.shape[1] // (planes * TEAM)
    some = planes // parts
    units = some * block
    moves = []
    for k in range(parts):
        for q in range(TEAM):
            for j, ref in enumerate((gate_in, up_in)):
                starts = [(TEAM * g + q) * block for g in range(k * some, (k + 1) * some)]
                sorted_units[k, q, :, j * units : (j + 1) * units] = jnp.concatenate(
                    [ref[:, at : at + block] for at in starts], axis=1
                )
        moves += [
            sender(sorted_units.at[k, flipped(place, m)], gate_up[k].at[place], flipped(me, m))
            for m in SWAP_ORDER
        ]
    keeps = [
        pltpu.make_async_copy(sorted_units.at[k, place], gate_up[k].at[place], own.at[k])
        for k in range(parts)
    ]
    for copy in keeps:
        copy.start()
    for copy in (*moves, *keeps):
        copy.wait()


def units_out(gate, up, planes, parts, collective):
    vmem = pl.BlockSpec(memory_space=pltpu.VMEM)
    anywhere = pl.BlockSpec(memory_space=pl.ANY)
    units = (TEAM, gate.shape[0], 2 * gate.shape[1] // TEAM // parts)
    links = (TEAM - 1) * parts
    return pl.pallas_call(
        functools.partial(units_kernel, planes, parts),
        out_shape=(jax.ShapeDtypeStruct(units, bf16),) * parts,
        in_specs=[vmem, vmem],
        out_specs=(anywhere,) * parts,
        scratch_shapes=[
            pltpu.VMEM((parts, *units), bf16),
            pltpu.SemaphoreType.DMA((links,)),
            pltpu.SemaphoreType.DMA((links,)),
            pltpu.SemaphoreType.DMA((parts,)),
        ],
        compiler_params=params(collective, LIMIT),
    )(gate, up)


def units_home_kernel(planes, parts, *refs):
    x_refs, (gate_ref, up_ref, landed, send, receive, own) = refs[:parts], refs[parts:]
    me = lax.axis_index("fsdp")
    place = lax.rem(me, TEAM)
    keeps = [
        pltpu.make_async_copy(x.at[place], landed.at[k, place], own.at[k])
        for k, x in enumerate(x_refs)
    ]
    for copy in keeps:
        copy.start()
    greet(me, range(1, TEAM))
    sender = Sender(send, receive)
    moves = [
        sender(x.at[flipped(place, m)], landed.at[k, place], flipped(me, m))
        for k, x in enumerate(x_refs)
        for m in SWAP_ORDER
    ]
    for copy in moves:
        copy.wait_recv()
    for copy in keeps:
        copy.wait()
    block = gate_ref.shape[1] // (planes * TEAM)
    some = planes // parts
    span = TEAM * block
    for j, ref in enumerate((gate_ref, up_ref)):
        for g in range(planes):
            at = (j * some + g % some) * block
            ref[:, g * span : (g + 1) * span] = jnp.concatenate(
                [landed[g // some, q, :, at : at + block].astype(f32) for q in range(TEAM)],
                axis=1,
            )
    sender.finish()


def units_home(xs, planes, collective):
    parts = len(xs)
    _, rows, width = xs[0].shape
    vmem = pl.BlockSpec(memory_space=pltpu.VMEM)
    like = jax.ShapeDtypeStruct
    links = (TEAM - 1) * parts
    return pl.pallas_call(
        functools.partial(units_home_kernel, planes, parts),
        out_shape=(like((rows, TEAM * parts * width // 2), f32),) * 2,
        in_specs=[pl.BlockSpec(memory_space=pl.ANY)] * parts,
        out_specs=(vmem, vmem),
        scratch_shapes=[
            pltpu.VMEM((parts, *xs[0].shape), xs[0].dtype),
            pltpu.SemaphoreType.DMA((links,)),
            pltpu.SemaphoreType.DMA((links,)),
            pltpu.SemaphoreType.DMA((parts,)),
        ],
        compiler_params=params(collective, LIMIT),
    )(*xs)


def close_kernel(planes, x_ref, gains, *refs):
    query_ref, key_ref, value_ref, output_ref, gain_ref, *refs = refs
    landed, mine, near_in, mid, far_in, send, receive, own = refs
    from_heads = x_ref.at[pl.ds(TEAM * landed.shape[1], mine.shape[0])]
    me = lax.axis_index("fsdp")
    place = lax.rem(me, TEAM)
    plane = lax.div(me, TEAM)
    others = [lax.rem(me + TEAM * k, planes * TEAM) for k in range(1, planes)]
    rows = landed.shape[1]

    def part(target):
        return x_ref.at[pl.ds(pl.multiple_of(target * rows, rows), rows)]

    keep = pltpu.make_async_copy(part(place), landed.at[place], own.at[0])
    keep.start()
    back, to = head_owner(me, planes)
    greet(me, range(1, TEAM), others, (to, back))
    sender = Sender(send, receive)
    k = sender.take()
    over = remote(from_heads, mine, send.at[k], receive.at[k], to)
    here = pltpu.make_async_copy(from_heads, mine, own.at[1])
    pl.when(to != me)(over.start)
    pl.when(to == me)(here.start)
    near = [
        sender(gains.at[flipped(place, m)], near_in.at[m - 1], flipped(me, m)) for m in SWAP_ORDER
    ]
    moves = [
        sender(part(flipped(place, m)), landed.at[place], flipped(me, m)) for m in SWAP_ORDER
    ]
    for copy in near:
        copy.wait_recv()
    summed = gains[place]
    for mask in range(1, TEAM):
        summed = summed + near_in[mask - 1]
    mid[...] = summed
    far = [
        sender(mid.at[lax.rem(plane + k + 1, planes)], far_in.at[k], other)
        for k, other in enumerate(others)
    ]
    pl.when(to != me)(over.wait)
    pl.when(to == me)(here.wait)
    width = mine.shape[1]
    for c in range(output_ref.shape[1] // width):
        output_ref[:, c * width : (c + 1) * width] = mine[c * rows : (c + 1) * rows].astype(f32)
    for copy in moves:
        copy.wait_recv()
    keep.wait()
    at = 0
    for ref in (query_ref, key_ref, value_ref):
        part_width = ref.shape[1] // TEAM
        for q in range(TEAM):
            ref[:, q * part_width : (q + 1) * part_width] = landed[
                q, :, at : at + part_width
            ].astype(f32)
        at += part_width
    for copy in far:
        copy.wait_recv()
    result = mid[plane]
    for k in range(planes - 1):
        result = result + far_in[k]
    gain_ref[...] = result
    sender.finish()


def closing(x, gains, rows, widths, planes, collective):
    links = 2 * (TEAM - 1) + planes
    block = gains.shape[2:]
    vmem = pl.BlockSpec(memory_space=pltpu.VMEM)
    like = jax.ShapeDtypeStruct
    return pl.pallas_call(
        functools.partial(close_kernel, planes),
        out_shape=(*(like((rows, w), f32) for w in widths), like(block, f32)),
        in_specs=[pl.BlockSpec(memory_space=pl.ANY), vmem],
        out_specs=(vmem,) * 5,
        scratch_shapes=[
            pltpu.VMEM((TEAM, rows, x.shape[1]), x.dtype),
            pltpu.VMEM((x.shape[0] - TEAM * rows, x.shape[1]), x.dtype),
            pltpu.VMEM((TEAM - 1, planes, *block), f32),
            pltpu.VMEM((planes, *block), f32),
            pltpu.VMEM((planes - 1, *block), f32),
            pltpu.SemaphoreType.DMA((links,)),
            pltpu.SemaphoreType.DMA((links,)),
            pltpu.SemaphoreType.DMA((2,)),
        ],
        compiler_params=params(collective, LIMIT),
    )(x, gains)


def visible_and_tables(ids_row, table):
    rows = ids_row.shape[1]
    row_at = lax.broadcasted_iota(jnp.int32, (rows, rows), 0)
    column_at = lax.broadcasted_iota(jnp.int32, (rows, rows), 1)
    ids_column = jnp.sum(jnp.where(row_at == column_at, ids_row, 0.0), axis=1, keepdims=True)
    visible = (ids_column == ids_row) & (column_at <= row_at)
    sequence = table.shape[0]
    place = jnp.sum(visible.astype(f32), axis=1, keepdims=True) - 1.0
    at = lax.broadcasted_iota(jnp.int32, (rows, sequence), 1).astype(f32)
    chosen = (at == place).astype(bf16)
    both = simple_product(chosen, table)
    width = 2 * HEAD_SIZE
    both = (both[:, :width] + both[:, width : 2 * width]) + both[:, 2 * width :]
    return visible, both[:, :HEAD_SIZE], both[:, HEAD_SIZE:]


def softmax(query, key, visible):
    scores = dot_last(query, key) * HEAD_SIZE ** (-0.5)
    scores = jnp.where(visible, scores, -1e30)
    expos = jnp.exp(scores - jnp.max(scores, axis=1, keepdims=True))
    return expos / jnp.sum(expos, axis=1, keepdims=True)


def attend_kernel(
    x_ref, gain, weight, ids_row, table, query_gain, key_gain,
    normed_ref, raw_ref, turned_ref, value_ref, context_ref,
):
    x = x_ref[...].astype(f32)
    scale = lax.rsqrt(jnp.mean(x * x, axis=1, keepdims=True) + epsilon)
    normed = (x * scale * gain[...]).astype(bf16)
    normed_ref[...] = normed
    projected = simple_product(normed, weight[...])
    visible, cosine, sine = visible_and_tables(ids_row[0], table[...])
    heads = context_ref.shape[1] // HEAD_SIZE
    raw_ref[...] = projected[:, : (heads + 1) * HEAD_SIZE]
    value = projected[:, (heads + 1) * HEAD_SIZE :].astype(bf16)
    value_ref[...] = value
    turned = []
    for h in range(heads + 1):
        raw = projected[:, h * HEAD_SIZE : (h + 1) * HEAD_SIZE]
        head_gain = query_gain if h < heads else key_gain
        y = raw * lax.rsqrt(jnp.mean(raw * raw, axis=1, keepdims=True) + epsilon) * head_gain[...]
        y = y * cosine + pltpu.roll(y, HEAD_SIZE // 2, 1) * sine
        turned.append(y.astype(bf16))
        turned_ref[:, h * HEAD_SIZE : (h + 1) * HEAD_SIZE] = turned[-1]
    for h in range(heads):
        probs = softmax(turned[h], turned[heads], visible).astype(bf16)
        context = simple_product(probs, value)
        context_ref[:, h * HEAD_SIZE : (h + 1) * HEAD_SIZE] = context.astype(bf16)


def by_step(*shape):
    return pl.BlockSpec(shape, lambda i: (i, *(0 for _ in shape[1:])))


def fixed(*shape):
    return pl.BlockSpec(shape, lambda i: tuple(0 for _ in shape))


def attend(x, gain, weight, ids, table, query_gain, key_gain):
    rows, width = x.shape
    out = weight.shape[1]
    like = jax.ShapeDtypeStruct
    heads = out - 2 * HEAD_SIZE
    return pl.pallas_call(
        attend_kernel,
        grid=(rows // STEP,),
        out_shape=(
            like((rows, width), bf16),
            like((rows, heads + HEAD_SIZE), f32),
            like((rows, heads + HEAD_SIZE), bf16),
            like((rows, HEAD_SIZE), bf16),
            like((rows, heads), bf16),
        ),
        in_specs=[
            by_step(STEP, width),
            fixed(1, width),
            fixed(width, out),
            by_step(1, 1, STEP),
            fixed(*table.shape),
            fixed(1, HEAD_SIZE),
            fixed(1, HEAD_SIZE),
        ],
        out_specs=(
            by_step(STEP, width),
            by_step(STEP, heads + HEAD_SIZE),
            by_step(STEP, heads + HEAD_SIZE),
            by_step(STEP, HEAD_SIZE),
            by_step(STEP, heads),
        ),
        compiler_params=pltpu.CompilerParams(vmem_limit_bytes=LIMIT),
        cost_estimate=pl.CostEstimate(
            flops=2 * rows * width * out, bytes_accessed=8 * rows * width, transcendentals=0
        ),
    )(x, gain, weight, ids, table, query_gain, key_gain)


def attend_back_kernel(
    grad_ref, out_weight, context_ref, raw_ref, turned_ref, value_ref, normed_ref,
    ids_row, table, query_gain, key_gain,
    grad_raw_ref, merged_ref, grad_gains_ref, out_sum, weight_sum,
):
    step = pl.program_id(0)

    @pl.when(step == 0)
    def _():
        out_sum[...] = jnp.zeros_like(out_sum)
        weight_sum[...] = jnp.zeros_like(weight_sum)
        grad_gains_ref[...] = jnp.zeros_like(grad_gains_ref)

    grad = grad_ref[...]
    grad_context = dot_last(grad, out_weight[...]).astype(bf16)
    out_sum[...] += dot_first(context_ref[...], grad)
    visible, cosine, sine = visible_and_tables(ids_row[0], table[...])
    heads = context_ref.shape[1] // HEAD_SIZE
    value = value_ref[...]
    key = turned_ref[:, heads * HEAD_SIZE :]
    grads = []
    grad_value = 0.0
    grad_key = 0.0
    for h in range(heads):
        at = slice(h * HEAD_SIZE, (h + 1) * HEAD_SIZE)
        query = turned_ref[:, at]
        probs = softmax(query, key, visible)
        grad_value = grad_value + dot_first(probs.astype(bf16), grad_context[:, at])
        grad_probs = dot_last(grad_context[:, at], value)
        inner = jnp.sum(probs * grad_probs, axis=1, keepdims=True)
        grad_scores = (probs * (grad_probs - inner)).astype(bf16)
        grads.append(simple_product(grad_scores, key) * HEAD_SIZE ** (-0.5))
        grad_key = grad_key + dot_first(grad_scores, query) * HEAD_SIZE ** (-0.5)
    grads.append(grad_key)
    parts = []
    for h in range(heads + 1):
        raw = raw_ref[:, h * HEAD_SIZE : (h + 1) * HEAD_SIZE]
        head_gain = query_gain[...] if h < heads else key_gain[...]
        scale = lax.rsqrt(jnp.mean(raw * raw, axis=1, keepdims=True) + epsilon)
        turned = grads[h] * cosine + pltpu.roll(grads[h] * sine, HEAD_SIZE // 2, 1)
        row = 0 if h < heads else 1
        grad_gains_ref[row : row + 1, :] += jnp.sum(turned * raw * scale, axis=0, keepdims=True)
        turned = turned * head_gain
        mean = jnp.mean(turned * raw, axis=1, keepdims=True)
        parts.append((turned * scale - raw * (scale * scale * scale * mean)).astype(bf16))
    parts.append(grad_value.astype(bf16))
    grad_raw = jnp.concatenate(parts, axis=1)
    grad_raw_ref[...] = grad_raw
    weight_sum[...] += dot_first(normed_ref[...], grad_raw)

    @pl.when(step == pl.num_programs(0) - 1)
    def _():
        planes, _, width = merged_ref.shape
        rows, block = weight_sum.shape[0] // planes, out_sum.shape[0] // planes
        for g in range(planes):
            merged_ref[g, :rows] = weight_sum[g * rows : (g + 1) * rows].astype(bf16)
            for c in range(out_sum.shape[1] // width):
                at = rows + c * block
                merged_ref[g, at : at + block] = out_sum[
                    g * block : (g + 1) * block, c * width : (c + 1) * width
                ].astype(bf16)


def attend_back(
    grad, out_weight, context, raw, turned, value, normed, ids, table, query_gain, key_gain, planes
):
    rows, width = grad.shape
    heads = context.shape[1]
    out = heads + 2 * HEAD_SIZE
    merged = (planes, (width + heads * width // out) // planes, out)
    like = jax.ShapeDtypeStruct
    return pl.pallas_call(
        attend_back_kernel,
        grid=(rows // STEP,),
        out_shape=(
            like((rows, out), bf16),
            like(merged, bf16),
            like((8, HEAD_SIZE), f32),
        ),
        in_specs=[
            by_step(STEP, width),
            fixed(heads, width),
            by_step(STEP, heads),
            by_step(STEP, heads + HEAD_SIZE),
            by_step(STEP, heads + HEAD_SIZE),
            by_step(STEP, HEAD_SIZE),
            by_step(STEP, width),
            by_step(1, 1, STEP),
            fixed(*table.shape),
            fixed(1, HEAD_SIZE),
            fixed(1, HEAD_SIZE),
        ],
        out_specs=(
            by_step(STEP, out),
            fixed(*merged),
            fixed(8, HEAD_SIZE),
        ),
        scratch_shapes=[pltpu.VMEM((heads, width), f32), pltpu.VMEM((width, out), f32)],
        compiler_params=pltpu.CompilerParams(vmem_limit_bytes=LIMIT),
        cost_estimate=pl.CostEstimate(
            flops=2 * rows * width * (out + 2 * heads),
            bytes_accessed=8 * rows * width,
            transcendentals=0,
        ),
    )(grad, out_weight, context, raw, turned, value, normed, ids, table, query_gain, key_gain)


def hidden(two, weight):
    return simple_product(two, weight)


def hidden_grads(both, cot, down):
    units = both.shape[1] // 2
    gate, up = both[:, :units], both[:, units:]
    grad_act = dot_last(cot, down)
    sigma = 1.0 / (1.0 + jnp.exp(-gate))
    silu_gate = gate * sigma
    act = (silu_gate * up).astype(bf16)
    grad_gate = (grad_act * up * (sigma * (1.0 + gate * (1.0 - sigma)))).astype(bf16)
    grad_up = (grad_act * silu_gate).astype(bf16)
    return act, grad_gate, grad_up


def feed_kernel(
    two_in, cot_in, weight_in, down_in, two_out, act, grad_both,
    two, cot, weight, down, both, send, receive, own,
):
    me = lax.axis_index("fsdp")
    place = lax.rem(me, TEAM)
    keeps = []
    for source, target in (
        (two_in, two.at[place]),
        (weight_in, weight),
        (down_in.at[pl.ds(0, down.shape[0])], down),
        (cot_in, cot),
    ):
        copy = pltpu.make_async_copy(source, target, own.at[len(keeps)])
        copy.start()
        keeps.append(copy)
    greet(me, (1, 2, 4))
    sender = Sender(send, receive)
    moves = Gather(sender, two_in, two, me)
    moves.start()
    rows, units = act.shape[1:]
    outs = []

    def work(mask):
        chip = pl.ds(2 * lax.div(flipped(place, mask), 2), 2)
        copy = pltpu.make_async_copy(two.at[chip], two_out.at[chip], own.at[4 + len(outs)])
        copy.start()
        outs.append(copy)
        flat = two[chip].reshape(2 * rows, two.shape[2])
        both[...] = simple_product(flat, weight[...])
        flat = cot[chip].reshape(2 * rows, two.shape[2])
        a, grad_gate, grad_up = hidden_grads(both[...], flat, down[...])
        act[chip] = a.reshape(2, rows, units)
        grad_both[chip, :, :units] = grad_gate.reshape(2, rows, units)
        grad_both[chip, :, units:] = grad_up.reshape(2, rows, units)

    moves.forward()
    moves.across()
    for copy in keeps:
        copy.wait()
    for copy in moves.late[:2]:
        copy.wait_recv()
    work(0)
    moves.diagonal()
    for mask, first, second in ((2, 2, 4), (4, 3, 5), (6, 6, 7)):
        moves.late[first].wait_recv()
        moves.late[second].wait_recv()
        work(mask)
    sender.finish()
    for copy in outs:
        copy.wait()


def feed(two, cot, weight, down, collective):
    rows, width = two.shape
    units = weight.shape[1] // 2
    vmem = pl.BlockSpec(memory_space=pltpu.VMEM)
    anywhere = pl.BlockSpec(memory_space=pl.ANY)
    like = jax.ShapeDtypeStruct
    return pl.pallas_call(
        feed_kernel,
        out_shape=(
            like((TEAM, rows, width), bf16),
            like((TEAM, rows, units), bf16),
            like((TEAM, rows, 2 * units), bf16),
        ),
        in_specs=[anywhere] * 4,
        out_specs=(anywhere, vmem, vmem),
        scratch_shapes=[
            pltpu.VMEM((TEAM, rows, width), bf16),
            pltpu.VMEM(cot.shape, bf16),
            pltpu.VMEM(weight.shape, bf16),
            pltpu.VMEM((units, width), bf16),
            pltpu.VMEM((2 * rows, 2 * units), f32),
            pltpu.SemaphoreType.DMA((14,)),
            pltpu.SemaphoreType.DMA((14,)),
            pltpu.SemaphoreType.DMA((8,)),
        ],
        compiler_params=params(collective, LIMIT),
        cost_estimate=pl.CostEstimate(
            flops=6 * TEAM * rows * width * units,
            bytes_accessed=6 * TEAM * rows * width,
            transcendentals=0,
        ),
    )(two, cot, weight, down)


def feed_rest_kernel(two, cot, weight, down, act, grad_both):
    blocks, rows, units = act.shape
    both = simple_product(two[...].reshape(blocks * rows, -1), weight[...])
    flat = cot[...].reshape(blocks * rows, -1)
    a, grad_gate, grad_up = hidden_grads(both, flat, down[...])
    act[...] = a.reshape(blocks, rows, units)
    grad_both[:, :, :units] = grad_gate.reshape(blocks, rows, units)
    grad_both[:, :, units:] = grad_up.reshape(blocks, rows, units)


def feed_rest(two, cot, weight, down, part):
    _, rows, width = two.shape
    units = weight.shape[1] // 2
    like = jax.ShapeDtypeStruct
    return pl.pallas_call(
        feed_rest_kernel,
        grid=(TEAM // 2,),
        out_shape=(like((TEAM, rows, units), bf16), like((TEAM, rows, 2 * units), bf16)),
        in_specs=[
            by_step(2, rows, width),
            by_step(2, rows, width),
            fixed(*weight.shape),
            pl.BlockSpec((units, width), lambda i: (part, 0)),
        ],
        out_specs=(by_step(2, rows, units), by_step(2, rows, 2 * units)),
        compiler_params=pltpu.CompilerParams(vmem_limit_bytes=LIMIT),
        cost_estimate=pl.CostEstimate(
            flops=6 * TEAM * rows * width * units,
            bytes_accessed=4 * TEAM * rows * width,
            transcendentals=0,
        ),
    )(two, cot, weight, down)


def local(
    devices,
    tokens,
    segments,
    micro_live,
    cotangent,
    w_query,
    key_weight,
    value_weight,
    w_output,
    attn_gain,
    query_norm_gain,
    key_gain,
    w_gate,
    w_up,
    w_down,
    mlp_gain,
):
    planes = devices // TEAM
    lines = [[place + TEAM * k for k in range(planes)] for place in range(TEAM)]
    slots, sequence = segments.shape
    token_count, width = tokens.shape
    groups = QUERY_HEADS // KEY_VALUE_HEADS
    rows = w_query.shape[0]
    parts = 2 if planes % 2 == 0 else 1
    team_rows = TEAM * token_count
    head_width = groups * HEAD_SIZE
    me = lax.axis_index("fsdp")
    plane = me // TEAM

    def gather_line(x):
        return lax.all_gather(x, "fsdp", axis=0, tiled=True, axis_index_groups=lines)

    def sum_line(x):
        return lax.psum_scatter(
            x, "fsdp", scatter_dimension=0, tiled=True, axis_index_groups=lines
        )

    slot_live = (lax.broadcasted_iota(jnp.int32, (slots, 1), 0) < micro_live[0]).astype(f32)
    row_live = jnp.broadcast_to(slot_live, (slots, sequence)).reshape(token_count, 1)
    cot_b = cotangent * row_live.astype(bf16)

    down_weight = gather_line(w_down)
    unit_slices = units_out(w_gate, w_up, planes, parts, 3)
    query_in, *unit_slices = lax.optimization_barrier((w_query, *unit_slices))
    smalls = [x[None] for x in (attn_gain, mlp_gain, query_norm_gain, key_gain)] + [segments]
    opened = opening(
        query_in, key_weight, value_weight, w_output, tokens, cot_b, smalls, planes, 1
    )
    qkv_weight, output_weight, team_tokens, team_cot = opened[:4]
    norm_gain, mlp_norm_gain, qgain, kgain, ids = opened[4:]
    mlp_norm_gain = mlp_norm_gain.reshape(width)
    qkv_weight = qkv_weight.reshape(width, -1)
    output_weight = output_weight.reshape(head_width, width)
    *unit_slices, _ = lax.optimization_barrier((*unit_slices, qkv_weight))
    unit_weights = [gather_line(x.reshape(TEAM * rows, -1)) for x in unit_slices]
    table = jnp.asarray(rotation_tables(sequence))

    inputs = tokens.astype(f32)
    team_normed, raw, turned, value_b, context_b = attend(
        team_tokens.reshape(team_rows, width), norm_gain, qkv_weight, ids, table, qgain, kgain
    )
    middle = inputs + reduce(
        [context_b.reshape(TEAM, token_count, head_width)], [output_weight], False, 2
    )

    normed_two = root_mean_square_norm(middle, mlp_norm_gain).astype(bf16)
    team_two, act, grad_both = feed(normed_two, team_cot, unit_weights[0], down_weight, 0)
    acts, grads_both = [act], [grad_both]
    flat_two = team_two.reshape(team_rows, width)

    def unit_grads(grad_both):
        return dot_first(flat_two, grad_both.reshape(team_rows, -1)).astype(bf16)

    grad_units = [unit_grads(grad_both)]
    for k in range(1, parts):
        rest_two, grad_units[k - 1] = lax.optimization_barrier((team_two, grad_units[k - 1]))
        act, grad_both = feed_rest(rest_two, team_cot, unit_weights[k], down_weight, k)
        acts.append(act)
        grads_both.append(grad_both)
        grad_units.append(unit_grads(grad_both))
    grad_units = [sum_line(g) for g in grad_units]
    grad_down = sum_line(
        jnp.concatenate(
            [
                dot_first(a.reshape(team_rows, -1), team_cot.reshape(team_rows, width))
                for a in acts
            ],
            axis=0,
        ).astype(bf16)
    )
    grad_normed_two = reduce(grads_both, unit_weights, True, 4)
    _, pull_two = jax.vjp(root_mean_square_norm, middle, mlp_norm_gain)
    middle_part, grad_mgain = pull_two(grad_normed_two)
    grad_middle = cot_b.astype(f32) + middle_part
    team_grad = gather(grad_middle.astype(bf16), 10)

    grad_qkv, grad_attention, grad_head_gains = attend_back(
        team_grad,
        output_weight,
        context_b,
        raw,
        turned,
        value_b,
        team_normed,
        ids,
        table,
        qgain,
        kgain,
        planes,
    )
    grad_attention = sum_line(grad_attention.reshape(-1, grad_attention.shape[2]))
    grad_normed = reduce(
        [grad_qkv.reshape(TEAM, token_count, -1)], [qkv_weight], True, 5
    )
    _, pull_one = jax.vjp(root_mean_square_norm, inputs, norm_gain.reshape(width))
    input_part, grad_again = pull_one(grad_normed)
    grad_tokens = (grad_middle + input_part).astype(bf16)
    layer_out = (row_live * (middle + reduce(acts, [down_weight] * parts, False, 7, cut=True))).astype(bf16)

    def by_owner(vector):
        vector = vector.reshape(devices, -1)
        return jnp.pad(vector, ((0, 0), (0, 128 - vector.shape[1])))

    gains = jnp.stack(
        [by_owner(v) for v in (grad_again, grad_mgain, grad_head_gains[0], grad_head_gains[1])], axis=1
    )
    gains = jnp.pad(gains, ((0, 0), (0, 4), (0, 0)))
    gains = gains.reshape(planes, TEAM, 8, 128).transpose(1, 0, 2, 3)

    *grad_units, _ = lax.optimization_barrier((*grad_units, layer_out))
    grad_gate, grad_up = units_home(
        [g.reshape(TEAM, rows, -1) for g in grad_units], planes, 8
    )
    grad_attention, grad_gate, grad_up = lax.optimization_barrier(
        (grad_attention, grad_gate, grad_up)
    )
    grad_query, grad_key, grad_value_w, grad_output, gains = closing(
        grad_attention,
        gains,
        rows,
        (w_query.shape[1], key_weight.shape[1], value_weight.shape[1], width),
        planes,
        9,
    )
    grad_down, gains = lax.optimization_barrier((grad_down, gains))
    return (
        layer_out,
        grad_tokens,
        grad_query,
        grad_key,
        grad_value_w,
        grad_output,
        gains[0, : attn_gain.shape[0]],
        gains[2, : query_norm_gain.shape[0]],
        gains[3, : key_gain.shape[0]],
        grad_gate,
        grad_up,
        grad_down.astype(f32),
        gains[1, : mlp_gain.shape[0]],
    )


def solution(mesh):
    by_rows, by_entry = P("fsdp", None), P("fsdp")
    return jax.shard_map(
        functools.partial(local, mesh.shape["fsdp"]),
        mesh=mesh,
        in_specs=(
            by_rows,
            by_rows,
            by_entry,
            by_rows,
            by_rows,
            by_rows,
            by_rows,
            by_rows,
            by_entry,
            by_entry,
            by_entry,
            by_rows,
            by_rows,
            by_rows,
            by_entry,
        ),
        out_specs=(
            by_rows,
            by_rows,
            by_rows,
            by_rows,
            by_rows,
            by_rows,
            by_entry,
            by_entry,
            by_entry,
            by_rows,
            by_rows,
            by_rows,
            by_entry,
        ),
        check_vma=False,
    )
```

```python
import functools

import jax
import jax.numpy as jnp
import numpy as np
from jax import lax
from jax.experimental import pallas as pl
from jax.experimental.pallas import tpu as pltpu
from jax.sharding import PartitionSpec as P

QUERY_HEADS = 16
KEY_VALUE_HEADS = 8
HEAD_SIZE = 128
TEAM = 8
STEP = 256

epsilon = 1e-06
base_theta = 1000000.0
MESH = pl.DeviceIdType.MESH
LIMIT = 60 * 2**20
f32 = jnp.float32
bf16 = jnp.bfloat16


def root_mean_square_norm(values, gain):
    return values * lax.rsqrt(jnp.mean(values * values, axis=-1, keepdims=True) + epsilon) * gain


def rotation_tables(positions):
    half = HEAD_SIZE // 2
    powers = -np.arange(half, dtype=np.float32) * np.float32(2.0) / np.float32(HEAD_SIZE)
    freqs = np.power(np.float32(base_theta), powers).astype(np.float32)
    angles = np.arange(positions, dtype=np.float32)[:, None] * freqs
    cosine, sine = np.cos(angles), np.sin(angles)
    rest = np.concatenate([cosine, cosine, -sine, sine], axis=1).astype(np.float32)
    parts = []
    for _ in range(3):
        parts.append(rest.astype(jnp.bfloat16))
        rest = rest - parts[-1].astype(np.float32)
    return np.concatenate(parts, axis=1)


def dot_last(left, right):
    return lax.dot_general(
        left, right, (((1,), (1,)), ((), ())), preferred_element_type=jnp.float32
    )


def dot_first(left, right):
    return lax.dot_general(
        left, right, (((0,), (0,)), ((), ())), preferred_element_type=jnp.float32
    )


def simple_product(left, right):
    return jnp.dot(left, right, preferred_element_type=jnp.float32)


def flipped(index, mask):
    for bit in (1, 2, 4):
        if mask & bit:
            index = index + bit * (1 - 2 * lax.rem(lax.div(index, bit), 2))
    return index


def greet(me, masks, others=()):
    barrier = pltpu.get_barrier_semaphore()
    for device in (*(flipped(me, mask) for mask in masks), *others):
        pl.semaphore_signal(barrier, inc=1, device_id=(device,), device_id_type=MESH)
    pl.semaphore_wait(barrier, len(masks) + len(others))


def remote(source, target, send, receive, device):
    return pltpu.make_async_remote_copy(
        src_ref=source,
        dst_ref=target,
        send_sem=send,
        recv_sem=receive,
        device_id=(device,),
        device_id_type=MESH,
    )


def params(collective, limit=None):
    if limit is None:
        return pltpu.CompilerParams(collective_id=collective, has_side_effects=True)
    return pltpu.CompilerParams(
        collective_id=collective, has_side_effects=True, vmem_limit_bytes=limit
    )


class Gather:
    def __init__(self, begin, x, o, me):
        self.begin, self.x, self.o, self.me = begin, x, o, me
        self.place = lax.rem(me, TEAM)
        self.half = x.shape[0] // 2

    def part(self, ref, which):
        return ref.at[pl.ds(which * self.half, self.half)]

    def first(self, which, mask):
        target = self.part(self.o.at[self.place], which)
        return self.begin(self.part(self.x, which), target, flipped(self.me, mask))

    def relay(self, origin, which, mask):
        ref = self.part(self.o.at[flipped(self.place, origin)], which)
        return self.begin(ref, ref, flipped(self.me, mask))

    def start(self):
        self.x0, self.y1 = self.first(0, 2), self.first(1, 4)
        self.x1, self.y0 = self.first(1, 2), self.first(0, 4)
        self.late = [self.first(0, 1), self.first(1, 1)]

    def forward(self):
        self.x0.wait_recv()
        self.d0 = self.relay(2, 0, 4)
        self.y1.wait_recv()
        self.d1 = self.relay(4, 1, 2)
        self.late += [self.relay(2, 0, 1), self.relay(4, 1, 1)]

    def across(self):
        self.x1.wait_recv()
        self.late.append(self.relay(2, 1, 1))
        self.y0.wait_recv()
        self.late.append(self.relay(4, 0, 1))

    def diagonal(self):
        self.d0.wait_recv()
        self.late.append(self.relay(6, 0, 1))
        self.d1.wait_recv()
        self.late.append(self.relay(6, 1, 1))

    def arrive(self):
        for copy in self.late:
            copy.wait_recv()


class Sender:
    def __init__(self, send, receive):
        self.send, self.receive, self.count, self.started = send, receive, 0, []

    def take(self):
        self.count += 1
        return self.count - 1

    def __call__(self, source, target, device):
        k = self.take()
        copy = remote(source, target, self.send.at[k], self.receive.at[k], device)
        copy.start()
        self.started.append(copy)
        return copy

    def finish(self):
        for copy in self.started:
            copy.wait_send()


TILE = 512
STRIP = 16


class TeamSum:
    def __init__(self, sender, me, out, buffers, lefts, rights, turned):
        self.sender, self.me, self.out = sender, me, out
        self.mix, self.from_core, self.from_x, self.from_y = buffers
        self.lefts, self.rights, self.turned = lefts, rights, turned
        place = lax.rem(me, TEAM)
        self.core = lax.rem(place, 2)
        self.rows, self.width = out.shape
        self.half = self.rows // 2
        self.chips = [lax.div(flipped(place, mask), 2) for mask in (6, 2, 4, 0)]
        self.across = []

    def product(self, j):
        @pl.loop(0, self.width // TILE)
        def _(t):
            at = pl.ds(pl.multiple_of(t * TILE, TILE), TILE)
            value = 0.0
            for left, right in zip(self.lefts, self.rights):
                both = left[pl.ds(2 * self.chips[j], 2)].reshape(2 * self.rows, left.shape[2])
                if self.turned:
                    value = value + dot_last(both, right[at, :])
                else:
                    value = value + simple_product(both, right[:, at])
            self.mix[j, :, :, at] = value.astype(bf16).reshape(2, self.rows, TILE)

        self.across.append(
            self.sender(self.mix.at[j, 1 - self.core], self.from_core.at[j], flipped(self.me, 1))
        )

    def combine(self, j):
        self.across[j].wait_recv()

        @pl.loop(0, self.rows // STRIP)
        def _(i):
            at = pl.ds(i * STRIP, STRIP)
            self.mix[j, self.core, at, :] = (
                self.mix[j, self.core, at, :].astype(f32) + self.from_core[j, at, :].astype(f32)
            ).astype(bf16)

    def begin(self, j, which, ref, slot, mask):
        source = self.mix.at[j, self.core, pl.ds(which * self.half, self.half)]
        return self.sender(source, ref.at[slot], flipped(self.me, mask))

    def add_relayed(self, j, which, ref):
        @pl.loop(0, self.half // STRIP)
        def _(i):
            at = pl.ds(which * self.half + i * STRIP, STRIP)
            self.mix[j, self.core, at, :] = (
                self.mix[j, self.core, at, :].astype(f32)
                + ref[0, pl.ds(i * STRIP, STRIP), :].astype(f32)
            ).astype(bf16)

    def start(self):
        self.product(0)
        self.product(1)
        self.combine(0)
        self.d_x = self.begin(0, 0, self.from_x, 0, 2)
        self.d_y = self.begin(0, 1, self.from_y, 0, 4)
        self.product(2)
        self.combine(1)
        self.x_0 = self.begin(1, 0, self.from_x, 1, 2)
        self.combine(2)
        self.y_1 = self.begin(2, 1, self.from_y, 1, 4)

    def own(self):
        self.product(3)

    def relay(self):
        self.d_x.wait_recv()
        self.add_relayed(2, 0, self.from_x)
        self.y_0 = self.begin(2, 0, self.from_y, 2, 4)
        self.d_y.wait_recv()
        self.add_relayed(1, 1, self.from_y)
        self.x_1 = self.begin(1, 1, self.from_x, 2, 2)

    def gather_half(self, which, slot_x, slot_y):
        @pl.loop(0, self.half // STRIP)
        def _(i):
            at = pl.ds(which * self.half + i * STRIP, STRIP)
            here = pl.ds(i * STRIP, STRIP)
            self.out[at, :] = (
                self.mix[3, self.core, at, :].astype(f32) + self.from_core[3, at, :].astype(f32)
            ) + (
                self.from_x[slot_x, here, :].astype(f32) + self.from_y[slot_y, here, :].astype(f32)
            )

    def finish(self):
        self.across[3].wait_recv()
        self.x_0.wait_recv()
        self.y_0.wait_recv()
        self.gather_half(0, 1, 2)
        self.y_1.wait_recv()
        self.x_1.wait_recv()
        self.gather_half(1, 2, 1)


SUM_COPIES = 10


def sum_buffers(rows, width):
    return [
        pltpu.VMEM((4, 2, rows, width), bf16),
        pltpu.VMEM((4, rows, width), bf16),
        pltpu.VMEM((3, rows // 2, width), bf16),
        pltpu.VMEM((3, rows // 2, width), bf16),
    ]


class Loader:
    def __init__(self, sems):
        self.sems, self.copies = sems, []

    def __call__(self, source, target):
        copy = pltpu.make_async_copy(source, target, self.sems.at[len(self.copies)])
        copy.start()
        self.copies.append(copy)
        return copy

    def wait(self):
        for copy in self.copies:
            copy.wait()


def rows_of(ref, k, rows):
    return ref.at[pl.ds(k * rows, rows)]


def turned_product(left, right, out, part, parts):
    blocks, rows, units = left.shape
    width = right.shape[2]
    tiles = width // TILE
    flat = left[...].reshape(blocks * rows, units)

    @pl.loop(part * tiles // parts, (part + 1) * tiles // parts)
    def _(t):
        at = pl.ds(pl.multiple_of(t * TILE, TILE), TILE)
        value = dot_first(flat, right[:, :, at].reshape(blocks * rows, TILE))
        out[:, at] = value.astype(bf16)


def turned_rows(left, right, out, part, parts):
    blocks, rows, width = left.shape
    tiles = width // TILE
    flat = right[...].reshape(blocks * rows, right.shape[2])

    @pl.loop(part * tiles // parts, (part + 1) * tiles // parts)
    def _(t):
        at = pl.ds(pl.multiple_of(t * TILE, TILE), TILE)
        value = dot_first(left[:, :, at].reshape(blocks * rows, TILE), flat)
        out[at, :] = value.astype(bf16)


def sum_kernel(left, right, out, *rest):
    buffers, (left_here, right_here, send, receive, own) = rest[:4], rest[4:]
    me = lax.axis_index("fsdp")
    loader = Loader(own)
    loader(right, right_here)
    loader(left, left_here)
    greet(me, (1, 2, 4))
    loader.wait()
    sender = Sender(send, receive)
    total = TeamSum(sender, me, out, buffers, [left_here], [right_here], False)
    total.start()
    total.own()
    total.relay()
    total.finish()
    sender.finish()


def team_sum(left, right, collective):
    _, rows, depth = left.shape
    width = right.shape[1]
    anywhere = pl.BlockSpec(memory_space=pl.ANY)
    return pl.pallas_call(
        sum_kernel,
        out_shape=jax.ShapeDtypeStruct((rows, width), f32),
        in_specs=[anywhere, anywhere],
        out_specs=pl.BlockSpec(memory_space=pltpu.VMEM),
        scratch_shapes=[
            *sum_buffers(rows, width),
            pltpu.VMEM(left.shape, bf16),
            pltpu.VMEM(right.shape, bf16),
            pltpu.SemaphoreType.DMA((SUM_COPIES,)),
            pltpu.SemaphoreType.DMA((SUM_COPIES,)),
            pltpu.SemaphoreType.DMA((2,)),
        ],
        compiler_params=params(collective, LIMIT),
        cost_estimate=pl.CostEstimate(
            flops=2 * TEAM * rows * depth * width,
            bytes_accessed=2 * TEAM * rows * depth + 2 * depth * width + 4 * rows * width,
            transcendentals=0,
        ),
    )(left, right)


def feed_back_kernel(parts, two, *refs):
    grads, weights, refs = refs[:parts], refs[parts : 2 * parts], refs[2 * parts :]
    out, weight_out, buffers, refs = refs[0], refs[1], refs[2:6], refs[6:]
    grads_here, weights_here = refs[:parts], refs[parts : 2 * parts]
    two_here, send, receive, own = refs[2 * parts :]
    me = lax.axis_index("fsdp")
    loader = Loader(own)
    for source, target in zip((*grads, *weights), (*grads_here, *weights_here)):
        loader(source, target)
    greet(me, (1, 2, 4))
    loader.wait()
    loader(two, two_here)
    sender = Sender(send, receive)
    total = TeamSum(sender, me, out, buffers, grads_here, weights_here, True)
    total.start()
    loader.copies[-1].wait()
    total.relay()
    total.own()
    turned_rows(two_here, grads_here[-1], weight_out, 0, 1)
    total.finish()
    sender.finish()


def feed_back(two, grads, weights, collective):
    _, rows, width = two.shape
    parts, units = len(grads), grads[0].shape[2]
    anywhere = pl.BlockSpec(memory_space=pl.ANY)
    vmem = pl.BlockSpec(memory_space=pltpu.VMEM)
    like = jax.ShapeDtypeStruct
    return pl.pallas_call(
        functools.partial(feed_back_kernel, parts),
        out_shape=(like((rows, width), f32), like((width, units), bf16)),
        in_specs=[anywhere] * (1 + 2 * parts),
        out_specs=(vmem, vmem),
        scratch_shapes=[
            *sum_buffers(rows, width),
            *(pltpu.VMEM(x.shape, bf16) for x in (*grads, *weights, two)),
            pltpu.SemaphoreType.DMA((SUM_COPIES,)),
            pltpu.SemaphoreType.DMA((SUM_COPIES,)),
            pltpu.SemaphoreType.DMA((2 * parts + 1,)),
        ],
        compiler_params=params(collective, LIMIT),
        cost_estimate=pl.CostEstimate(
            flops=2 * TEAM * rows * units * width * (parts + 1),
            bytes_accessed=2 * TEAM * rows * (units * parts + width),
            transcendentals=0,
        ),
    )(two, *grads, *weights)


def gather_down_kernel(parts, x, cot, *refs):
    acts, refs = refs[:parts], refs[parts:]
    o_ref, down_out, refs = refs[0], refs[1], refs[2:]
    acts_here, (cot_here, send, receive, own) = refs[:parts], refs[parts:]
    me = lax.axis_index("fsdp")
    loader = Loader(own)
    loader(x, o_ref.at[lax.rem(me, TEAM)])
    loader(cot, cot_here)
    for source, target in zip(acts, acts_here):
        loader(source, target)
    greet(me, (1, 2, 4))
    sender = Sender(send, receive)
    moves = Gather(sender, x, o_ref, me)
    units = acts_here[0].shape[2]

    def work(k):
        turned_product(
            acts_here[k // 2], cot_here, rows_of(down_out, k // 2, units), k % 2, 2
        )

    moves.start()
    loader.wait()
    work(0)
    moves.forward()
    work(1)
    moves.across()
    if parts > 1:
        work(2)
    moves.diagonal()
    if parts > 1:
        work(3)
    moves.arrive()
    sender.finish()


def gather_down(x, cot, acts, collective):
    rows, width = x.shape
    parts, units = len(acts), acts[0].shape[2]
    anywhere = pl.BlockSpec(memory_space=pl.ANY)
    vmem = pl.BlockSpec(memory_space=pltpu.VMEM)
    like = jax.ShapeDtypeStruct
    return pl.pallas_call(
        functools.partial(gather_down_kernel, parts),
        out_shape=(like((TEAM, rows, width), x.dtype), like((parts * units, width), bf16)),
        in_specs=[vmem, anywhere] + [anywhere] * parts,
        out_specs=(anywhere, vmem),
        scratch_shapes=[
            *(pltpu.VMEM(a.shape, bf16) for a in acts),
            pltpu.VMEM(cot.shape, bf16),
            pltpu.SemaphoreType.DMA((14,)),
            pltpu.SemaphoreType.DMA((14,)),
            pltpu.SemaphoreType.DMA((2 + parts,)),
        ],
        compiler_params=params(collective, LIMIT),
        cost_estimate=pl.CostEstimate(
            flops=2 * TEAM * rows * width * units * parts,
            bytes_accessed=6 * TEAM * rows * width,
            transcendentals=0,
        ),
    )(x, cot, *acts)


def last_sums_kernel(planes, parts, grad_qkv, qkv_weight, down, *refs):
    acts, units, refs = refs[:parts], refs[parts : 2 * parts], refs[2 * parts :]
    grad_normed, layer, gate, up, refs = *refs[:4], refs[4:]
    first, second, refs = refs[:4], refs[4:8], refs[8:]
    acts_here, downs_here, refs = refs[:parts], refs[parts : 2 * parts], refs[2 * parts :]
    grad_here, weight_here, landed, send, receive, own = refs
    me = lax.axis_index("fsdp")
    place = lax.rem(me, TEAM)
    loader = Loader(own)
    loader(grad_qkv, grad_here)
    loader(qkv_weight, weight_here)
    for k in range(parts):
        loader(units[k].at[place], landed.at[k, place])
        loader(acts[k], acts_here[k])
        loader(rows_of(down, k, downs_here[k].shape[0]), downs_here[k])
    greet(me, range(1, TEAM))
    sender = Sender(send, receive)
    moves = [
        sender(units[k].at[flipped(place, m)], landed.at[k, place], flipped(me, m))
        for k in range(parts)
        for m in SWAP_ORDER
    ]
    loader.wait()
    one = TeamSum(sender, me, grad_normed, first, [grad_here], [weight_here], True)
    two = TeamSum(sender, me, layer, second, acts_here, downs_here, False)
    one.start()
    one.own()
    two.start()
    one.relay()
    two.own()
    two.relay()
    for copy in moves:
        copy.wait_recv()
    block = gate.shape[1] // (planes * TEAM)
    some = planes // parts
    span = TEAM * block
    for j, ref in enumerate((gate, up)):
        for g in range(planes):
            at = (j * some + g % some) * block
            ref[:, g * span : (g + 1) * span] = jnp.concatenate(
                [landed[g // some, q, :, at : at + block] for q in range(TEAM)], axis=1
            )
    one.finish()
    two.finish()
    sender.finish()


def last_sums(grad_qkv, qkv_weight, acts, down, units, planes, collective):
    _, rows, depth = grad_qkv.shape
    width = qkv_weight.shape[0]
    parts = len(acts)
    anywhere = pl.BlockSpec(memory_space=pl.ANY)
    vmem = pl.BlockSpec(memory_space=pltpu.VMEM)
    like = jax.ShapeDtypeStruct
    _, own_rows, some = units[0].shape
    links = 2 * SUM_COPIES + (TEAM - 1) * parts
    home = like((own_rows, TEAM * parts * some // 2), bf16)
    return pl.pallas_call(
        functools.partial(last_sums_kernel, planes, parts),
        out_shape=(like((rows, width), f32),) * 2 + (home,) * 2,
        in_specs=[anywhere] * (3 + 2 * parts),
        out_specs=(vmem,) * 4,
        scratch_shapes=[
            *sum_buffers(rows, width),
            *sum_buffers(rows, width),
            *(pltpu.VMEM(a.shape, bf16) for a in acts),
            *(pltpu.VMEM((a.shape[2], width), bf16) for a in acts),
            pltpu.VMEM(grad_qkv.shape, bf16),
            pltpu.VMEM(qkv_weight.shape, bf16),
            pltpu.VMEM((parts, *units[0].shape), bf16),
            pltpu.SemaphoreType.DMA((links,)),
            pltpu.SemaphoreType.DMA((links,)),
            pltpu.SemaphoreType.DMA((2 + 3 * parts,)),
        ],
        compiler_params=params(collective, LIMIT),
        cost_estimate=pl.CostEstimate(
            flops=2 * TEAM * rows * width * (depth + sum(a.shape[2] for a in acts)),
            bytes_accessed=4 * TEAM * rows * depth,
            transcendentals=0,
        ),
    )(grad_qkv, qkv_weight, down, *acts, *units)


class Line:
    def __init__(self, sender, ref, planes, me):
        self.sender, self.ref, self.planes = sender, ref, planes
        self.plane, self.place = lax.div(me, TEAM), lax.rem(me, TEAM)
        self.flows = [(sign, [sender.take() for _ in range(planes - 1)]) for sign in (1, -1)]

    def passing(self, step, sign, ks, source):
        block = jnp.clip(source, 0, self.planes - 1)
        beyond = jnp.clip(self.plane + sign, 0, self.planes - 1) * TEAM + self.place
        ref, k = self.ref.at[block], ks[step]
        return remote(ref, ref, self.sender.send.at[k], self.sender.receive.at[k], beyond)

    def goes(self, step, sign):
        source, onward = self.plane - sign * step, self.plane + sign
        last = self.planes - 1
        return (source >= 0) & (source <= last) & (onward >= 0) & (onward <= last)

    def start(self, step):
        for sign, ks in self.flows:
            going = self.passing(step, sign, ks, self.plane - sign * step)
            pl.when(self.goes(step, sign))(going.start)

    def arrive(self, step):
        for sign, ks in self.flows:
            source = self.plane - sign * (step + 1)
            coming = self.passing(step, sign, ks, source)
            pl.when((source >= 0) & (source <= self.planes - 1))(coming.wait_recv)

    def sent(self, step):
        for sign, ks in self.flows:
            going = self.passing(step, sign, ks, self.plane - sign * step)
            pl.when(self.goes(step, sign))(going.wait_send)


SWAP_ORDER = (6, 7, 2, 3, 4, 5, 1)


def open_kernel(
    planes, parts, query_in, key_in, value_in, output_in, tokens_in, gate_in, up_in, *refs
):
    smalls, refs = refs[:5], refs[5:]
    gate_up, refs = refs[:parts], refs[parts:]
    qkv, output_raw, output, tokens, *gain_refs, numbers = refs[:9]
    small_in, small, sorted_units, send, receive, own = refs[9:]
    slots, sequence = smalls[4].shape
    small_in[...] = jnp.zeros_like(small_in)
    for k, ref in enumerate(smalls):
        small_in[k : k + ref.shape[0], : ref.shape[1]] = ref[...].astype(f32)
    me = lax.axis_index("fsdp")
    place = lax.rem(me, TEAM)
    plane = lax.div(me, TEAM)
    team = me - place
    others = [lax.rem(me + TEAM * k, planes * TEAM) for k in range(1, planes)]
    sender = Sender(send, receive)
    keeps = []

    def keep(source, target):
        copy = pltpu.make_async_copy(source, target, own.at[len(keeps)])
        copy.start()
        keeps.append(copy)

    qkv_parts, at = [], 0
    for ref in (query_in, key_in, value_in):
        part = ref.shape[1] // TEAM
        qkv_parts.append((ref, part, qkv.at[plane, place, :, pl.ds(at, part)]))
        at += part

    def columns(ref, part, target):
        return ref.at[:, pl.ds(pl.multiple_of(target * part, part), part)]

    for ref, part, target in qkv_parts:
        keep(columns(ref, part, place), target)
    keep(small_in, small.at[me])
    keep(tokens_in, tokens.at[place])
    keep(output_in, output_raw.at[plane])
    greet(me, range(1, TEAM), others)

    qkv_line = Line(sender, qkv, planes, me)
    out_line = Line(sender, output_raw, planes, me)
    rows_tokens = Gather(sender, tokens_in, tokens, me)
    spread_send = [sender.take() for _ in range(planes)]
    spread_own = len(keeps)

    def outgoing(k):
        number = TEAM * k + place
        partner, there = lax.div(number, planes), lax.rem(number, planes)
        s, r = send.at[spread_send[0] + k], receive.at[spread_send[0] + there]
        over = remote(output_raw.at[k], output.at[there], s, r, team + partner)
        here = pltpu.make_async_copy(output_raw.at[k], output.at[there], own.at[spread_own + k])
        return partner, over, here

    def incoming(k):
        partner = lax.rem(planes * place + k, TEAM)
        s, r = send.at[spread_send[k]], receive.at[spread_send[k]]
        return partner, remote(output_raw.at[k], output.at[k], s, r, team + partner)

    def spread_one(k, inside):
        partner, over, here = outgoing(jnp.clip(k, 0, planes - 1))
        pl.when(inside & (partner != place))(over.start)
        pl.when(inside & (partner == place))(here.start)

    def step_out(step):
        out_line.arrive(step)
        if step < planes - 2:
            out_line.start(step + 1)
        spread_one(plane - step - 1, plane - step - 1 >= 0)
        spread_one(plane + step + 1, plane + step + 1 <= planes - 1)

    swaps = [
        sender(columns(ref, part, flipped(place, m)), target, flipped(me, m))
        for m in SWAP_ORDER
        for ref, part, target in qkv_parts
    ]
    near = [sender(small_in, small.at[me], flipped(me, m)) for m in SWAP_ORDER]
    keeps[-1].wait()
    out_line.start(0)
    block = gate_in.shape[1] // (planes * TEAM)
    some = planes // parts
    units = some * block
    for k in range(parts):
        for q in range(TEAM):
            for j, ref in enumerate((gate_in, up_in)):
                starts = [(TEAM * g + q) * block for g in range(k * some, (k + 1) * some)]
                sorted_units[k, q, :, j * units : (j + 1) * units] = jnp.concatenate(
                    [ref[:, at : at + block] for at in starts], axis=1
                )
    for copy in swaps:
        copy.wait_recv()
    for copy in keeps[:3]:
        copy.wait()
    qkv_line.start(0)
    rows_tokens.start()
    moves = [
        sender(sorted_units.at[k, flipped(place, m)], gate_up[k].at[place], flipped(me, m))
        for k in range(parts)
        for m in SWAP_ORDER
    ]
    kept_units = [
        pltpu.make_async_copy(
            sorted_units.at[k, place], gate_up[k].at[place], own.at[spread_own + planes + k]
        )
        for k in range(parts)
    ]
    for copy in kept_units:
        copy.start()
    spread_one(plane, True)
    rows_tokens.forward()
    step_out(0)
    for copy in near:
        copy.wait_recv()
    keeps[3].wait()
    shared = small.at[pl.ds(team, TEAM)]
    far = [sender(shared, shared, other) for other in others]
    rows_tokens.across()
    for step in range(planes - 1):
        qkv_line.arrive(step)
        if step < planes - 2:
            qkv_line.start(step + 1)
            step_out(step + 1)
        if step == 0:
            rows_tokens.diagonal()
        if step == 1:
            for copy in far:
                copy.wait_recv()
            for k, ref in enumerate(gain_refs):
                part = smalls[k].shape[1]
                ref[...] = jnp.concatenate(
                    [small[i, k : k + 1, :part] for i in range(planes * TEAM)], axis=1
                )
            per_step = STEP // sequence
            for i in range(numbers.shape[0]):
                pieces = []
                for m in range(i * per_step, (i + 1) * per_step):
                    row = 4 + m % slots
                    pieces.append(small[team + m // slots, row : row + 1, :sequence] + 64.0 * m)
                numbers[i] = jnp.concatenate(pieces, axis=1)
    rows_tokens.arrive()
    for copy in moves:
        copy.wait_recv()
    for copy in kept_units:
        copy.wait()
    for k in range(planes):
        partner, over, here = outgoing(k)
        pl.when(partner != place)(over.wait_send)
        pl.when(partner == place)(here.wait)
        partner, arriving = incoming(k)
        pl.when(partner != place)(arriving.wait_recv)
    for step in range(planes - 1):
        qkv_line.sent(step)
        out_line.sent(step)
    sender.finish()
    for copy in keeps[4:-1]:
        copy.wait()


def opening(query, key, value, output, tokens, gate, up, smalls, planes, parts, collective):
    links = 28 + 4 * (planes - 1) + 14 + planes - 1 + planes + parts * (TEAM - 1)
    anywhere = pl.BlockSpec(memory_space=pl.ANY)
    vmem = pl.BlockSpec(memory_space=pltpu.VMEM)
    like = jax.ShapeDtypeStruct
    rows = query.shape[0]
    width = (query.shape[1] + key.shape[1] + value.shape[1]) // TEAM
    units = (TEAM, rows, 2 * gate.shape[1] // TEAM // parts)
    devices = planes * TEAM
    return pl.pallas_call(
        functools.partial(open_kernel, planes, parts),
        out_shape=(
            *((like(units, bf16),) * parts),
            like((planes, TEAM, rows, width), bf16),
            like((planes, *output.shape), bf16),
            like((planes, *output.shape), bf16),
            like((TEAM, *tokens.shape), bf16),
            *(like((1, devices * x.shape[1]), f32) for x in smalls[:4]),
            like((TEAM * tokens.shape[0] // STEP, 1, STEP), f32),
        ),
        in_specs=[vmem] * 12,
        out_specs=(anywhere,) * (4 + parts) + (vmem,) * 5,
        scratch_shapes=[
            pltpu.VMEM((8, 128), f32),
            pltpu.VMEM((devices, 8, 128), f32),
            pltpu.VMEM((parts, *units), bf16),
            pltpu.SemaphoreType.DMA((links,)),
            pltpu.SemaphoreType.DMA((links,)),
            pltpu.SemaphoreType.DMA((6 + planes + parts,)),
        ],
        compiler_params=params(collective, LIMIT),
    )(query, key, value, output, tokens, gate, up, *smalls)


def close_kernel(planes, x_ref, gains, *refs):
    query_ref, key_ref, value_ref, output_ref, gain_ref, *refs = refs
    landed, mine, near_in, mid, far_in, send, receive, own = refs
    me = lax.axis_index("fsdp")
    place = lax.rem(me, TEAM)
    plane = lax.div(me, TEAM)
    others = [lax.rem(me + TEAM * k, planes * TEAM) for k in range(1, planes)]
    rows = landed.shape[1]

    def part(target):
        return x_ref.at[pl.ds(pl.multiple_of(target * rows, rows), rows)]

    keep = pltpu.make_async_copy(part(place), landed.at[place], own.at[0])
    keep.start()
    keep_mine = pltpu.make_async_copy(
        x_ref.at[pl.ds(TEAM * rows, mine.shape[0])], mine, own.at[1]
    )
    keep_mine.start()
    greet(me, range(1, TEAM), others)
    sender = Sender(send, receive)
    near = [
        sender(gains.at[flipped(place, m)], near_in.at[m - 1], flipped(me, m)) for m in SWAP_ORDER
    ]
    moves = [
        sender(part(flipped(place, m)), landed.at[place], flipped(me, m)) for m in SWAP_ORDER
    ]
    for copy in near:
        copy.wait_recv()
    summed = gains[place]
    for mask in range(1, TEAM):
        summed = summed + near_in[mask - 1]
    mid[...] = summed
    far = [
        sender(mid.at[lax.rem(plane + k + 1, planes)], far_in.at[k], other)
        for k, other in enumerate(others)
    ]
    keep_mine.wait()
    width = mine.shape[1]
    for c in range(output_ref.shape[1] // width):
        output_ref[:, c * width : (c + 1) * width] = mine[c * rows : (c + 1) * rows]
    for copy in moves:
        copy.wait_recv()
    keep.wait()
    at = 0
    for ref in (query_ref, key_ref, value_ref):
        part_width = ref.shape[1] // TEAM
        for q in range(TEAM):
            ref[:, q * part_width : (q + 1) * part_width] = landed[q, :, at : at + part_width]
        at += part_width
    for copy in far:
        copy.wait_recv()
    result = mid[plane]
    for k in range(planes - 1):
        result = result + far_in[k]
    gain_ref[...] = result
    sender.finish()


def closing(x, gains, rows, widths, planes, collective):
    links = 2 * (TEAM - 1) + planes - 1
    block = gains.shape[2:]
    vmem = pl.BlockSpec(memory_space=pltpu.VMEM)
    like = jax.ShapeDtypeStruct
    return pl.pallas_call(
        functools.partial(close_kernel, planes),
        out_shape=(*(like((rows, w), bf16) for w in widths), like(block, f32)),
        in_specs=[pl.BlockSpec(memory_space=pl.ANY), vmem],
        out_specs=(vmem,) * 5,
        scratch_shapes=[
            pltpu.VMEM((TEAM, rows, x.shape[1]), x.dtype),
            pltpu.VMEM((x.shape[0] - TEAM * rows, x.shape[1]), x.dtype),
            pltpu.VMEM((TEAM - 1, planes, *block), f32),
            pltpu.VMEM((planes, *block), f32),
            pltpu.VMEM((planes - 1, *block), f32),
            pltpu.SemaphoreType.DMA((links,)),
            pltpu.SemaphoreType.DMA((links,)),
            pltpu.SemaphoreType.DMA((2,)),
        ],
        compiler_params=params(collective, LIMIT),
    )(x, gains)


def visible_and_tables(ids_row, table):
    rows = ids_row.shape[1]
    row_at = lax.broadcasted_iota(jnp.int32, (rows, rows), 0)
    column_at = lax.broadcasted_iota(jnp.int32, (rows, rows), 1)
    ids_column = jnp.sum(jnp.where(row_at == column_at, ids_row, 0.0), axis=1, keepdims=True)
    visible = (ids_column == ids_row) & (column_at <= row_at)
    sequence = table.shape[0]
    place = jnp.sum(visible.astype(f32), axis=1, keepdims=True) - 1.0
    at = lax.broadcasted_iota(jnp.int32, (rows, sequence), 1).astype(f32)
    chosen = (at == place).astype(bf16)
    both = simple_product(chosen, table)
    width = 2 * HEAD_SIZE
    both = (both[:, :width] + both[:, width : 2 * width]) + both[:, 2 * width :]
    return visible, both[:, :HEAD_SIZE], both[:, HEAD_SIZE:]


def softmax(query, key, visible):
    scores = dot_last(query, key) * HEAD_SIZE ** (-0.5)
    scores = jnp.where(visible, scores, -1e30)
    expos = jnp.exp(scores - jnp.max(scores, axis=1, keepdims=True))
    return expos / jnp.sum(expos, axis=1, keepdims=True)


def attend_kernel(
    x_ref, gain, weight, ids_row, table, query_gain, key_gain,
    normed_ref, raw_ref, turned_ref, value_ref, context_ref,
):
    x = x_ref[...].astype(f32)
    scale = lax.rsqrt(jnp.mean(x * x, axis=1, keepdims=True) + epsilon)
    normed = (x * scale * gain[...]).astype(bf16)
    normed_ref[...] = normed
    projected = simple_product(normed, weight[...])
    visible, cosine, sine = visible_and_tables(ids_row[0], table[...])
    heads = context_ref.shape[1] // HEAD_SIZE
    raw_ref[...] = projected[:, : (heads + 1) * HEAD_SIZE]
    value = projected[:, (heads + 1) * HEAD_SIZE :].astype(bf16)
    value_ref[...] = value
    turned = []
    for h in range(heads + 1):
        raw = projected[:, h * HEAD_SIZE : (h + 1) * HEAD_SIZE]
        head_gain = query_gain if h < heads else key_gain
        y = raw * lax.rsqrt(jnp.mean(raw * raw, axis=1, keepdims=True) + epsilon) * head_gain[...]
        y = y * cosine + pltpu.roll(y, HEAD_SIZE // 2, 1) * sine
        turned.append(y.astype(bf16))
        turned_ref[:, h * HEAD_SIZE : (h + 1) * HEAD_SIZE] = turned[-1]
    for h in range(heads):
        probs = softmax(turned[h], turned[heads], visible).astype(bf16)
        context = simple_product(probs, value)
        context_ref[:, h * HEAD_SIZE : (h + 1) * HEAD_SIZE] = context.astype(bf16)


def by_step(*shape):
    return pl.BlockSpec(shape, lambda i: (i, *(0 for _ in shape[1:])))


def fixed(*shape):
    return pl.BlockSpec(shape, lambda i: tuple(0 for _ in shape))


def attend(x, gain, weight, ids, table, query_gain, key_gain):
    rows, width = x.shape
    out = weight.shape[1]
    like = jax.ShapeDtypeStruct
    heads = out - 2 * HEAD_SIZE
    return pl.pallas_call(
        attend_kernel,
        grid=(rows // STEP,),
        out_shape=(
            like((rows, width), bf16),
            like((rows, heads + HEAD_SIZE), f32),
            like((rows, heads + HEAD_SIZE), bf16),
            like((rows, HEAD_SIZE), bf16),
            like((rows, heads), bf16),
        ),
        in_specs=[
            by_step(STEP, width),
            fixed(1, width),
            fixed(width, out),
            by_step(1, 1, STEP),
            fixed(*table.shape),
            fixed(1, HEAD_SIZE),
            fixed(1, HEAD_SIZE),
        ],
        out_specs=(
            by_step(STEP, width),
            by_step(STEP, heads + HEAD_SIZE),
            by_step(STEP, heads + HEAD_SIZE),
            by_step(STEP, HEAD_SIZE),
            by_step(STEP, heads),
        ),
        compiler_params=pltpu.CompilerParams(vmem_limit_bytes=LIMIT),
        cost_estimate=pl.CostEstimate(
            flops=2 * rows * width * out, bytes_accessed=8 * rows * width, transcendentals=0
        ),
    )(x, gain, weight, ids, table, query_gain, key_gain)


def attend_back_kernel(planes, grad_in, out_weight, context, raw_in, turned_in, value_in, normed_in,
    ids_row, table, query_gain, key_gain, grad_raw_ref, merged, grad_gains_ref,
    grad_ref, raw_ref, turned_ref, value_ref, normed_ref, out_sum, weight_sum, send, receive, own,
):
    me = lax.axis_index("fsdp")
    place = lax.rem(me, TEAM)
    team = me - place
    loader = Loader(own)
    loader(grad_in, grad_ref)
    for source, target in (
        (raw_in, raw_ref), (turned_in, turned_ref), (value_in, value_ref), (normed_in, normed_ref)
    ):
        loader(source, target)
    greet(me, range(1, TEAM))
    loader.copies[0].wait()

    total, width = grad_ref.shape
    heads = context.shape[1] // HEAD_SIZE
    out = weight_sum.shape[1]
    rows, block = weight_sum.shape[0] // planes, out_sum.shape[0] // planes
    cuts = width // out

    def source(k, c):
        return out_sum.at[pl.ds(k * block, block), pl.ds(c * out, out)]

    def target(k, c):
        return merged.at[k, pl.ds(rows + c * block, block)]

    def outgoing(k, c):
        number = planes * place + k
        partner, there = lax.rem(number, TEAM), lax.div(number, TEAM)
        s, r = send.at[k * cuts + c], receive.at[there * cuts + c]
        over = remote(source(k, c), target(there, c), s, r, team + partner)
        here = pltpu.make_async_copy(source(k, c), target(there, c), own.at[5 + k * cuts + c])
        return partner, over, here

    def incoming(k, c):
        partner = lax.div(TEAM * k + place, planes)
        s, r = send.at[k * cuts + c], receive.at[k * cuts + c]
        return partner, remote(source(k, c), target(k, c), s, r, team + partner)

    for c in range(cuts):
        at = slice(c * out, (c + 1) * out)
        out_sum[:, at] = dot_first(context[...], grad_ref[:, at]).astype(bf16)
        for k in range(planes):
            partner, over, here = outgoing(k, c)
            pl.when(partner != place)(over.start)
            pl.when(partner == place)(here.start)

    grad_gains_ref[...] = jnp.zeros_like(grad_gains_ref)
    for copy in loader.copies[1:]:
        copy.wait()

    @pl.loop(0, total // STEP)
    def _(i):
        here = pl.ds(pl.multiple_of(i * STEP, STEP), STEP)
        grad_context = dot_last(grad_ref[here, :], out_weight[...]).astype(bf16)
        visible, cosine, sine = visible_and_tables(ids_row[i], table[...])
        value = value_ref[here, :]
        key = turned_ref[here, heads * HEAD_SIZE :]
        grads = []
        grad_value = 0.0
        grad_key = 0.0
        for h in range(heads):
            at = slice(h * HEAD_SIZE, (h + 1) * HEAD_SIZE)
            query = turned_ref[here, at]
            probs = softmax(query, key, visible)
            grad_value = grad_value + dot_first(probs.astype(bf16), grad_context[:, at])
            grad_probs = dot_last(grad_context[:, at], value)
            inner = jnp.sum(probs * grad_probs, axis=1, keepdims=True)
            grad_scores = (probs * (grad_probs - inner)).astype(bf16)
            grads.append(simple_product(grad_scores, key) * HEAD_SIZE ** (-0.5))
            grad_key = grad_key + dot_first(grad_scores, query) * HEAD_SIZE ** (-0.5)
        grads.append(grad_key)
        parts = []
        for h in range(heads + 1):
            raw = raw_ref[here, h * HEAD_SIZE : (h + 1) * HEAD_SIZE]
            head_gain = query_gain[...] if h < heads else key_gain[...]
            scale = lax.rsqrt(jnp.mean(raw * raw, axis=1, keepdims=True) + epsilon)
            turned = grads[h] * cosine + pltpu.roll(grads[h] * sine, HEAD_SIZE // 2, 1)
            row = 0 if h < heads else 1
            grad_gains_ref[row : row + 1, :] += jnp.sum(turned * raw * scale, axis=0, keepdims=True)
            turned = turned * head_gain
            mean = jnp.mean(turned * raw, axis=1, keepdims=True)
            parts.append((turned * scale - raw * (scale * scale * scale * mean)).astype(bf16))
        parts.append(grad_value.astype(bf16))
        grad_raw_ref[here, :] = jnp.concatenate(parts, axis=1)

    @pl.loop(0, planes)
    def _(g):
        at = pl.ds(pl.multiple_of(g * rows, rows), rows)
        weight_sum[at, :] = dot_first(normed_ref[:, at], grad_raw_ref[...]).astype(bf16)

    homes = []
    for g in range(planes):
        copy = pltpu.make_async_copy(
            weight_sum.at[pl.ds(g * rows, rows)],
            merged.at[g, pl.ds(0, rows)],
            own.at[5 + planes * cuts + g],
        )
        copy.start()
        homes.append(copy)
    for k in range(planes):
        for c in range(cuts):
            partner, over, here = outgoing(k, c)
            pl.when(partner != place)(over.wait_send)
            pl.when(partner == place)(here.wait)
            partner, arriving = incoming(k, c)
            pl.when(partner != place)(arriving.wait_recv)
    for copy in homes:
        copy.wait()


def attend_back(
    grad, out_weight, context, raw, turned, value, normed, ids, table, query_gain, key_gain,
    planes, collective,
):
    rows, width = grad.shape
    heads = context.shape[1]
    out = heads + 2 * HEAD_SIZE
    merged = (planes, (width + heads * width // out) // planes, out)
    copies = planes * (width // out)
    anywhere = pl.BlockSpec(memory_space=pl.ANY)
    vmem = pl.BlockSpec(memory_space=pltpu.VMEM)
    like = jax.ShapeDtypeStruct
    return pl.pallas_call(
        functools.partial(attend_back_kernel, planes),
        out_shape=(like((rows, out), bf16), like(merged, bf16), like((8, HEAD_SIZE), f32)),
        in_specs=[anywhere, vmem, vmem] + [anywhere] * 4 + [vmem] * 4,
        out_specs=(vmem, anywhere, vmem),
        scratch_shapes=[
            *(pltpu.VMEM(x.shape, x.dtype) for x in (grad, raw, turned, value, normed)),
            pltpu.VMEM((heads, width), bf16),
            pltpu.VMEM((width, out), bf16),
            pltpu.SemaphoreType.DMA((copies,)),
            pltpu.SemaphoreType.DMA((copies,)),
            pltpu.SemaphoreType.DMA((5 + copies + planes,)),
        ],
        compiler_params=params(collective, LIMIT),
        cost_estimate=pl.CostEstimate(
            flops=2 * rows * width * (out + 2 * heads),
            bytes_accessed=8 * rows * width,
            transcendentals=0,
        ),
    )(grad, out_weight, context, raw, turned, value, normed, ids, table, query_gain, key_gain)


def hidden(two, weight):
    return simple_product(two, weight)


def hidden_grads(both, cot, down):
    units = both.shape[1] // 2
    gate, up = both[:, :units], both[:, units:]
    grad_act = dot_last(cot, down)
    sigma = 1.0 / (1.0 + jnp.exp(-gate))
    silu_gate = gate * sigma
    act = (silu_gate * up).astype(bf16)
    grad_gate = (grad_act * up * (sigma * (1.0 + gate * (1.0 - sigma)))).astype(bf16)
    grad_up = (grad_act * silu_gate).astype(bf16)
    return act, grad_gate, grad_up


def feed_kernel(
    two_in, cot_in, weight_in, down_in, two_out, cot_out, act, grad_both, grad_weight,
    two, cot, weight, down, both, weight_sum, send, receive, own,
):
    me = lax.axis_index("fsdp")
    place = lax.rem(me, TEAM)
    loader = Loader(own)
    loader(two_in, two.at[place])
    loader(cot_in, cot.at[place])
    loader(weight_in, weight)
    loader(rows_of(down_in, 0, down.shape[0]), down)
    greet(me, (1, 2, 4))
    sender = Sender(send, receive)
    rows_two = Gather(sender, two_in, two, me)
    rows_cot = Gather(sender, cot_in, cot, me)
    rows_two.start()
    rows_cot.start()
    rows, units = act.shape[1:]
    width = two.shape[2]
    weight_sum[...] = jnp.zeros_like(weight_sum)

    crossed = {0: (0, 1), 2: (2, 4), 4: (3, 5), 6: (6, 7)}

    def chip_rows(moves, mask, target):
        for k in crossed[mask]:
            moves.late[k].wait_recv()
        chip = pl.ds(2 * lax.div(flipped(place, mask), 2), 2)
        loader(moves.o.at[chip], target.at[chip])
        return chip, moves.o[chip].reshape(2 * rows, width)

    def forward(mask):
        _, flat = chip_rows(rows_two, mask, two_out)
        both[mask // 2] = simple_product(flat, weight[...])

    def backward(mask):
        chip, flat = chip_rows(rows_cot, mask, cot_out)
        a, grad_gate, grad_up = hidden_grads(both[mask // 2], flat, down[...])
        act[chip] = a.reshape(2, rows, units)
        grads = jnp.concatenate([grad_gate, grad_up], axis=1)
        grad_both[chip] = grads.reshape(2, rows, 2 * units)
        for t in range(width // TILE):
            at = slice(t * TILE, (t + 1) * TILE)
            left = two[chip, :, at].reshape(2 * rows, TILE)
            weight_sum[at, :] += dot_first(left, grads)

    rows_two.forward()
    rows_two.across()
    loader.wait()
    forward(0)
    backward(0)
    rows_cot.forward()
    forward(2)
    forward(4)
    rows_cot.across()
    backward(2)
    rows_two.diagonal()
    backward(4)
    forward(6)
    rows_cot.diagonal()
    backward(6)
    grad_weight[...] = weight_sum[...].astype(bf16)
    sender.finish()
    for copy in loader.copies[4:]:
        copy.wait()


def feed(two, cot, weight, down, collective):
    rows, width = two.shape
    units = weight.shape[1] // 2
    vmem = pl.BlockSpec(memory_space=pltpu.VMEM)
    anywhere = pl.BlockSpec(memory_space=pl.ANY)
    like = jax.ShapeDtypeStruct
    return pl.pallas_call(
        feed_kernel,
        out_shape=(
            like((TEAM, rows, width), bf16),
            like((TEAM, rows, width), bf16),
            like((TEAM, rows, units), bf16),
            like((TEAM, rows, 2 * units), bf16),
            like(weight.shape, bf16),
        ),
        in_specs=[anywhere] * 4,
        out_specs=(anywhere, anywhere, vmem, vmem, vmem),
        scratch_shapes=[
            pltpu.VMEM((TEAM, rows, width), bf16),
            pltpu.VMEM((TEAM, rows, width), bf16),
            pltpu.VMEM(weight.shape, bf16),
            pltpu.VMEM((units, width), bf16),
            pltpu.VMEM((TEAM // 2, 2 * rows, 2 * units), f32),
            pltpu.VMEM(weight.shape, f32),
            pltpu.SemaphoreType.DMA((28,)),
            pltpu.SemaphoreType.DMA((28,)),
            pltpu.SemaphoreType.DMA((12,)),
        ],
        compiler_params=params(collective, LIMIT),
        cost_estimate=pl.CostEstimate(
            flops=10 * TEAM * rows * width * units,
            bytes_accessed=8 * TEAM * rows * width,
            transcendentals=0,
        ),
    )(two, cot, weight, down)


def feed_rest_kernel(two, cot, weight, down, act, grad_both):
    blocks, rows, units = act.shape
    both = simple_product(two[...].reshape(blocks * rows, -1), weight[...])
    flat = cot[...].reshape(blocks * rows, -1)
    a, grad_gate, grad_up = hidden_grads(both, flat, down[...])
    act[...] = a.reshape(blocks, rows, units)
    grad_both[:, :, :units] = grad_gate.reshape(blocks, rows, units)
    grad_both[:, :, units:] = grad_up.reshape(blocks, rows, units)


def feed_rest(two, cot, weight, down, part):
    _, rows, width = two.shape
    units = weight.shape[1] // 2
    like = jax.ShapeDtypeStruct
    return pl.pallas_call(
        feed_rest_kernel,
        grid=(TEAM // 2,),
        out_shape=(like((TEAM, rows, units), bf16), like((TEAM, rows, 2 * units), bf16)),
        in_specs=[
            by_step(2, rows, width),
            by_step(2, rows, width),
            fixed(*weight.shape),
            pl.BlockSpec((units, width), lambda i: (part, 0)),
        ],
        out_specs=(by_step(2, rows, units), by_step(2, rows, 2 * units)),
        compiler_params=pltpu.CompilerParams(vmem_limit_bytes=LIMIT),
        cost_estimate=pl.CostEstimate(
            flops=6 * TEAM * rows * width * units,
            bytes_accessed=4 * TEAM * rows * width,
            transcendentals=0,
        ),
    )(two, cot, weight, down)


def local(
    devices,
    tokens,
    segments,
    micro_live,
    cotangent,
    w_query,
    key_weight,
    value_weight,
    w_output,
    attn_gain,
    query_norm_gain,
    key_gain,
    w_gate,
    w_up,
    w_down,
    mlp_gain,
):
    planes = devices // TEAM
    lines = [[place + TEAM * k for k in range(planes)] for place in range(TEAM)]
    slots, sequence = segments.shape
    token_count, width = tokens.shape
    groups = QUERY_HEADS // KEY_VALUE_HEADS
    rows = w_query.shape[0]
    parts = 2 if planes % 2 == 0 else 1
    team_rows = TEAM * token_count
    head_width = groups * HEAD_SIZE
    me = lax.axis_index("fsdp")
    plane = me // TEAM

    def gather_line(x):
        return lax.all_gather(x, "fsdp", axis=0, tiled=True, axis_index_groups=lines)

    def sum_line(x):
        return lax.psum_scatter(
            x, "fsdp", scatter_dimension=0, tiled=True, axis_index_groups=lines
        )

    slot_live = (lax.broadcasted_iota(jnp.int32, (slots, 1), 0) < micro_live[0]).astype(f32)
    row_live = jnp.broadcast_to(slot_live, (slots, sequence)).reshape(token_count, 1)
    cot_b = cotangent * row_live.astype(bf16)

    down_weight = gather_line(w_down)
    smalls = [x[None] for x in (attn_gain, mlp_gain, query_norm_gain, key_gain)] + [segments]
    opened = opening(
        w_query,
        key_weight,
        value_weight,
        w_output,
        tokens,
        w_gate,
        w_up,
        smalls,
        planes,
        parts,
        1,
    )
    unit_slices, opened = opened[:parts], opened[parts:]
    qkv_weight, _, output_weight, team_tokens = opened[:4]
    norm_gain, mlp_norm_gain, qgain, kgain, ids = opened[4:]
    mlp_norm_gain = mlp_norm_gain.reshape(width)
    qkv_weight = qkv_weight.reshape(width, -1)
    output_weight = output_weight.reshape(head_width, width)
    unit_weights = [gather_line(x.reshape(TEAM * rows, -1)) for x in unit_slices]
    table = jnp.asarray(rotation_tables(sequence))

    inputs = tokens.astype(f32)
    team_normed, raw, turned, value_b, context_b = attend(
        team_tokens.reshape(team_rows, width), norm_gain, qkv_weight, ids, table, qgain, kgain
    )
    middle = inputs + team_sum(
        context_b.reshape(TEAM, token_count, head_width), output_weight, 2
    )

    normed_two = root_mean_square_norm(middle, mlp_norm_gain).astype(bf16)
    team_two, team_cot, act, grad_both, first_units = feed(
        normed_two, cot_b, unit_weights[0], down_weight, 0
    )
    acts, grads_both, grad_units = [act], [grad_both], [first_units]
    for k in range(1, parts):
        act, grad_both = feed_rest(team_two, team_cot, unit_weights[k], down_weight, k)
        acts.append(act)
        grads_both.append(grad_both)
    grad_normed_two, last_units = feed_back(team_two, grads_both, unit_weights, 4)
    grad_units = [sum_line(g) for g in (*grad_units, last_units)[:parts]]
    _, pull_two = jax.vjp(root_mean_square_norm, middle, mlp_norm_gain)
    middle_part, grad_mgain = pull_two(grad_normed_two)
    grad_middle = cot_b.astype(f32) + middle_part
    team_grad, grad_down = gather_down(grad_middle.astype(bf16), team_cot, acts, 10)
    team_grad = team_grad.reshape(team_rows, width)
    grad_down = sum_line(grad_down)

    grad_qkv, grad_attention, grad_head_gains = attend_back(
        team_grad,
        output_weight,
        context_b,
        raw,
        turned,
        value_b,
        team_normed,
        ids,
        table,
        qgain,
        kgain,
        planes,
        6,
    )
    grad_attention = sum_line(grad_attention.reshape(-1, grad_attention.shape[2]))
    grad_normed, summed_out, grad_gate, grad_up = last_sums(
        grad_qkv.reshape(TEAM, token_count, -1),
        qkv_weight,
        acts,
        down_weight,
        [g.reshape(TEAM, rows, -1) for g in grad_units],
        planes,
        5,
    )
    grad_gate, grad_up = grad_gate.astype(f32), grad_up.astype(f32)
    _, pull_one = jax.vjp(root_mean_square_norm, inputs, norm_gain.reshape(width))
    input_part, grad_again = pull_one(grad_normed)
    grad_tokens = (grad_middle + input_part).astype(bf16)
    layer_out = (row_live * (middle + summed_out)).astype(bf16)

    def by_owner(vector):
        vector = vector.reshape(devices, -1)
        return jnp.pad(vector, ((0, 0), (0, 128 - vector.shape[1])))

    gains = jnp.stack(
        [by_owner(v) for v in (grad_again, grad_mgain, grad_head_gains[0], grad_head_gains[1])], axis=1
    )
    gains = jnp.pad(gains, ((0, 0), (0, 4), (0, 0)))
    gains = gains.reshape(planes, TEAM, 8, 128).transpose(1, 0, 2, 3)

    grad_attention, grad_gate, grad_up, layer_out, grad_tokens = lax.optimization_barrier(
        (grad_attention, grad_gate, grad_up, layer_out, grad_tokens)
    )
    grad_query, grad_key, grad_value_w, grad_output, gains = closing(
        grad_attention,
        gains,
        rows,
        (w_query.shape[1], key_weight.shape[1], value_weight.shape[1], width),
        planes,
        9,
    )
    attention_grads = tuple(
        g.astype(f32) for g in (grad_query, grad_key, grad_value_w, grad_output)
    )
    gains = (
        gains[0, : attn_gain.shape[0]],
        gains[2, : query_norm_gain.shape[0]],
        gains[3, : key_gain.shape[0]],
        gains[1, : mlp_gain.shape[0]],
    )
    grad_down, attention_grads, gains = lax.optimization_barrier(
        (grad_down, attention_grads, gains)
    )
    return (
        layer_out,
        grad_tokens,
        *attention_grads,
        *gains[:3],
        grad_gate,
        grad_up,
        grad_down.astype(f32),
        gains[3],
    )


def solution(mesh):
    by_rows, by_entry = P("fsdp", None), P("fsdp")
    return jax.shard_map(
        functools.partial(local, mesh.shape["fsdp"]),
        mesh=mesh,
        in_specs=(
            by_rows,
            by_rows,
            by_entry,
            by_rows,
            by_rows,
            by_rows,
            by_rows,
            by_rows,
            by_entry,
            by_entry,
            by_entry,
            by_rows,
            by_rows,
            by_rows,
            by_entry,
        ),
        out_specs=(
            by_rows,
            by_rows,
            by_rows,
            by_rows,
            by_rows,
            by_rows,
            by_entry,
            by_entry,
            by_entry,
            by_rows,
            by_rows,
            by_rows,
            by_entry,
        ),
        check_vma=False,
    )
```

```python
import functools

import jax
import jax.numpy as jnp
import numpy as np
from jax import lax
from jax.experimental import pallas as pl
from jax.experimental.pallas import tpu as pltpu
from jax.sharding import PartitionSpec as P

QUERY_HEADS = 16
KEY_VALUE_HEADS = 8
HEAD_SIZE = 128
TEAM = 8
STEP = 256

epsilon = 1e-06
base_theta = 1000000.0
MESH = pl.DeviceIdType.MESH
LIMIT = 60 * 2**20
f32 = jnp.float32
bf16 = jnp.bfloat16


def root_mean_square_norm(values, gain):
    return values * lax.rsqrt(jnp.mean(values * values, axis=-1, keepdims=True) + epsilon) * gain


def rotation_tables(positions):
    half = HEAD_SIZE // 2
    powers = -np.arange(half, dtype=np.float32) * np.float32(2.0) / np.float32(HEAD_SIZE)
    freqs = np.power(np.float32(base_theta), powers).astype(np.float32)
    angles = np.arange(positions, dtype=np.float32)[:, None] * freqs
    cosine, sine = np.cos(angles), np.sin(angles)
    rest = np.concatenate([cosine, cosine, -sine, sine], axis=1).astype(np.float32)
    parts = []
    for _ in range(3):
        parts.append(rest.astype(jnp.bfloat16))
        rest = rest - parts[-1].astype(np.float32)
    return np.concatenate(parts, axis=1)


def dot_last(left, right):
    return lax.dot_general(
        left, right, (((1,), (1,)), ((), ())), preferred_element_type=jnp.float32
    )


def dot_first(left, right):
    return lax.dot_general(
        left, right, (((0,), (0,)), ((), ())), preferred_element_type=jnp.float32
    )


def simple_product(left, right):
    return jnp.dot(left, right, preferred_element_type=jnp.float32)


def flipped(index, mask):
    for bit in (1, 2, 4):
        if mask & bit:
            index = index + bit * (1 - 2 * lax.rem(lax.div(index, bit), 2))
    return index


def greet(me, masks, others=()):
    barrier = pltpu.get_barrier_semaphore()
    for device in (*(flipped(me, mask) for mask in masks), *others):
        pl.semaphore_signal(barrier, inc=1, device_id=(device,), device_id_type=MESH)
    pl.semaphore_wait(barrier, len(masks) + len(others))


def remote(source, target, send, receive, device):
    return pltpu.make_async_remote_copy(
        src_ref=source,
        dst_ref=target,
        send_sem=send,
        recv_sem=receive,
        device_id=(device,),
        device_id_type=MESH,
    )


def params(collective, limit=None):
    if limit is None:
        return pltpu.CompilerParams(collective_id=collective, has_side_effects=True)
    return pltpu.CompilerParams(
        collective_id=collective, has_side_effects=True, vmem_limit_bytes=limit
    )


class Gather:
    def __init__(self, begin, x, o, me):
        self.begin, self.x, self.o, self.me = begin, x, o, me
        self.place = lax.rem(me, TEAM)
        self.half = x.shape[0] // 2

    def part(self, ref, which):
        return ref.at[pl.ds(which * self.half, self.half)]

    def first(self, which, mask):
        target = self.part(self.o.at[self.place], which)
        return self.begin(self.part(self.x, which), target, flipped(self.me, mask))

    def relay(self, origin, which, mask):
        ref = self.part(self.o.at[flipped(self.place, origin)], which)
        return self.begin(ref, ref, flipped(self.me, mask))

    def start(self):
        self.x0, self.y1 = self.first(0, 2), self.first(1, 4)
        self.x1, self.y0 = self.first(1, 2), self.first(0, 4)
        self.late = [self.first(0, 1), self.first(1, 1)]

    def forward(self):
        self.x0.wait_recv()
        self.d0 = self.relay(2, 0, 4)
        self.y1.wait_recv()
        self.d1 = self.relay(4, 1, 2)
        self.late += [self.relay(2, 0, 1), self.relay(4, 1, 1)]

    def across(self):
        self.x1.wait_recv()
        self.late.append(self.relay(2, 1, 1))
        self.y0.wait_recv()
        self.late.append(self.relay(4, 0, 1))

    def diagonal(self):
        self.d0.wait_recv()
        self.late.append(self.relay(6, 0, 1))
        self.d1.wait_recv()
        self.late.append(self.relay(6, 1, 1))

    def arrive(self):
        for copy in self.late:
            copy.wait_recv()


class Sender:
    def __init__(self, send, receive):
        self.send, self.receive, self.count, self.started = send, receive, 0, []

    def take(self):
        self.count += 1
        return self.count - 1

    def __call__(self, source, target, device):
        k = self.take()
        copy = remote(source, target, self.send.at[k], self.receive.at[k], device)
        copy.start()
        self.started.append(copy)
        return copy

    def finish(self):
        for copy in self.started:
            copy.wait_send()


class Line:
    def __init__(self, sender, ref, planes, me):
        self.sender, self.ref, self.planes = sender, ref, planes
        self.plane, self.place = lax.div(me, TEAM), lax.rem(me, TEAM)
        self.flows = [(sign, [sender.take() for _ in range(planes - 1)]) for sign in (1, -1)]

    def passing(self, step, sign, ks, source):
        block = jnp.clip(source, 0, self.planes - 1)
        beyond = jnp.clip(self.plane + sign, 0, self.planes - 1) * TEAM + self.place
        ref, k = self.ref.at[block], ks[step]
        return remote(ref, ref, self.sender.send.at[k], self.sender.receive.at[k], beyond)

    def goes(self, step, sign):
        source, onward = self.plane - sign * step, self.plane + sign
        last = self.planes - 1
        return (source >= 0) & (source <= last) & (onward >= 0) & (onward <= last)

    def start(self, step):
        for sign, ks in self.flows:
            going = self.passing(step, sign, ks, self.plane - sign * step)
            pl.when(self.goes(step, sign))(going.start)

    def arrive(self, step):
        for sign, ks in self.flows:
            source = self.plane - sign * (step + 1)
            coming = self.passing(step, sign, ks, source)
            pl.when((source >= 0) & (source <= self.planes - 1))(coming.wait_recv)

    def sent(self, step):
        for sign, ks in self.flows:
            going = self.passing(step, sign, ks, self.plane - sign * step)
            pl.when(self.goes(step, sign))(going.wait_send)

    def through(self, first, last):
        for step in range(first, last):
            self.arrive(step)
            if step + 1 < last:
                self.start(step + 1)
        for step in range(first, last):
            self.sent(step)


def line_peers(me, planes):
    return [lax.rem(me + TEAM * k, planes * TEAM) for k in range(1, planes)]


TILE = 512
STRIP = 16


class TeamSum:
    def __init__(self, sender, me, out, buffers, lefts, rights, turned):
        self.sender, self.me, self.out = sender, me, out
        self.mix, self.from_core, self.from_x, self.from_y = buffers
        self.lefts, self.rights, self.turned = lefts, rights, turned
        place = lax.rem(me, TEAM)
        self.core = lax.rem(place, 2)
        self.rows, self.width = out.shape
        self.half = self.rows // 2
        self.chips = [lax.div(flipped(place, mask), 2) for mask in (6, 2, 4, 0)]
        self.across = []

    def product(self, j):
        @pl.loop(0, self.width // TILE)
        def _(t):
            at = pl.ds(pl.multiple_of(t * TILE, TILE), TILE)
            value = 0.0
            for left, right in zip(self.lefts, self.rights):
                if len(left.shape) == 2:
                    first = pl.multiple_of(self.chips[j] * 2 * self.rows, 2 * self.rows)
                    both = left[pl.ds(first, 2 * self.rows), :]
                else:
                    both = left[pl.ds(2 * self.chips[j], 2)].reshape(2 * self.rows, left.shape[2])
                if self.turned:
                    value = value + dot_last(both, right[at, :])
                else:
                    value = value + simple_product(both, right[:, at])
            self.mix[j, :, :, at] = value.astype(bf16).reshape(2, self.rows, TILE)

        self.across.append(
            self.sender(self.mix.at[j, 1 - self.core], self.from_core.at[j], flipped(self.me, 1))
        )

    def combine(self, j):
        self.across[j].wait_recv()

        @pl.loop(0, self.rows // STRIP)
        def _(i):
            at = pl.ds(i * STRIP, STRIP)
            self.mix[j, self.core, at, :] = (
                self.mix[j, self.core, at, :].astype(f32) + self.from_core[j, at, :].astype(f32)
            ).astype(bf16)

    def begin(self, j, which, ref, slot, mask):
        source = self.mix.at[j, self.core, pl.ds(which * self.half, self.half)]
        return self.sender(source, ref.at[slot], flipped(self.me, mask))

    def add_relayed(self, j, which, ref):
        @pl.loop(0, self.half // STRIP)
        def _(i):
            at = pl.ds(which * self.half + i * STRIP, STRIP)
            self.mix[j, self.core, at, :] = (
                self.mix[j, self.core, at, :].astype(f32)
                + ref[0, pl.ds(i * STRIP, STRIP), :].astype(f32)
            ).astype(bf16)

    def start(self):
        self.product(0)
        self.product(1)
        self.combine(0)
        self.d_x = self.begin(0, 0, self.from_x, 0, 2)
        self.d_y = self.begin(0, 1, self.from_y, 0, 4)
        self.product(2)
        self.combine(1)
        self.x_0 = self.begin(1, 0, self.from_x, 1, 2)
        self.combine(2)
        self.y_1 = self.begin(2, 1, self.from_y, 1, 4)

    def own(self):
        self.product(3)

    def relay(self):
        self.d_x.wait_recv()
        self.add_relayed(2, 0, self.from_x)
        self.y_0 = self.begin(2, 0, self.from_y, 2, 4)
        self.d_y.wait_recv()
        self.add_relayed(1, 1, self.from_y)
        self.x_1 = self.begin(1, 1, self.from_x, 2, 2)

    def gather_half(self, which, slot_x, slot_y):
        @pl.loop(0, self.half // STRIP)
        def _(i):
            at = pl.ds(which * self.half + i * STRIP, STRIP)
            here = pl.ds(i * STRIP, STRIP)
            self.out[at, :] = (
                self.mix[3, self.core, at, :].astype(f32) + self.from_core[3, at, :].astype(f32)
            ) + (
                self.from_x[slot_x, here, :].astype(f32) + self.from_y[slot_y, here, :].astype(f32)
            )

    def finish(self):
        self.across[3].wait_recv()
        self.x_0.wait_recv()
        self.y_0.wait_recv()
        self.gather_half(0, 1, 2)
        self.y_1.wait_recv()
        self.x_1.wait_recv()
        self.gather_half(1, 2, 1)


SUM_COPIES = 10


def sum_buffers(rows, width):
    return [
        pltpu.VMEM((4, 2, rows, width), bf16),
        pltpu.VMEM((4, rows, width), bf16),
        pltpu.VMEM((3, rows // 2, width), bf16),
        pltpu.VMEM((3, rows // 2, width), bf16),
    ]


class Loader:
    def __init__(self, sems):
        self.sems, self.copies = sems, []

    def __call__(self, source, target):
        copy = pltpu.make_async_copy(source, target, self.sems.at[len(self.copies)])
        copy.start()
        self.copies.append(copy)
        return copy

    def wait(self):
        for copy in self.copies:
            copy.wait()


def rows_of(ref, k, rows):
    return ref.at[pl.ds(k * rows, rows)]


def turned_product(left, right, out, part, parts):
    blocks, rows, units = left.shape
    width = right.shape[2]
    tiles = width // TILE
    flat = left[...].reshape(blocks * rows, units)

    @pl.loop(part * tiles // parts, (part + 1) * tiles // parts)
    def _(t):
        at = pl.ds(pl.multiple_of(t * TILE, TILE), TILE)
        value = dot_first(flat, right[:, :, at].reshape(blocks * rows, TILE))
        out[:, at] = value.astype(bf16)


def turned_rows(left, right, out, part, parts):
    blocks, rows, width = left.shape
    tiles = width // TILE
    flat = right[...].reshape(blocks * rows, right.shape[2])

    @pl.loop(part * tiles // parts, (part + 1) * tiles // parts)
    def _(t):
        at = pl.ds(pl.multiple_of(t * TILE, TILE), TILE)
        value = dot_first(left[:, :, at].reshape(blocks * rows, TILE), flat)
        out[at, :] = value.astype(bf16)


def feed_back_kernel(parts, two, *refs):
    grads, weights, refs = refs[:parts], refs[parts : 2 * parts], refs[2 * parts :]
    out, weight_out, buffers, refs = refs[0], refs[1], refs[2:6], refs[6:]
    grads_here, weights_here = refs[:parts], refs[parts : 2 * parts]
    two_here, send, receive, own = refs[2 * parts :]
    me = lax.axis_index("fsdp")
    loader = Loader(own)
    for source, target in zip((*grads, *weights), (*grads_here, *weights_here)):
        loader(source, target)
    greet(me, (1, 2, 4))
    loader.wait()
    loader(two, two_here)
    sender = Sender(send, receive)
    total = TeamSum(sender, me, out, buffers, grads_here, weights_here, True)
    total.start()
    loader.copies[-1].wait()
    total.relay()
    total.own()
    turned_rows(two_here, grads_here[-1], weight_out, 0, 1)
    total.finish()
    sender.finish()


def feed_back(two, grads, weights, collective):
    _, rows, width = two.shape
    parts, units = len(grads), grads[0].shape[2]
    anywhere = pl.BlockSpec(memory_space=pl.ANY)
    vmem = pl.BlockSpec(memory_space=pltpu.VMEM)
    like = jax.ShapeDtypeStruct
    return pl.pallas_call(
        functools.partial(feed_back_kernel, parts),
        out_shape=(like((rows, width), f32), like((width, units), bf16)),
        in_specs=[anywhere] * (1 + 2 * parts),
        out_specs=(vmem, vmem),
        scratch_shapes=[
            *sum_buffers(rows, width),
            *(pltpu.VMEM(x.shape, bf16) for x in (*grads, *weights, two)),
            pltpu.SemaphoreType.DMA((SUM_COPIES,)),
            pltpu.SemaphoreType.DMA((SUM_COPIES,)),
            pltpu.SemaphoreType.DMA((2 * parts + 1,)),
        ],
        compiler_params=params(collective, LIMIT),
        cost_estimate=pl.CostEstimate(
            flops=2 * TEAM * rows * units * width * (parts + 1),
            bytes_accessed=2 * TEAM * rows * (units * parts + width),
            transcendentals=0,
        ),
    )(two, *grads, *weights)


def gather_down_kernel(parts, x, cot, *refs):
    acts, refs = refs[:parts], refs[parts:]
    o_ref, down_out, refs = refs[0], refs[1], refs[2:]
    acts_here, (cot_here, send, receive, own) = refs[:parts], refs[parts:]
    me = lax.axis_index("fsdp")
    loader = Loader(own)
    loader(x, o_ref.at[lax.rem(me, TEAM)])
    loader(cot, cot_here)
    for source, target in zip(acts, acts_here):
        loader(source, target)
    greet(me, (1, 2, 4))
    sender = Sender(send, receive)
    moves = Gather(sender, x, o_ref, me)
    units = acts_here[0].shape[2]

    def work(k):
        turned_product(
            acts_here[k // 2], cot_here, rows_of(down_out, k // 2, units), k % 2, 2
        )

    moves.start()
    loader.wait()
    work(0)
    moves.forward()
    work(1)
    moves.across()
    if parts > 1:
        work(2)
    moves.diagonal()
    if parts > 1:
        work(3)
    moves.arrive()
    sender.finish()


def gather_down(x, cot, acts, collective):
    rows, width = x.shape
    parts, units = len(acts), acts[0].shape[2]
    anywhere = pl.BlockSpec(memory_space=pl.ANY)
    vmem = pl.BlockSpec(memory_space=pltpu.VMEM)
    like = jax.ShapeDtypeStruct
    return pl.pallas_call(
        functools.partial(gather_down_kernel, parts),
        out_shape=(like((TEAM, rows, width), x.dtype), like((parts * units, width), bf16)),
        in_specs=[vmem, anywhere] + [anywhere] * parts,
        out_specs=(anywhere, vmem),
        scratch_shapes=[
            *(pltpu.VMEM(a.shape, bf16) for a in acts),
            pltpu.VMEM(cot.shape, bf16),
            pltpu.SemaphoreType.DMA((14,)),
            pltpu.SemaphoreType.DMA((14,)),
            pltpu.SemaphoreType.DMA((2 + parts,)),
        ],
        compiler_params=params(collective, LIMIT),
        cost_estimate=pl.CostEstimate(
            flops=2 * TEAM * rows * width * units * parts,
            bytes_accessed=6 * TEAM * rows * width,
            transcendentals=0,
        ),
    )(x, cot, *acts)


def last_sums_kernel(planes, parts, grad_qkv, qkv_weight, down, *refs):
    acts, units, refs = refs[:parts], refs[parts : 2 * parts], refs[2 * parts :]
    grad_normed, layer, gate, up, refs = *refs[:4], refs[4:]
    first, second, refs = refs[:4], refs[4:8], refs[8:]
    acts_here, downs_here, refs = refs[:parts], refs[parts : 2 * parts], refs[2 * parts :]
    grad_here, weight_here, landed, send, receive, own = refs
    me = lax.axis_index("fsdp")
    place = lax.rem(me, TEAM)
    loader = Loader(own)
    loader(grad_qkv, grad_here)
    loader(qkv_weight, weight_here)
    for k in range(parts):
        loader(units[k].at[place], landed.at[k, place])
        loader(acts[k], acts_here[k])
        loader(rows_of(down, k, downs_here[k].shape[0]), downs_here[k])
    greet(me, range(1, TEAM))
    sender = Sender(send, receive)
    moves = [
        sender(units[k].at[flipped(place, m)], landed.at[k, place], flipped(me, m))
        for k in range(parts)
        for m in SWAP_ORDER
    ]
    loader.wait()
    one = TeamSum(sender, me, grad_normed, first, [grad_here], [weight_here], True)
    two = TeamSum(sender, me, layer, second, acts_here, downs_here, False)
    one.start()
    one.own()
    two.start()
    one.relay()
    two.own()
    two.relay()
    for copy in moves:
        copy.wait_recv()
    block = gate.shape[1] // (planes * TEAM)
    some = planes // parts
    span = TEAM * block
    for j, ref in enumerate((gate, up)):
        for g in range(planes):
            at = (j * some + g % some) * block
            ref[:, g * span : (g + 1) * span] = jnp.concatenate(
                [landed[g // some, q, :, at : at + block] for q in range(TEAM)], axis=1
            )
    one.finish()
    two.finish()
    sender.finish()


def last_sums(grad_qkv, qkv_weight, acts, down, units, planes, collective):
    _, rows, depth = grad_qkv.shape
    width = qkv_weight.shape[0]
    parts = len(acts)
    anywhere = pl.BlockSpec(memory_space=pl.ANY)
    vmem = pl.BlockSpec(memory_space=pltpu.VMEM)
    like = jax.ShapeDtypeStruct
    _, own_rows, some = units[0].shape
    links = 2 * SUM_COPIES + (TEAM - 1) * parts
    home = like((own_rows, TEAM * parts * some // 2), bf16)
    return pl.pallas_call(
        functools.partial(last_sums_kernel, planes, parts),
        out_shape=(like((rows, width), f32),) * 2 + (home,) * 2,
        in_specs=[anywhere] * (3 + 2 * parts),
        out_specs=(vmem,) * 4,
        scratch_shapes=[
            *sum_buffers(rows, width),
            *sum_buffers(rows, width),
            *(pltpu.VMEM(a.shape, bf16) for a in acts),
            *(pltpu.VMEM((a.shape[2], width), bf16) for a in acts),
            pltpu.VMEM(grad_qkv.shape, bf16),
            pltpu.VMEM(qkv_weight.shape, bf16),
            pltpu.VMEM((parts, *units[0].shape), bf16),
            pltpu.SemaphoreType.DMA((links,)),
            pltpu.SemaphoreType.DMA((links,)),
            pltpu.SemaphoreType.DMA((2 + 3 * parts,)),
        ],
        compiler_params=params(collective, LIMIT),
        cost_estimate=pl.CostEstimate(
            flops=2 * TEAM * rows * width * (depth + sum(a.shape[2] for a in acts)),
            bytes_accessed=4 * TEAM * rows * depth,
            transcendentals=0,
        ),
    )(grad_qkv, qkv_weight, down, *acts, *units)


SWAP_ORDER = (6, 7, 2, 3, 4, 5, 1)


def open_kernel(
    planes, parts, query_in, key_in, value_in, output_in, tokens_in, gate_in, up_in, down_in, *refs
):
    smalls, refs = refs[:5], refs[5:]
    gate_up, refs = refs[:parts], refs[parts:]
    qkv, output_raw, output, tokens, down, *gain_refs, numbers = refs[:10]
    small_in, small, sorted_units, send, receive, own = refs[10:]
    slots, sequence = smalls[4].shape
    small_in[...] = jnp.zeros_like(small_in)
    for k, ref in enumerate(smalls):
        small_in[k : k + ref.shape[0], : ref.shape[1]] = ref[...].astype(f32)
    me = lax.axis_index("fsdp")
    place = lax.rem(me, TEAM)
    plane = lax.div(me, TEAM)
    team = me - place
    others = [lax.rem(me + TEAM * k, planes * TEAM) for k in range(1, planes)]
    sender = Sender(send, receive)
    keeps = []

    def keep(source, target):
        copy = pltpu.make_async_copy(source, target, own.at[len(keeps)])
        copy.start()
        keeps.append(copy)

    qkv_parts, at = [], 0
    for ref in (query_in, key_in, value_in):
        part = ref.shape[1] // TEAM
        qkv_parts.append((ref, part, qkv.at[plane, place, :, pl.ds(at, part)]))
        at += part

    def columns(ref, part, target):
        return ref.at[:, pl.ds(pl.multiple_of(target * part, part), part)]

    for ref, part, target in qkv_parts:
        keep(columns(ref, part, place), target)
    keep(small_in, small.at[me])
    keep(tokens_in, tokens.at[place])
    keep(down_in, down.at[plane])
    keep(output_in, output_raw.at[plane])
    greet(me, range(1, TEAM), others)

    qkv_line = Line(sender, qkv, planes, me)
    out_line = Line(sender, output_raw, planes, me)
    down_line = Line(sender, down, planes, me)
    rows_tokens = Gather(sender, tokens_in, tokens, me)
    spread_send = [sender.take() for _ in range(planes)]
    spread_own = len(keeps)

    def outgoing(k):
        number = TEAM * k + place
        partner, there = lax.div(number, planes), lax.rem(number, planes)
        s, r = send.at[spread_send[0] + k], receive.at[spread_send[0] + there]
        over = remote(output_raw.at[k], output.at[there], s, r, team + partner)
        here = pltpu.make_async_copy(output_raw.at[k], output.at[there], own.at[spread_own + k])
        return partner, over, here

    def incoming(k):
        partner = lax.rem(planes * place + k, TEAM)
        s, r = send.at[spread_send[k]], receive.at[spread_send[k]]
        return partner, remote(output_raw.at[k], output.at[k], s, r, team + partner)

    def spread_one(k, inside):
        partner, over, here = outgoing(jnp.clip(k, 0, planes - 1))
        pl.when(inside & (partner != place))(over.start)
        pl.when(inside & (partner == place))(here.start)

    def step_out(step):
        out_line.arrive(step)
        if step < planes - 2:
            out_line.start(step + 1)
        spread_one(plane - step - 1, plane - step - 1 >= 0)
        spread_one(plane + step + 1, plane + step + 1 <= planes - 1)

    swaps = [
        sender(columns(ref, part, flipped(place, m)), target, flipped(me, m))
        for m in SWAP_ORDER
        for ref, part, target in qkv_parts
    ]
    near = [sender(small_in, small.at[me], flipped(me, m)) for m in SWAP_ORDER]
    keeps[-1].wait()
    out_line.start(0)
    keeps[-2].wait()
    down_line.start(0)
    block = gate_in.shape[1] // (planes * TEAM)
    some = planes // parts
    units = some * block
    for k in range(parts):
        for q in range(TEAM):
            for j, ref in enumerate((gate_in, up_in)):
                starts = [(TEAM * g + q) * block for g in range(k * some, (k + 1) * some)]
                sorted_units[k, q, :, j * units : (j + 1) * units] = jnp.concatenate(
                    [ref[:, at : at + block] for at in starts], axis=1
                )
    for copy in swaps:
        copy.wait_recv()
    for copy in keeps[:3]:
        copy.wait()
    qkv_line.start(0)
    rows_tokens.start()
    moves = [
        sender(sorted_units.at[k, flipped(place, m)], gate_up[k].at[plane, place], flipped(me, m))
        for k in range(parts)
        for m in SWAP_ORDER
    ]
    kept_units = [
        pltpu.make_async_copy(
            sorted_units.at[k, place], gate_up[k].at[plane, place], own.at[spread_own + planes + k]
        )
        for k in range(parts)
    ]
    for copy in kept_units:
        copy.start()
    spread_one(plane, True)
    rows_tokens.forward()
    step_out(0)
    for copy in near:
        copy.wait_recv()
    keeps[3].wait()
    shared = small.at[pl.ds(team, TEAM)]
    far = [sender(shared, shared, other) for other in others]
    rows_tokens.across()
    for step in range(planes - 1):
        qkv_line.arrive(step)
        if step < planes - 2:
            qkv_line.start(step + 1)
            step_out(step + 1)
        down_line.arrive(step)
        if step < planes - 2:
            down_line.start(step + 1)
        if step == 0:
            rows_tokens.diagonal()
        if step == 1:
            for copy in far:
                copy.wait_recv()
            for k, ref in enumerate(gain_refs):
                part = smalls[k].shape[1]
                ref[...] = jnp.concatenate(
                    [small[i, k : k + 1, :part] for i in range(planes * TEAM)], axis=1
                )
            per_step = STEP // sequence
            for i in range(numbers.shape[0]):
                pieces = []
                for m in range(i * per_step, (i + 1) * per_step):
                    row = 4 + m % slots
                    pieces.append(small[team + m // slots, row : row + 1, :sequence] + 64.0 * m)
                numbers[i] = jnp.concatenate(pieces, axis=1)
    rows_tokens.arrive()
    for copy in moves:
        copy.wait_recv()
    for copy in kept_units:
        copy.wait()
    for k in range(planes):
        partner, over, here = outgoing(k)
        pl.when(partner != place)(over.wait_send)
        pl.when(partner == place)(here.wait)
        partner, arriving = incoming(k)
        pl.when(partner != place)(arriving.wait_recv)
    for step in range(planes - 1):
        qkv_line.sent(step)
        out_line.sent(step)
        down_line.sent(step)
    sender.finish()
    for copy in keeps[4:-2]:
        copy.wait()


def opening(query, key, value, output, tokens, gate, up, down, smalls, planes, parts, collective):
    links = 28 + 6 * (planes - 1) + 14 + planes - 1 + planes + parts * (TEAM - 1)
    anywhere = pl.BlockSpec(memory_space=pl.ANY)
    vmem = pl.BlockSpec(memory_space=pltpu.VMEM)
    like = jax.ShapeDtypeStruct
    rows = query.shape[0]
    width = (query.shape[1] + key.shape[1] + value.shape[1]) // TEAM
    units = (TEAM, rows, 2 * gate.shape[1] // TEAM // parts)
    devices = planes * TEAM
    return pl.pallas_call(
        functools.partial(open_kernel, planes, parts),
        out_shape=(
            *((like((planes, *units), bf16),) * parts),
            like((planes, TEAM, rows, width), bf16),
            like((planes, *output.shape), bf16),
            like((planes, *output.shape), bf16),
            like((TEAM, *tokens.shape), bf16),
            like((planes, *down.shape), bf16),
            *(like((1, devices * x.shape[1]), f32) for x in smalls[:4]),
            like((TEAM * tokens.shape[0] // STEP, 1, STEP), f32),
        ),
        in_specs=[vmem] * 13,
        out_specs=(anywhere,) * (5 + parts) + (vmem,) * 5,
        scratch_shapes=[
            pltpu.VMEM((8, 128), f32),
            pltpu.VMEM((devices, 8, 128), f32),
            pltpu.VMEM((parts, *units), bf16),
            pltpu.SemaphoreType.DMA((links,)),
            pltpu.SemaphoreType.DMA((links,)),
            pltpu.SemaphoreType.DMA((7 + planes + parts,)),
        ],
        compiler_params=params(collective, LIMIT),
    )(query, key, value, output, tokens, gate, up, down, *smalls)


def close_kernel(planes, x_ref, gains, *refs):
    query_ref, key_ref, value_ref, output_ref, gain_ref, *refs = refs
    landed, mine, near_in, mid, far_in, send, receive, own = refs
    me = lax.axis_index("fsdp")
    place = lax.rem(me, TEAM)
    plane = lax.div(me, TEAM)
    others = [lax.rem(me + TEAM * k, planes * TEAM) for k in range(1, planes)]
    rows = landed.shape[1]

    def part(target):
        return x_ref.at[pl.ds(pl.multiple_of(target * rows, rows), rows)]

    keep = pltpu.make_async_copy(part(place), landed.at[place], own.at[0])
    keep.start()
    keep_mine = pltpu.make_async_copy(
        x_ref.at[pl.ds(TEAM * rows, mine.shape[0])], mine, own.at[1]
    )
    keep_mine.start()
    greet(me, range(1, TEAM), others)
    sender = Sender(send, receive)
    near = [
        sender(gains.at[flipped(place, m)], near_in.at[m - 1], flipped(me, m)) for m in SWAP_ORDER
    ]
    moves = [
        sender(part(flipped(place, m)), landed.at[place], flipped(me, m)) for m in SWAP_ORDER
    ]
    for copy in near:
        copy.wait_recv()
    summed = gains[place]
    for mask in range(1, TEAM):
        summed = summed + near_in[mask - 1]
    mid[...] = summed
    far = [
        sender(mid.at[lax.rem(plane + k + 1, planes)], far_in.at[k], other)
        for k, other in enumerate(others)
    ]
    keep_mine.wait()
    width = mine.shape[1]
    for c in range(output_ref.shape[1] // width):
        output_ref[:, c * width : (c + 1) * width] = mine[c * rows : (c + 1) * rows]
    for copy in moves:
        copy.wait_recv()
    keep.wait()
    at = 0
    for ref in (query_ref, key_ref, value_ref):
        part_width = ref.shape[1] // TEAM
        for q in range(TEAM):
            ref[:, q * part_width : (q + 1) * part_width] = landed[q, :, at : at + part_width]
        at += part_width
    for copy in far:
        copy.wait_recv()
    result = mid[plane]
    for k in range(planes - 1):
        result = result + far_in[k]
    gain_ref[...] = result
    sender.finish()


def closing(x, gains, rows, widths, planes, collective):
    links = 2 * (TEAM - 1) + planes - 1
    block = gains.shape[2:]
    vmem = pl.BlockSpec(memory_space=pltpu.VMEM)
    like = jax.ShapeDtypeStruct
    return pl.pallas_call(
        functools.partial(close_kernel, planes),
        out_shape=(*(like((rows, w), bf16) for w in widths), like(block, f32)),
        in_specs=[pl.BlockSpec(memory_space=pl.ANY), vmem],
        out_specs=(vmem,) * 5,
        scratch_shapes=[
            pltpu.VMEM((TEAM, rows, x.shape[1]), x.dtype),
            pltpu.VMEM((x.shape[0] - TEAM * rows, x.shape[1]), x.dtype),
            pltpu.VMEM((TEAM - 1, planes, *block), f32),
            pltpu.VMEM((planes, *block), f32),
            pltpu.VMEM((planes - 1, *block), f32),
            pltpu.SemaphoreType.DMA((links,)),
            pltpu.SemaphoreType.DMA((links,)),
            pltpu.SemaphoreType.DMA((2,)),
        ],
        compiler_params=params(collective, LIMIT),
    )(x, gains)


def visible_and_tables(ids_row, table):
    rows = ids_row.shape[1]
    row_at = lax.broadcasted_iota(jnp.int32, (rows, rows), 0)
    column_at = lax.broadcasted_iota(jnp.int32, (rows, rows), 1)
    ids_column = jnp.sum(jnp.where(row_at == column_at, ids_row, 0.0), axis=1, keepdims=True)
    visible = (ids_column == ids_row) & (column_at <= row_at)
    sequence = table.shape[0]
    place = jnp.sum(visible.astype(f32), axis=1, keepdims=True) - 1.0
    at = lax.broadcasted_iota(jnp.int32, (rows, sequence), 1).astype(f32)
    chosen = (at == place).astype(bf16)
    both = simple_product(chosen, table)
    width = 2 * HEAD_SIZE
    both = (both[:, :width] + both[:, width : 2 * width]) + both[:, 2 * width :]
    return visible, both[:, :HEAD_SIZE], both[:, HEAD_SIZE:]


def softmax(query, key, visible):
    scores = dot_last(query, key) * HEAD_SIZE ** (-0.5)
    scores = jnp.where(visible, scores, -1e30)
    expos = jnp.exp(scores - jnp.max(scores, axis=1, keepdims=True))
    return expos / jnp.sum(expos, axis=1, keepdims=True)


def by_step(*shape):
    return pl.BlockSpec(shape, lambda i: (i, *(0 for _ in shape[1:])))


def fixed(*shape):
    return pl.BlockSpec(shape, lambda i: tuple(0 for _ in shape))


def attend_kernel(
    planes, x_in, gain, weight, ids_row, table, query_gain, key_gain, right_in, tokens, cot_in, live,
    mlp_gain, _, normed_out, raw_out, turned_out, value_out, context_out, out, two, cot, units,
    x_ref, normed_ref, raw_ref, turned_ref, value_ref, context_ref, cot_own,
    mix, from_core, from_x, from_y, right, send, receive, own,
):
    me = lax.axis_index("fsdp")
    loader = Loader(own)
    steps = x_ref.shape[0] // STEP
    for i in range(steps):
        loader(rows_of(x_in, i, STEP), rows_of(x_ref, i, STEP))
    load_right = loader(right_in, right)
    cot_own[...] = cot_in[...] * live[...]
    keep = loader(cot_own, cot.at[lax.rem(me, TEAM)])
    greet(me, (1, 2, 4), line_peers(me, planes))
    sender = Sender(send, receive)
    line = Line(sender, units, planes, me)
    rows_cot = Gather(sender, cot_own, cot, me)
    line.start(0)
    rows_cot.start()
    heads = context_ref.shape[1] // HEAD_SIZE
    homes = []

    def attention(i):
        loader.copies[i].wait()
        here = slice(i * STEP, (i + 1) * STEP)
        x = x_ref[here].astype(f32)
        scale = lax.rsqrt(jnp.mean(x * x, axis=1, keepdims=True) + epsilon)
        normed = (x * scale * gain[...]).astype(bf16)
        normed_ref[here] = normed
        projected = simple_product(normed, weight[...])
        visible, cosine, sine = visible_and_tables(ids_row[i], table[...])
        raw_ref[here] = projected[:, : (heads + 1) * HEAD_SIZE]
        value = projected[:, (heads + 1) * HEAD_SIZE :].astype(bf16)
        value_ref[here] = value
        turned = []
        for h in range(heads + 1):
            at = slice(h * HEAD_SIZE, (h + 1) * HEAD_SIZE)
            raw = projected[:, at]
            head_gain = query_gain if h < heads else key_gain
            scale = lax.rsqrt(jnp.mean(raw * raw, axis=1, keepdims=True) + epsilon)
            y = raw * scale * head_gain[...]
            y = y * cosine + pltpu.roll(y, HEAD_SIZE // 2, 1) * sine
            turned.append(y.astype(bf16))
            turned_ref[here, at] = turned[-1]
        for h in range(heads):
            probs = softmax(turned[h], turned[heads], visible).astype(bf16)
            context = simple_product(probs, value)
            context_ref[here, h * HEAD_SIZE : (h + 1) * HEAD_SIZE] = context.astype(bf16)
        for ref, home in (
            (normed_ref, normed_out), (raw_ref, raw_out), (turned_ref, turned_out),
            (value_ref, value_out), (context_ref, context_out),
        ):
            homes.append(loader(rows_of(ref, i, STEP), rows_of(home, i, STEP)))

    for i in range(steps):
        attention(i)
        if i == steps // 2 - 1:
            rows_cot.forward()
    rows_cot.across()
    line.arrive(0)
    if planes > 2:
        line.start(1)
    load_right.wait()
    buffers = [mix, from_core, from_x, from_y]
    total = TeamSum(sender, me, out, buffers, [context_ref], [right], False)
    total.start()
    rows_cot.diagonal()
    total.own()
    total.relay()
    if planes > 2:
        line.arrive(1)
    if planes > 3:
        line.start(2)
    total.finish()

    @pl.loop(0, out.shape[0] // STRIP)
    def _(i):
        at = pl.ds(i * STRIP, STRIP)
        middle = tokens[at, :].astype(f32) + out[at, :]
        out[at, :] = middle
        scale = lax.rsqrt(jnp.mean(middle * middle, axis=1, keepdims=True) + epsilon)
        two[at, :] = (middle * scale * mlp_gain[...]).astype(bf16)

    rows_cot.arrive()
    if planes > 3:
        line.through(2, planes - 1)
    for step in range(min(2, planes - 1)):
        line.sent(step)
    sender.finish()
    for copy in (keep, *homes):
        copy.wait()


def attend(
    x, gain, weight, ids, table, query_gain, key_gain, right, tokens, cot, live, mlp_gain, units,
    planes, collective,
):
    rows, width = x.shape
    out = weight.shape[1]
    heads = out - 2 * HEAD_SIZE
    own_rows = tokens.shape[0]
    steps = rows // STEP
    like = jax.ShapeDtypeStruct
    anywhere = pl.BlockSpec(memory_space=pl.ANY)
    vmem = pl.BlockSpec(memory_space=pltpu.VMEM)
    kept = (
        like((rows, width), bf16),
        like((rows, heads + HEAD_SIZE), f32),
        like((rows, heads + HEAD_SIZE), bf16),
        like((rows, HEAD_SIZE), bf16),
        like((rows, heads), bf16),
    )
    links = SUM_COPIES + 14 + 2 * (planes - 1)
    return pl.pallas_call(
        functools.partial(attend_kernel, planes),
        out_shape=(
            *kept,
            like((own_rows, width), f32),
            like((own_rows, width), bf16),
            like((TEAM, own_rows, width), bf16),
            like(units.shape, bf16),
        ),
        in_specs=[anywhere] + [vmem] * 6 + [anywhere] + [vmem] * 4 + [anywhere],
        out_specs=(*([anywhere] * 5), vmem, vmem, anywhere, anywhere),
        input_output_aliases={12: 8},
        scratch_shapes=[
            pltpu.VMEM((rows, width), bf16),
            *(pltpu.VMEM(x.shape, x.dtype) for x in kept),
            pltpu.VMEM((own_rows, width), bf16),
            *sum_buffers(own_rows, width),
            pltpu.VMEM(right.shape, bf16),
            pltpu.SemaphoreType.DMA((links,)),
            pltpu.SemaphoreType.DMA((links,)),
            pltpu.SemaphoreType.DMA((6 * steps + 2,)),
        ],
        compiler_params=params(collective, LIMIT),
        cost_estimate=pl.CostEstimate(
            flops=2 * rows * width * (out + heads),
            bytes_accessed=8 * rows * width,
            transcendentals=0,
        ),
    )(
        x, gain, weight, ids, table, query_gain, key_gain, right, tokens, cot, live, mlp_gain, units
    )


def attend_back_kernel(planes, grad_in, out_weight, context, raw_in, turned_in, value_in, normed_in,
    ids_row, table, query_gain, key_gain, grad_raw_ref, merged, grad_gains_ref,
    grad_ref, raw_ref, turned_ref, value_ref, normed_ref, out_sum, weight_sum, send, receive, own,
):
    me = lax.axis_index("fsdp")
    place = lax.rem(me, TEAM)
    team = me - place
    loader = Loader(own)
    loader(grad_in, grad_ref)
    for source, target in (
        (raw_in, raw_ref), (turned_in, turned_ref), (value_in, value_ref), (normed_in, normed_ref)
    ):
        loader(source, target)
    greet(me, range(1, TEAM))
    loader.copies[0].wait()

    total, width = grad_ref.shape
    heads = context.shape[1] // HEAD_SIZE
    out = weight_sum.shape[1]
    rows, block = weight_sum.shape[0] // planes, out_sum.shape[0] // planes
    cuts = width // out

    def source(k, c):
        return out_sum.at[pl.ds(k * block, block), pl.ds(c * out, out)]

    def target(k, c):
        return merged.at[k, pl.ds(rows + c * block, block)]

    def outgoing(k, c):
        number = planes * place + k
        partner, there = lax.rem(number, TEAM), lax.div(number, TEAM)
        s, r = send.at[k * cuts + c], receive.at[there * cuts + c]
        over = remote(source(k, c), target(there, c), s, r, team + partner)
        here = pltpu.make_async_copy(source(k, c), target(there, c), own.at[5 + k * cuts + c])
        return partner, over, here

    def incoming(k, c):
        partner = lax.div(TEAM * k + place, planes)
        s, r = send.at[k * cuts + c], receive.at[k * cuts + c]
        return partner, remote(source(k, c), target(k, c), s, r, team + partner)

    for c in range(cuts):
        at = slice(c * out, (c + 1) * out)
        out_sum[:, at] = dot_first(context[...], grad_ref[:, at]).astype(bf16)
        for k in range(planes):
            partner, over, here = outgoing(k, c)
            pl.when(partner != place)(over.start)
            pl.when(partner == place)(here.start)

    grad_gains_ref[...] = jnp.zeros_like(grad_gains_ref)
    for copy in loader.copies[1:]:
        copy.wait()

    @pl.loop(0, total // STEP)
    def _(i):
        here = pl.ds(pl.multiple_of(i * STEP, STEP), STEP)
        grad_context = dot_last(grad_ref[here, :], out_weight[...]).astype(bf16)
        visible, cosine, sine = visible_and_tables(ids_row[i], table[...])
        value = value_ref[here, :]
        key = turned_ref[here, heads * HEAD_SIZE :]
        grads = []
        grad_value = 0.0
        grad_key = 0.0
        for h in range(heads):
            at = slice(h * HEAD_SIZE, (h + 1) * HEAD_SIZE)
            query = turned_ref[here, at]
            probs = softmax(query, key, visible)
            grad_value = grad_value + dot_first(probs.astype(bf16), grad_context[:, at])
            grad_probs = dot_last(grad_context[:, at], value)
            inner = jnp.sum(probs * grad_probs, axis=1, keepdims=True)
            grad_scores = (probs * (grad_probs - inner)).astype(bf16)
            grads.append(simple_product(grad_scores, key) * HEAD_SIZE ** (-0.5))
            grad_key = grad_key + dot_first(grad_scores, query) * HEAD_SIZE ** (-0.5)
        grads.append(grad_key)
        parts = []
        for h in range(heads + 1):
            raw = raw_ref[here, h * HEAD_SIZE : (h + 1) * HEAD_SIZE]
            head_gain = query_gain[...] if h < heads else key_gain[...]
            scale = lax.rsqrt(jnp.mean(raw * raw, axis=1, keepdims=True) + epsilon)
            turned = grads[h] * cosine + pltpu.roll(grads[h] * sine, HEAD_SIZE // 2, 1)
            row = 0 if h < heads else 1
            grad_gains_ref[row : row + 1, :] += jnp.sum(turned * raw * scale, axis=0, keepdims=True)
            turned = turned * head_gain
            mean = jnp.mean(turned * raw, axis=1, keepdims=True)
            parts.append((turned * scale - raw * (scale * scale * scale * mean)).astype(bf16))
        parts.append(grad_value.astype(bf16))
        grad_raw_ref[here, :] = jnp.concatenate(parts, axis=1)

    @pl.loop(0, planes)
    def _(g):
        at = pl.ds(pl.multiple_of(g * rows, rows), rows)
        weight_sum[at, :] = dot_first(normed_ref[:, at], grad_raw_ref[...]).astype(bf16)

    homes = []
    for g in range(planes):
        copy = pltpu.make_async_copy(
            weight_sum.at[pl.ds(g * rows, rows)],
            merged.at[g, pl.ds(0, rows)],
            own.at[5 + planes * cuts + g],
        )
        copy.start()
        homes.append(copy)
    for k in range(planes):
        for c in range(cuts):
            partner, over, here = outgoing(k, c)
            pl.when(partner != place)(over.wait_send)
            pl.when(partner == place)(here.wait)
            partner, arriving = incoming(k, c)
            pl.when(partner != place)(arriving.wait_recv)
    for copy in homes:
        copy.wait()


def attend_back(
    grad, out_weight, context, raw, turned, value, normed, ids, table, query_gain, key_gain,
    planes, collective,
):
    rows, width = grad.shape
    heads = context.shape[1]
    out = heads + 2 * HEAD_SIZE
    merged = (planes, (width + heads * width // out) // planes, out)
    copies = planes * (width // out)
    anywhere = pl.BlockSpec(memory_space=pl.ANY)
    vmem = pl.BlockSpec(memory_space=pltpu.VMEM)
    like = jax.ShapeDtypeStruct
    return pl.pallas_call(
        functools.partial(attend_back_kernel, planes),
        out_shape=(like((rows, out), bf16), like(merged, bf16), like((8, HEAD_SIZE), f32)),
        in_specs=[anywhere, vmem, vmem] + [anywhere] * 4 + [vmem] * 4,
        out_specs=(vmem, anywhere, vmem),
        scratch_shapes=[
            *(pltpu.VMEM(x.shape, x.dtype) for x in (grad, raw, turned, value, normed)),
            pltpu.VMEM((heads, width), bf16),
            pltpu.VMEM((width, out), bf16),
            pltpu.SemaphoreType.DMA((copies,)),
            pltpu.SemaphoreType.DMA((copies,)),
            pltpu.SemaphoreType.DMA((5 + copies + planes,)),
        ],
        compiler_params=params(collective, LIMIT),
        cost_estimate=pl.CostEstimate(
            flops=2 * rows * width * (out + 2 * heads),
            bytes_accessed=8 * rows * width,
            transcendentals=0,
        ),
    )(grad, out_weight, context, raw, turned, value, normed, ids, table, query_gain, key_gain)


def hidden(two, weight):
    return simple_product(two, weight)


def hidden_grads(both, cot, down):
    units = both.shape[1] // 2
    gate, up = both[:, :units], both[:, units:]
    grad_act = dot_last(cot, down)
    sigma = 1.0 / (1.0 + jnp.exp(-gate))
    silu_gate = gate * sigma
    act = (silu_gate * up).astype(bf16)
    grad_gate = (grad_act * up * (sigma * (1.0 + gate * (1.0 - sigma)))).astype(bf16)
    grad_up = (grad_act * silu_gate).astype(bf16)
    return act, grad_gate, grad_up


def feed_kernel(
    planes, two_in, cot_in, weight_in, down_in, _, two_out, act_out, grad_both_out,
    weight_out, units_ref, two, cot, weight, down, both, weight_sum, act, grad_both, grad_weight,
    send, receive, own,
):
    me = lax.axis_index("fsdp")
    place = lax.rem(me, TEAM)
    loader = Loader(own)
    loader(two_in, two.at[place])
    loader(cot_in, cot)
    loader(weight_in, weight)
    loader(rows_of(down_in, 0, down.shape[0]), down)
    greet(me, (1, 2, 4), line_peers(me, planes))
    sender = Sender(send, receive)
    rows_two = Gather(sender, two_in, two, me)
    line = Line(sender, units_ref, planes, me)
    rows_two.start()
    line.start(0)
    rows, units = act.shape[1:]
    width = two.shape[2]

    crossed = {0: (0, 1), 2: (2, 4), 4: (3, 5), 6: (6, 7)}

    def chip_of(mask):
        return pl.ds(2 * lax.div(flipped(place, mask), 2), 2)

    def work(mask):
        for k in crossed[mask]:
            rows_two.late[k].wait_recv()
        chip = chip_of(mask)
        loader(two.at[chip], two_out.at[chip])
        both[...] = simple_product(two[chip].reshape(2 * rows, width), weight[...])
        flat = cot[chip].reshape(2 * rows, width)
        a, grad_gate, grad_up = hidden_grads(both[...], flat, down[...])
        act[chip] = a.reshape(2, rows, units)
        loader(act.at[chip], act_out.at[chip])
        grads = jnp.concatenate([grad_gate, grad_up], axis=1)
        grad_both[chip] = grads.reshape(2, rows, 2 * units)
        loader(grad_both.at[chip], grad_both_out.at[chip])
        for t in range(width // TILE):
            at = slice(t * TILE, (t + 1) * TILE)
            left = two[chip, :, at].reshape(2 * rows, TILE)
            term = dot_first(left, grads)
            if mask == 0:
                weight_sum[at, :] = term
            elif mask != 6:
                weight_sum[at, :] += term
            else:
                tile = pl.ds(t * TILE, TILE)
                grad_weight[at, :] = (weight_sum[at, :] + term).astype(bf16)
                loader(grad_weight.at[tile], weight_out.at[tile])

    rows_two.forward()
    loader.wait()
    work(0)
    rows_two.across()
    line.arrive(0)
    if planes > 2:
        line.start(1)
    work(2)
    rows_two.diagonal()
    work(4)
    if planes > 2:
        line.arrive(1)
    if planes > 3:
        line.start(2)
    work(6)
    if planes > 3:
        line.through(2, planes - 1)
    for step in range(min(2, planes - 1)):
        line.sent(step)
    sender.finish()
    for copy in loader.copies[4:]:
        copy.wait()


def feed(two, cot, weight, down, next_units, planes, collective):
    rows, width = two.shape
    units = weight.shape[1] // 2
    anywhere = pl.BlockSpec(memory_space=pl.ANY)
    like = jax.ShapeDtypeStruct
    return pl.pallas_call(
        functools.partial(feed_kernel, planes),
        out_shape=(
            like((TEAM, rows, width), bf16),
            like((TEAM, rows, units), bf16),
            like((TEAM, rows, 2 * units), bf16),
            like(weight.shape, bf16),
            like(next_units.shape, bf16),
        ),
        in_specs=[anywhere] * 5,
        out_specs=(anywhere,) * 5,
        input_output_aliases={4: 4},
        scratch_shapes=[
            pltpu.VMEM((TEAM, rows, width), bf16),
            pltpu.VMEM((TEAM, rows, width), bf16),
            pltpu.VMEM(weight.shape, bf16),
            pltpu.VMEM((units, width), bf16),
            pltpu.VMEM((2 * rows, 2 * units), f32),
            pltpu.VMEM(weight.shape, f32),
            pltpu.VMEM((TEAM, rows, units), bf16),
            pltpu.VMEM((TEAM, rows, 2 * units), bf16),
            pltpu.VMEM(weight.shape, bf16),
            pltpu.SemaphoreType.DMA((14 + 2 * (planes - 1),)),
            pltpu.SemaphoreType.DMA((14 + 2 * (planes - 1),)),
            pltpu.SemaphoreType.DMA((16 + width // TILE,)),
        ],
        compiler_params=params(collective, LIMIT),
        cost_estimate=pl.CostEstimate(
            flops=10 * TEAM * rows * width * units,
            bytes_accessed=8 * TEAM * rows * width,
            transcendentals=0,
        ),
    )(two, cot, weight, down, next_units)


def feed_rest_kernel(two, cot, weight, down, act, grad_both):
    blocks, rows, units = act.shape
    both = simple_product(two[...].reshape(blocks * rows, -1), weight[...])
    flat = cot[...].reshape(blocks * rows, -1)
    a, grad_gate, grad_up = hidden_grads(both, flat, down[...])
    act[...] = a.reshape(blocks, rows, units)
    grad_both[:, :, :units] = grad_gate.reshape(blocks, rows, units)
    grad_both[:, :, units:] = grad_up.reshape(blocks, rows, units)


def feed_rest(two, cot, weight, down, part):
    _, rows, width = two.shape
    units = weight.shape[1] // 2
    like = jax.ShapeDtypeStruct
    return pl.pallas_call(
        feed_rest_kernel,
        grid=(TEAM // 2,),
        out_shape=(like((TEAM, rows, units), bf16), like((TEAM, rows, 2 * units), bf16)),
        in_specs=[
            by_step(2, rows, width),
            by_step(2, rows, width),
            fixed(*weight.shape),
            pl.BlockSpec((units, width), lambda i: (part, 0)),
        ],
        out_specs=(by_step(2, rows, units), by_step(2, rows, 2 * units)),
        compiler_params=pltpu.CompilerParams(vmem_limit_bytes=LIMIT),
        cost_estimate=pl.CostEstimate(
            flops=6 * TEAM * rows * width * units,
            bytes_accessed=4 * TEAM * rows * width,
            transcendentals=0,
        ),
    )(two, cot, weight, down)


def local(
    devices,
    tokens,
    segments,
    micro_live,
    cotangent,
    w_query,
    key_weight,
    value_weight,
    w_output,
    attn_gain,
    query_norm_gain,
    key_gain,
    w_gate,
    w_up,
    w_down,
    mlp_gain,
):
    planes = devices // TEAM
    lines = [[place + TEAM * k for k in range(planes)] for place in range(TEAM)]
    slots, sequence = segments.shape
    token_count, width = tokens.shape
    groups = QUERY_HEADS // KEY_VALUE_HEADS
    rows = w_query.shape[0]
    parts = 2
    team_rows = TEAM * token_count
    head_width = groups * HEAD_SIZE
    me = lax.axis_index("fsdp")
    plane = me // TEAM

    def sum_line(x):
        return lax.psum_scatter(
            x, "fsdp", scatter_dimension=0, tiled=True, axis_index_groups=lines
        )

    slot_live = (lax.broadcasted_iota(jnp.int32, (slots, 1), 0) < micro_live[0]).astype(f32)
    row_live = jnp.broadcast_to(slot_live, (slots, sequence)).reshape(token_count, 1)

    smalls = [x[None] for x in (attn_gain, mlp_gain, query_norm_gain, key_gain)] + [segments]
    opened = opening(
        w_query,
        key_weight,
        value_weight,
        w_output,
        tokens,
        w_gate,
        w_up,
        w_down,
        smalls,
        planes,
        parts,
        1,
    )
    unit_slices, opened = opened[:parts], opened[parts:]
    qkv_weight, _, output_weight, team_tokens, down_weight = opened[:5]
    norm_gain, mlp_norm_gain, qgain, kgain, ids = opened[5:]
    mlp_norm_gain = mlp_norm_gain.reshape(width)
    qkv_weight = qkv_weight.reshape(width, -1)
    output_weight = output_weight.reshape(head_width, width)
    down_weight = down_weight.reshape(-1, width)
    table = jnp.asarray(rotation_tables(sequence))

    inputs = tokens.astype(f32)
    first, second = unit_slices
    team_normed, raw, turned, value_b, context_b, middle, normed_two, team_cot, first = attend(
        team_tokens.reshape(team_rows, width),
        norm_gain,
        qkv_weight,
        ids,
        table,
        qgain,
        kgain,
        output_weight,
        tokens,
        cotangent,
        row_live.astype(bf16),
        mlp_norm_gain.reshape(1, width),
        first,
        planes,
        2,
    )

    unit_weights = [first.reshape(width, -1)]
    team_two, act, grad_both, first_units, second = feed(
        normed_two, team_cot, unit_weights[0], down_weight, second, planes, 0
    )
    unit_weights.append(second.reshape(width, -1))
    acts, grads_both, grad_units = [act], [grad_both], [first_units]
    for k in range(1, parts):
        act, grad_both = feed_rest(team_two, team_cot, unit_weights[k], down_weight, k)
        acts.append(act)
        grads_both.append(grad_both)
    grad_normed_two, last_units = feed_back(team_two, grads_both, unit_weights, 4)
    grad_units = [sum_line(g) for g in (*grad_units, last_units)[:parts]]
    _, pull_two = jax.vjp(root_mean_square_norm, middle, mlp_norm_gain)
    middle_part, grad_mgain = pull_two(grad_normed_two)
    grad_middle = (cotangent * row_live.astype(bf16)).astype(f32) + middle_part
    team_grad, grad_down = gather_down(grad_middle.astype(bf16), team_cot, acts, 10)
    team_grad = team_grad.reshape(team_rows, width)
    grad_down = sum_line(grad_down)

    grad_qkv, grad_attention, grad_head_gains = attend_back(
        team_grad,
        output_weight,
        context_b,
        raw,
        turned,
        value_b,
        team_normed,
        ids,
        table,
        qgain,
        kgain,
        planes,
        6,
    )
    grad_attention = sum_line(grad_attention.reshape(-1, grad_attention.shape[2]))
    grad_normed, summed_out, grad_gate, grad_up = last_sums(
        grad_qkv.reshape(TEAM, token_count, -1),
        qkv_weight,
        acts,
        down_weight,
        [g.reshape(TEAM, rows, -1) for g in grad_units],
        planes,
        5,
    )
    grad_gate, grad_up = grad_gate.astype(f32), grad_up.astype(f32)
    _, pull_one = jax.vjp(root_mean_square_norm, inputs, norm_gain.reshape(width))
    input_part, grad_again = pull_one(grad_normed)
    grad_tokens = (grad_middle + input_part).astype(bf16)
    layer_out = (row_live * (middle + summed_out)).astype(bf16)

    def by_owner(vector):
        vector = vector.reshape(devices, -1)
        return jnp.pad(vector, ((0, 0), (0, 128 - vector.shape[1])))

    gains = jnp.stack(
        [by_owner(v) for v in (grad_again, grad_mgain, grad_head_gains[0], grad_head_gains[1])], axis=1
    )
    gains = jnp.pad(gains, ((0, 0), (0, 4), (0, 0)))
    gains = gains.reshape(planes, TEAM, 8, 128).transpose(1, 0, 2, 3)

    grad_attention, grad_gate, grad_up, layer_out, grad_tokens = lax.optimization_barrier(
        (grad_attention, grad_gate, grad_up, layer_out, grad_tokens)
    )
    grad_query, grad_key, grad_value_w, grad_output, gains = closing(
        grad_attention,
        gains,
        rows,
        (w_query.shape[1], key_weight.shape[1], value_weight.shape[1], width),
        planes,
        9,
    )
    attention_grads = tuple(
        g.astype(f32) for g in (grad_query, grad_key, grad_value_w, grad_output)
    )
    gains = (
        gains[0, : attn_gain.shape[0]],
        gains[2, : query_norm_gain.shape[0]],
        gains[3, : key_gain.shape[0]],
        gains[1, : mlp_gain.shape[0]],
    )
    grad_down, attention_grads, gains = lax.optimization_barrier(
        (grad_down, attention_grads, gains)
    )
    return (
        layer_out,
        grad_tokens,
        *attention_grads,
        *gains[:3],
        grad_gate,
        grad_up,
        grad_down.astype(f32),
        gains[3],
    )


def solution(mesh):
    by_rows, by_entry = P("fsdp", None), P("fsdp")
    return jax.shard_map(
        functools.partial(local, mesh.shape["fsdp"]),
        mesh=mesh,
        in_specs=(
            by_rows,
            by_rows,
            by_entry,
            by_rows,
            by_rows,
            by_rows,
            by_rows,
            by_rows,
            by_entry,
            by_entry,
            by_entry,
            by_rows,
            by_rows,
            by_rows,
            by_entry,
        ),
        out_specs=(
            by_rows,
            by_rows,
            by_rows,
            by_rows,
            by_rows,
            by_rows,
            by_entry,
            by_entry,
            by_entry,
            by_rows,
            by_rows,
            by_rows,
            by_entry,
        ),
        check_vma=False,
    )
```

```python
import functools

import jax
import jax.numpy as jnp
import numpy as np
from jax import lax
from jax.experimental import pallas as pl
from jax.experimental.pallas import tpu as pltpu
from jax.sharding import PartitionSpec as P

QUERY_HEADS = 16
KEY_VALUE_HEADS = 8
HEAD_SIZE = 128
TEAM = 8
STEP = 256

epsilon = 1e-06
base_theta = 1000000.0
MESH = pl.DeviceIdType.MESH
LIMIT = 60 * 2**20
f32 = jnp.float32
bf16 = jnp.bfloat16


def root_mean_square_norm(values, gain):
    return values * lax.rsqrt(jnp.mean(values * values, axis=-1, keepdims=True) + epsilon) * gain


def rotation_tables(positions):
    half = HEAD_SIZE // 2
    powers = -np.arange(half, dtype=np.float32) * np.float32(2.0) / np.float32(HEAD_SIZE)
    freqs = np.power(np.float32(base_theta), powers).astype(np.float32)
    angles = np.arange(positions, dtype=np.float32)[:, None] * freqs
    cosine, sine = np.cos(angles), np.sin(angles)
    rest = np.concatenate([cosine, cosine, -sine, sine], axis=1).astype(np.float32)
    parts = []
    for _ in range(3):
        parts.append(rest.astype(jnp.bfloat16))
        rest = rest - parts[-1].astype(np.float32)
    return np.concatenate(parts, axis=1)


def dot_last(left, right):
    return lax.dot_general(
        left, right, (((1,), (1,)), ((), ())), preferred_element_type=jnp.float32
    )


def dot_first(left, right):
    return lax.dot_general(
        left, right, (((0,), (0,)), ((), ())), preferred_element_type=jnp.float32
    )


def simple_product(left, right):
    return jnp.dot(left, right, preferred_element_type=jnp.float32)


def flipped(index, mask):
    for bit in (1, 2, 4):
        if mask & bit:
            index = index + bit * (1 - 2 * lax.rem(lax.div(index, bit), 2))
    return index


def greet(me, masks, others=()):
    barrier = pltpu.get_barrier_semaphore()
    for device in (*(flipped(me, mask) for mask in masks), *others):
        pl.semaphore_signal(barrier, inc=1, device_id=(device,), device_id_type=MESH)
    pl.semaphore_wait(barrier, len(masks) + len(others))


def remote(source, target, send, receive, device):
    return pltpu.make_async_remote_copy(
        src_ref=source,
        dst_ref=target,
        send_sem=send,
        recv_sem=receive,
        device_id=(device,),
        device_id_type=MESH,
    )


def params(collective, limit=None):
    if limit is None:
        return pltpu.CompilerParams(collective_id=collective, has_side_effects=True)
    return pltpu.CompilerParams(
        collective_id=collective, has_side_effects=True, vmem_limit_bytes=limit
    )


class Gather:
    def __init__(self, begin, x, o, me):
        self.begin, self.x, self.o, self.me = begin, x, o, me
        self.place = lax.rem(me, TEAM)
        self.half = x.shape[0] // 2

    def part(self, ref, which):
        return ref.at[pl.ds(which * self.half, self.half)]

    def first(self, which, mask):
        target = self.part(self.o.at[self.place], which)
        return self.begin(self.part(self.x, which), target, flipped(self.me, mask))

    def relay(self, origin, which, mask):
        ref = self.part(self.o.at[flipped(self.place, origin)], which)
        return self.begin(ref, ref, flipped(self.me, mask))

    def start(self):
        self.x0, self.y1 = self.first(0, 2), self.first(1, 4)
        self.x1, self.y0 = self.first(1, 2), self.first(0, 4)
        self.late = [self.first(0, 1), self.first(1, 1)]

    def forward(self):
        self.x0.wait_recv()
        self.d0 = self.relay(2, 0, 4)
        self.y1.wait_recv()
        self.d1 = self.relay(4, 1, 2)
        self.late += [self.relay(2, 0, 1), self.relay(4, 1, 1)]

    def across(self):
        self.x1.wait_recv()
        self.late.append(self.relay(2, 1, 1))
        self.y0.wait_recv()
        self.late.append(self.relay(4, 0, 1))

    def diagonal(self):
        self.d0.wait_recv()
        self.late.append(self.relay(6, 0, 1))
        self.d1.wait_recv()
        self.late.append(self.relay(6, 1, 1))

    def arrive(self):
        for copy in self.late:
            copy.wait_recv()


class Sender:
    def __init__(self, send, receive):
        self.send, self.receive, self.count, self.started = send, receive, 0, []

    def take(self):
        self.count += 1
        return self.count - 1

    def __call__(self, source, target, device):
        k = self.take()
        copy = remote(source, target, self.send.at[k], self.receive.at[k], device)
        copy.start()
        self.started.append(copy)
        return copy

    def finish(self):
        for copy in self.started:
            copy.wait_send()


class Line:
    def __init__(self, sender, ref, planes, me):
        self.sender, self.ref, self.planes = sender, ref, planes
        self.plane, self.place = lax.div(me, TEAM), lax.rem(me, TEAM)
        self.flows = [(sign, [sender.take() for _ in range(planes - 1)]) for sign in (1, -1)]

    def passing(self, step, sign, ks, source):
        block = jnp.clip(source, 0, self.planes - 1)
        beyond = jnp.clip(self.plane + sign, 0, self.planes - 1) * TEAM + self.place
        ref, k = self.ref.at[block], ks[step]
        return remote(ref, ref, self.sender.send.at[k], self.sender.receive.at[k], beyond)

    def goes(self, step, sign):
        source, onward = self.plane - sign * step, self.plane + sign
        last = self.planes - 1
        return (source >= 0) & (source <= last) & (onward >= 0) & (onward <= last)

    def start(self, step):
        for sign, ks in self.flows:
            going = self.passing(step, sign, ks, self.plane - sign * step)
            pl.when(self.goes(step, sign))(going.start)

    def arrive(self, step):
        for sign, ks in self.flows:
            source = self.plane - sign * (step + 1)
            coming = self.passing(step, sign, ks, source)
            pl.when((source >= 0) & (source <= self.planes - 1))(coming.wait_recv)

    def sent(self, step):
        for sign, ks in self.flows:
            going = self.passing(step, sign, ks, self.plane - sign * step)
            pl.when(self.goes(step, sign))(going.wait_send)

    def through(self, first, last):
        for step in range(first, last):
            self.arrive(step)
            if step + 1 < last:
                self.start(step + 1)
        for step in range(first, last):
            self.sent(step)


def line_peers(me, planes):
    return [lax.rem(me + TEAM * k, planes * TEAM) for k in range(1, planes)]


TILE = 512
STRIP = 16


class TeamSum:
    def __init__(self, sender, me, out, buffers, lefts, rights, turned):
        self.sender, self.me, self.out = sender, me, out
        self.mix, self.from_core, self.from_x, self.from_y = buffers
        self.lefts, self.rights, self.turned = lefts, rights, turned
        place = lax.rem(me, TEAM)
        self.core = lax.rem(place, 2)
        self.rows, self.width = out.shape
        self.half = self.rows // 2
        self.chips = [lax.div(flipped(place, mask), 2) for mask in (6, 2, 4, 0)]
        self.across = []

    def product(self, j):
        @pl.loop(0, self.width // TILE)
        def _(t):
            at = pl.ds(pl.multiple_of(t * TILE, TILE), TILE)
            value = 0.0
            for left, right in zip(self.lefts, self.rights):
                if len(left.shape) == 2:
                    first = pl.multiple_of(self.chips[j] * 2 * self.rows, 2 * self.rows)
                    both = left[pl.ds(first, 2 * self.rows), :]
                else:
                    both = left[pl.ds(2 * self.chips[j], 2)].reshape(2 * self.rows, left.shape[2])
                if self.turned:
                    value = value + dot_last(both, right[at, :])
                else:
                    value = value + simple_product(both, right[:, at])
            self.mix[j, :, :, at] = value.astype(bf16).reshape(2, self.rows, TILE)

        self.across.append(
            self.sender(self.mix.at[j, 1 - self.core], self.from_core.at[j], flipped(self.me, 1))
        )

    def combine(self, j):
        self.across[j].wait_recv()

        @pl.loop(0, self.rows // STRIP)
        def _(i):
            at = pl.ds(i * STRIP, STRIP)
            self.mix[j, self.core, at, :] = (
                self.mix[j, self.core, at, :].astype(f32) + self.from_core[j, at, :].astype(f32)
            ).astype(bf16)

    def begin(self, j, which, ref, slot, mask):
        source = self.mix.at[j, self.core, pl.ds(which * self.half, self.half)]
        return self.sender(source, ref.at[slot], flipped(self.me, mask))

    def add_relayed(self, j, which, ref):
        @pl.loop(0, self.half // STRIP)
        def _(i):
            at = pl.ds(which * self.half + i * STRIP, STRIP)
            self.mix[j, self.core, at, :] = (
                self.mix[j, self.core, at, :].astype(f32)
                + ref[0, pl.ds(i * STRIP, STRIP), :].astype(f32)
            ).astype(bf16)

    def start(self):
        self.product(0)
        self.product(1)
        self.combine(0)
        self.d_x = self.begin(0, 0, self.from_x, 0, 2)
        self.d_y = self.begin(0, 1, self.from_y, 0, 4)
        self.product(2)
        self.combine(1)
        self.x_0 = self.begin(1, 0, self.from_x, 1, 2)
        self.combine(2)
        self.y_1 = self.begin(2, 1, self.from_y, 1, 4)

    def own(self):
        self.product(3)

    def relay(self):
        self.d_x.wait_recv()
        self.add_relayed(2, 0, self.from_x)
        self.y_0 = self.begin(2, 0, self.from_y, 2, 4)
        self.d_y.wait_recv()
        self.add_relayed(1, 1, self.from_y)
        self.x_1 = self.begin(1, 1, self.from_x, 2, 2)

    def gather_half(self, which, slot_x, slot_y):
        @pl.loop(0, self.half // STRIP)
        def _(i):
            at = pl.ds(which * self.half + i * STRIP, STRIP)
            here = pl.ds(i * STRIP, STRIP)
            self.out[at, :] = (
                self.mix[3, self.core, at, :].astype(f32) + self.from_core[3, at, :].astype(f32)
            ) + (
                self.from_x[slot_x, here, :].astype(f32) + self.from_y[slot_y, here, :].astype(f32)
            )

    def finish(self):
        self.across[3].wait_recv()
        self.x_0.wait_recv()
        self.y_0.wait_recv()
        self.gather_half(0, 1, 2)
        self.y_1.wait_recv()
        self.x_1.wait_recv()
        self.gather_half(1, 2, 1)


SUM_COPIES = 10


def sum_buffers(rows, width):
    return [
        pltpu.VMEM((4, 2, rows, width), bf16),
        pltpu.VMEM((4, rows, width), bf16),
        pltpu.VMEM((3, rows // 2, width), bf16),
        pltpu.VMEM((3, rows // 2, width), bf16),
    ]


class Loader:
    def __init__(self, sems):
        self.sems, self.copies = sems, []

    def __call__(self, source, target):
        copy = pltpu.make_async_copy(source, target, self.sems.at[len(self.copies)])
        copy.start()
        self.copies.append(copy)
        return copy

    def wait(self):
        for copy in self.copies:
            copy.wait()


def rows_of(ref, k, rows):
    return ref.at[pl.ds(k * rows, rows)]


def turned_product(left, right, out, part, parts):
    blocks, rows, units = left.shape
    width = right.shape[2]
    tiles = width // TILE
    flat = left[...].reshape(blocks * rows, units)

    @pl.loop(part * tiles // parts, (part + 1) * tiles // parts)
    def _(t):
        at = pl.ds(pl.multiple_of(t * TILE, TILE), TILE)
        value = dot_first(flat, right[:, :, at].reshape(blocks * rows, TILE))
        out[:, at] = value.astype(bf16)


def turned_rows(left, right, out, part, parts):
    blocks, rows, width = left.shape
    tiles = width // TILE
    flat = right[...].reshape(blocks * rows, right.shape[2])

    @pl.loop(part * tiles // parts, (part + 1) * tiles // parts)
    def _(t):
        at = pl.ds(pl.multiple_of(t * TILE, TILE), TILE)
        value = dot_first(left[:, :, at].reshape(blocks * rows, TILE), flat)
        out[at, :] = value.astype(bf16)


def feed_back_kernel(parts, two, *refs):
    grads, weights, refs = refs[:parts], refs[parts : 2 * parts], refs[2 * parts :]
    out, weight_out, buffers, refs = refs[0], refs[1], refs[2:6], refs[6:]
    grads_here, weights_here = refs[:parts], refs[parts : 2 * parts]
    two_here, send, receive, own = refs[2 * parts :]
    me = lax.axis_index("fsdp")
    loader = Loader(own)
    for source, target in zip((*grads, *weights), (*grads_here, *weights_here)):
        loader(source, target)
    greet(me, (1, 2, 4))
    loader.wait()
    loader(two, two_here)
    sender = Sender(send, receive)
    total = TeamSum(sender, me, out, buffers, grads_here, weights_here, True)
    total.start()
    loader.copies[-1].wait()
    total.relay()
    total.own()
    turned_rows(two_here, grads_here[-1], weight_out, 0, 1)
    total.finish()
    sender.finish()


def feed_back(two, grads, weights, collective):
    _, rows, width = two.shape
    parts, units = len(grads), grads[0].shape[2]
    anywhere = pl.BlockSpec(memory_space=pl.ANY)
    vmem = pl.BlockSpec(memory_space=pltpu.VMEM)
    like = jax.ShapeDtypeStruct
    return pl.pallas_call(
        functools.partial(feed_back_kernel, parts),
        out_shape=(like((rows, width), f32), like((width, units), bf16)),
        in_specs=[anywhere] * (1 + 2 * parts),
        out_specs=(vmem, vmem),
        scratch_shapes=[
            *sum_buffers(rows, width),
            *(pltpu.VMEM(x.shape, bf16) for x in (*grads, *weights, two)),
            pltpu.SemaphoreType.DMA((SUM_COPIES,)),
            pltpu.SemaphoreType.DMA((SUM_COPIES,)),
            pltpu.SemaphoreType.DMA((2 * parts + 1,)),
        ],
        compiler_params=params(collective, LIMIT),
        cost_estimate=pl.CostEstimate(
            flops=2 * TEAM * rows * units * width * (parts + 1),
            bytes_accessed=2 * TEAM * rows * (units * parts + width),
            transcendentals=0,
        ),
    )(two, *grads, *weights)


def gather_down_kernel(parts, x, cot, *refs):
    acts, refs = refs[:parts], refs[parts:]
    o_ref, down_out, refs = refs[0], refs[1], refs[2:]
    acts_here, (cot_here, send, receive, own) = refs[:parts], refs[parts:]
    me = lax.axis_index("fsdp")
    loader = Loader(own)
    loader(x, o_ref.at[lax.rem(me, TEAM)])
    loader(cot, cot_here)
    for source, target in zip(acts, acts_here):
        loader(source, target)
    greet(me, (1, 2, 4))
    sender = Sender(send, receive)
    moves = Gather(sender, x, o_ref, me)
    units = acts_here[0].shape[2]

    def work(k):
        turned_product(
            acts_here[k // 2], cot_here, rows_of(down_out, k // 2, units), k % 2, 2
        )

    moves.start()
    loader.wait()
    work(0)
    moves.forward()
    work(1)
    moves.across()
    if parts > 1:
        work(2)
    moves.diagonal()
    if parts > 1:
        work(3)
    moves.arrive()
    sender.finish()


def gather_down(x, cot, acts, collective):
    rows, width = x.shape
    parts, units = len(acts), acts[0].shape[2]
    anywhere = pl.BlockSpec(memory_space=pl.ANY)
    vmem = pl.BlockSpec(memory_space=pltpu.VMEM)
    like = jax.ShapeDtypeStruct
    return pl.pallas_call(
        functools.partial(gather_down_kernel, parts),
        out_shape=(like((TEAM, rows, width), x.dtype), like((parts * units, width), bf16)),
        in_specs=[vmem, anywhere] + [anywhere] * parts,
        out_specs=(anywhere, vmem),
        scratch_shapes=[
            *(pltpu.VMEM(a.shape, bf16) for a in acts),
            pltpu.VMEM(cot.shape, bf16),
            pltpu.SemaphoreType.DMA((14,)),
            pltpu.SemaphoreType.DMA((14,)),
            pltpu.SemaphoreType.DMA((2 + parts,)),
        ],
        compiler_params=params(collective, LIMIT),
        cost_estimate=pl.CostEstimate(
            flops=2 * TEAM * rows * width * units * parts,
            bytes_accessed=6 * TEAM * rows * width,
            transcendentals=0,
        ),
    )(x, cot, *acts)


def last_sums_kernel(planes, parts, grad_qkv, qkv_weight, down, out_blocks, before, *refs):
    acts, units, refs = refs[:parts], refs[parts : 2 * parts], refs[2 * parts :]
    grad_normed, layer, gate, up, output, after, *refs = refs
    first, second, refs = refs[:4], refs[4:8], refs[8:]
    acts_here, downs_here, refs = refs[:parts], refs[parts : 2 * parts], refs[2 * parts :]
    grad_here, weight_here, landed, mine, there, sems, out_sum, send, receive, own = refs
    me = lax.axis_index("fsdp")
    place = lax.rem(me, TEAM)
    loader = Loader(own)
    loader(grad_qkv, grad_here)
    loader(qkv_weight, weight_here)
    for k in range(parts):
        loader(units[k].at[place], landed.at[k, place])
        loader(acts[k], acts_here[k])
        loader(rows_of(down, k, downs_here[k].shape[0]), downs_here[k])
    greet(me, range(1, TEAM), line_peers(me, planes))
    sender = Sender(send, receive)
    line = LineSum(sender, out_blocks, before.at[0], after, mine, there, sems, planes, me, 1)
    line.start(0)
    moves = [
        sender(units[k].at[flipped(place, m)], landed.at[k, place], flipped(me, m))
        for k in range(parts)
        for m in SWAP_ORDER
    ]
    loader.wait()
    one = TeamSum(sender, me, grad_normed, first, [grad_here], [weight_here], True)
    two = TeamSum(sender, me, layer, second, acts_here, downs_here, False)
    one.start()
    one.own()
    two.start()
    one.relay()
    two.own()
    line.wait(0)
    if planes > 3:
        line.start(1)
    two.relay()
    for copy in moves:
        copy.wait_recv()
    block = gate.shape[1] // (planes * TEAM)
    some = planes // parts
    span = TEAM * block
    for j, ref in enumerate((gate, up)):
        for g in range(planes):
            at = (j * some + g % some) * block
            ref[:, g * span : (g + 1) * span] = jnp.concatenate(
                [landed[g // some, q, :, at : at + block] for q in range(TEAM)], axis=1
            )
    one.finish()
    two.finish()
    for k in range(1, planes - 2):
        if k > 1:
            line.start(k)
        line.wait(k)
    line.total(out_sum)
    width, rows = out_sum.shape[1], output.shape[0]
    for c in range(output.shape[1] // width):
        output[:, c * width : (c + 1) * width] = out_sum[c * rows : (c + 1) * rows]
    sender.finish()


def last_sums(grad_qkv, qkv_weight, acts, down, units, out_blocks, before, planes, collective):
    _, rows, depth = grad_qkv.shape
    width = qkv_weight.shape[0]
    parts = len(acts)
    anywhere = pl.BlockSpec(memory_space=pl.ANY)
    vmem = pl.BlockSpec(memory_space=pltpu.VMEM)
    like = jax.ShapeDtypeStruct
    _, own_rows, some = units[0].shape
    steps = planes - 2
    links = 2 * SUM_COPIES + (TEAM - 1) * parts + 2 * steps
    _, block, block_width = out_blocks.shape
    home = like((own_rows, TEAM * parts * some // 2), bf16)
    return pl.pallas_call(
        functools.partial(last_sums_kernel, planes, parts),
        out_shape=(like((rows, width), f32),) * 2
        + (home,) * 2
        + (like((own_rows, width), f32), like((steps, 2, block, block_width), bf16),),
        in_specs=[anywhere] * (5 + 2 * parts),
        out_specs=(vmem,) * 5 + (anywhere,),
        scratch_shapes=[
            *sum_buffers(rows, width),
            *sum_buffers(rows, width),
            *(pltpu.VMEM(a.shape, bf16) for a in acts),
            *(pltpu.VMEM((a.shape[2], width), bf16) for a in acts),
            pltpu.VMEM(grad_qkv.shape, bf16),
            pltpu.VMEM(qkv_weight.shape, bf16),
            pltpu.VMEM((parts, *units[0].shape), bf16),
            *line_scratch(block, block_width),
            pltpu.VMEM((block, block_width), f32),
            pltpu.SemaphoreType.DMA((links,)),
            pltpu.SemaphoreType.DMA((links,)),
            pltpu.SemaphoreType.DMA((2 + 3 * parts,)),
        ],
        compiler_params=params(collective, LIMIT),
        cost_estimate=pl.CostEstimate(
            flops=2 * TEAM * rows * width * (depth + sum(a.shape[2] for a in acts)),
            bytes_accessed=4 * TEAM * rows * depth,
            transcendentals=0,
        ),
    )(grad_qkv, qkv_weight, down, out_blocks, before, *acts, *units)


class LineSum:
    def __init__(self, sender, own, before, after, mine, there, sems, planes, me, first):
        self.sender, self.own, self.before, self.after = sender, own, before, after
        self.mine, self.there, self.sems = mine, there, sems
        self.planes, self.me, self.first = planes, me, first
        self.plane = lax.div(me, TEAM)
        self.flows = [(sign, [sender.take() for _ in range(after.shape[0])]) for sign in (1, -1)]

    def rank(self, sign):
        return self.plane if sign > 0 else self.planes - 1 - self.plane

    def block(self, sign, step):
        rank = jnp.clip(self.planes - 1 - (step - self.rank(sign)), 0, self.planes - 1)
        return rank if sign > 0 else self.planes - 1 - rank

    def sends(self, sign, step):
        rank = self.rank(sign)
        return (rank <= step) & (rank < self.planes - 1)

    def comes(self, sign, step):
        rank = self.rank(sign)
        return (rank >= 1) & (rank - 1 <= step)

    def copy(self, sign, k):
        d = 0 if sign > 0 else 1
        beyond = jnp.clip(self.plane + sign, 0, self.planes - 1) * TEAM + lax.rem(self.me, TEAM)
        sem = dict((sign, ks[k]) for sign, ks in self.flows)[sign]
        target = self.after.at[k, d]
        send, receive = self.sender.send.at[sem], self.sender.receive.at[sem]
        return remote(self.mine.at[d], target, send, receive, beyond)

    def start(self, k):
        step = self.first + k
        for d, (sign, _) in enumerate(self.flows):

            @pl.when(self.sends(sign, step))
            def _():
                load = pltpu.make_async_copy(
                    self.own.at[self.block(sign, step)], self.mine.at[d], self.sems.at[0]
                )
                load.start()
                load.wait()
                if step > 0:

                    @pl.when(self.rank(sign) >= 1)
                    def _():
                        source = self.after.at[k - 1, d] if k else self.before.at[d]
                        load = pltpu.make_async_copy(source, self.there, self.sems.at[1])
                        load.start()
                        load.wait()
                        self.add(d)

                self.copy(sign, k).start()

    def add(self, d):
        @pl.loop(0, self.there.shape[0] // STRIP)
        def _(i):
            at = pl.ds(i * STRIP, STRIP)
            self.mine[d, at, :] = (
                self.mine[d, at, :].astype(f32) + self.there[at, :].astype(f32)
            ).astype(bf16)

    def wait(self, k):
        step = self.first + k
        for sign, _ in self.flows:
            copy = self.copy(sign, k)
            pl.when(self.sends(sign, step))(copy.wait_send)
            pl.when(self.comes(sign, step))(copy.wait_recv)

    def rest(self):
        for k in range(self.after.shape[0]):
            if k:
                self.start(k)
            self.wait(k)

    def total(self, out):
        load = pltpu.make_async_copy(self.own.at[self.plane], self.mine.at[0], self.sems.at[0])
        load.start()
        load.wait()

        @pl.loop(0, out.shape[0] // STRIP)
        def _(i):
            at = pl.ds(i * STRIP, STRIP)
            out[at, :] = self.mine[0, at, :].astype(f32)

        for d, (sign, _) in enumerate(self.flows):

            @pl.when(self.rank(sign) >= 1)
            def _():
                load = pltpu.make_async_copy(
                    self.after.at[self.after.shape[0] - 1, d], self.there, self.sems.at[1]
                )
                load.start()
                load.wait()

                @pl.loop(0, out.shape[0] // STRIP)
                def _(i):
                    at = pl.ds(i * STRIP, STRIP)
                    out[at, :] = out[at, :] + self.there[at, :].astype(f32)


def line_scratch(rows, width):
    return [
        pltpu.VMEM((2, rows, width), bf16),
        pltpu.VMEM((rows, width), bf16),
        pltpu.SemaphoreType.DMA((2,)),
    ]


SWAP_ORDER = (6, 7, 2, 3, 4, 5, 1)


def open_kernel(
    planes, parts, query_in, key_in, value_in, output_in, tokens_in, gate_in, up_in, down_in, *refs
):
    smalls, refs = refs[:5], refs[5:]
    gate_up, refs = refs[:parts], refs[parts:]
    qkv, output_raw, output, tokens, down, *gain_refs, numbers = refs[:10]
    small_in, small, sorted_units, send, receive, own = refs[10:]
    slots, sequence = smalls[4].shape
    small_in[...] = jnp.zeros_like(small_in)
    for k, ref in enumerate(smalls):
        small_in[k : k + ref.shape[0], : ref.shape[1]] = ref[...].astype(f32)
    me = lax.axis_index("fsdp")
    place = lax.rem(me, TEAM)
    plane = lax.div(me, TEAM)
    team = me - place
    others = [lax.rem(me + TEAM * k, planes * TEAM) for k in range(1, planes)]
    sender = Sender(send, receive)
    keeps = []

    def keep(source, target):
        copy = pltpu.make_async_copy(source, target, own.at[len(keeps)])
        copy.start()
        keeps.append(copy)

    qkv_parts, at = [], 0
    for ref in (query_in, key_in, value_in):
        part = ref.shape[1] // TEAM
        qkv_parts.append((ref, part, qkv.at[plane, place, :, pl.ds(at, part)]))
        at += part

    def columns(ref, part, target):
        return ref.at[:, pl.ds(pl.multiple_of(target * part, part), part)]

    for ref, part, target in qkv_parts:
        keep(columns(ref, part, place), target)
    keep(small_in, small.at[me])
    keep(tokens_in, tokens.at[place])
    keep(down_in, down.at[plane])
    keep(output_in, output_raw.at[plane])
    greet(me, range(1, TEAM), others)

    qkv_line = Line(sender, qkv, planes, me)
    out_line = Line(sender, output_raw, planes, me)
    down_line = Line(sender, down, planes, me)
    rows_tokens = Gather(sender, tokens_in, tokens, me)
    spread_send = [sender.take() for _ in range(planes)]
    spread_own = len(keeps)

    def outgoing(k):
        number = TEAM * k + place
        partner, there = lax.div(number, planes), lax.rem(number, planes)
        s, r = send.at[spread_send[0] + k], receive.at[spread_send[0] + there]
        over = remote(output_raw.at[k], output.at[there], s, r, team + partner)
        here = pltpu.make_async_copy(output_raw.at[k], output.at[there], own.at[spread_own + k])
        return partner, over, here

    def incoming(k):
        partner = lax.rem(planes * place + k, TEAM)
        s, r = send.at[spread_send[k]], receive.at[spread_send[k]]
        return partner, remote(output_raw.at[k], output.at[k], s, r, team + partner)

    def spread_one(k, inside):
        partner, over, here = outgoing(jnp.clip(k, 0, planes - 1))
        pl.when(inside & (partner != place))(over.start)
        pl.when(inside & (partner == place))(here.start)

    def step_out(step):
        out_line.arrive(step)
        if step < planes - 2:
            out_line.start(step + 1)
        spread_one(plane - step - 1, plane - step - 1 >= 0)
        spread_one(plane + step + 1, plane + step + 1 <= planes - 1)

    swaps = [
        sender(columns(ref, part, flipped(place, m)), target, flipped(me, m))
        for m in SWAP_ORDER
        for ref, part, target in qkv_parts
    ]
    near = [sender(small_in, small.at[me], flipped(me, m)) for m in SWAP_ORDER]
    keeps[-1].wait()
    out_line.start(0)
    keeps[-2].wait()
    down_line.start(0)
    block = gate_in.shape[1] // (planes * TEAM)
    some = planes // parts
    units = some * block
    for k in range(parts):
        for q in range(TEAM):
            for j, ref in enumerate((gate_in, up_in)):
                starts = [(TEAM * g + q) * block for g in range(k * some, (k + 1) * some)]
                sorted_units[k, q, :, j * units : (j + 1) * units] = jnp.concatenate(
                    [ref[:, at : at + block] for at in starts], axis=1
                )
    for copy in swaps:
        copy.wait_recv()
    for copy in keeps[:3]:
        copy.wait()
    qkv_line.start(0)
    rows_tokens.start()
    moves = [
        sender(sorted_units.at[k, flipped(place, m)], gate_up[k].at[plane, place], flipped(me, m))
        for k in range(parts)
        for m in SWAP_ORDER
    ]
    kept_units = [
        pltpu.make_async_copy(
            sorted_units.at[k, place], gate_up[k].at[plane, place], own.at[spread_own + planes + k]
        )
        for k in range(parts)
    ]
    for copy in kept_units:
        copy.start()
    spread_one(plane, True)
    rows_tokens.forward()
    step_out(0)
    for copy in near:
        copy.wait_recv()
    keeps[3].wait()
    shared = small.at[pl.ds(team, TEAM)]
    far = [sender(shared, shared, other) for other in others]
    rows_tokens.across()
    for step in range(planes - 1):
        qkv_line.arrive(step)
        if step < planes - 2:
            qkv_line.start(step + 1)
            step_out(step + 1)
        down_line.arrive(step)
        if step < planes - 2:
            down_line.start(step + 1)
        if step == 0:
            rows_tokens.diagonal()
        if step == 1:
            for copy in far:
                copy.wait_recv()
            for k, ref in enumerate(gain_refs):
                part = smalls[k].shape[1]
                ref[...] = jnp.concatenate(
                    [small[i, k : k + 1, :part] for i in range(planes * TEAM)], axis=1
                )
            per_step = STEP // sequence
            for i in range(numbers.shape[0]):
                pieces = []
                for m in range(i * per_step, (i + 1) * per_step):
                    row = 4 + m % slots
                    pieces.append(small[team + m // slots, row : row + 1, :sequence] + 64.0 * m)
                numbers[i] = jnp.concatenate(pieces, axis=1)
    rows_tokens.arrive()
    for copy in moves:
        copy.wait_recv()
    for copy in kept_units:
        copy.wait()
    for k in range(planes):
        partner, over, here = outgoing(k)
        pl.when(partner != place)(over.wait_send)
        pl.when(partner == place)(here.wait)
        partner, arriving = incoming(k)
        pl.when(partner != place)(arriving.wait_recv)
    for step in range(planes - 1):
        qkv_line.sent(step)
        out_line.sent(step)
        down_line.sent(step)
    sender.finish()
    for copy in keeps[4:-2]:
        copy.wait()


def opening(query, key, value, output, tokens, gate, up, down, smalls, planes, parts, collective):
    links = 28 + 6 * (planes - 1) + 14 + planes - 1 + planes + parts * (TEAM - 1)
    anywhere = pl.BlockSpec(memory_space=pl.ANY)
    vmem = pl.BlockSpec(memory_space=pltpu.VMEM)
    like = jax.ShapeDtypeStruct
    rows = query.shape[0]
    width = (query.shape[1] + key.shape[1] + value.shape[1]) // TEAM
    units = (TEAM, rows, 2 * gate.shape[1] // TEAM // parts)
    devices = planes * TEAM
    return pl.pallas_call(
        functools.partial(open_kernel, planes, parts),
        out_shape=(
            *((like((planes, *units), bf16),) * parts),
            like((planes, TEAM, rows, width), bf16),
            like((planes, *output.shape), bf16),
            like((planes, *output.shape), bf16),
            like((TEAM, *tokens.shape), bf16),
            like((planes, *down.shape), bf16),
            *(like((1, devices * x.shape[1]), f32) for x in smalls[:4]),
            like((TEAM * tokens.shape[0] // STEP, 1, STEP), f32),
        ),
        in_specs=[vmem] * 13,
        out_specs=(anywhere,) * (5 + parts) + (vmem,) * 5,
        scratch_shapes=[
            pltpu.VMEM((8, 128), f32),
            pltpu.VMEM((devices, 8, 128), f32),
            pltpu.VMEM((parts, *units), bf16),
            pltpu.SemaphoreType.DMA((links,)),
            pltpu.SemaphoreType.DMA((links,)),
            pltpu.SemaphoreType.DMA((7 + planes + parts,)),
        ],
        compiler_params=params(collective, LIMIT),
    )(query, key, value, output, tokens, gate, up, down, *smalls)


def close_kernel(planes, x_ref, gains, *refs):
    query_ref, key_ref, value_ref, gain_ref, *refs = refs
    landed, near_in, mid, far_in, send, receive, own = refs
    me = lax.axis_index("fsdp")
    place = lax.rem(me, TEAM)
    plane = lax.div(me, TEAM)
    others = [lax.rem(me + TEAM * k, planes * TEAM) for k in range(1, planes)]
    rows = landed.shape[1]

    def part(target):
        return x_ref.at[pl.ds(pl.multiple_of(target * rows, rows), rows)]

    keep = pltpu.make_async_copy(part(place), landed.at[place], own.at[0])
    keep.start()
    greet(me, range(1, TEAM), others)
    sender = Sender(send, receive)
    near = [
        sender(gains.at[flipped(place, m)], near_in.at[m - 1], flipped(me, m)) for m in SWAP_ORDER
    ]
    moves = [
        sender(part(flipped(place, m)), landed.at[place], flipped(me, m)) for m in SWAP_ORDER
    ]
    for copy in near:
        copy.wait_recv()
    summed = gains[place]
    for mask in range(1, TEAM):
        summed = summed + near_in[mask - 1]
    mid[...] = summed
    far = [
        sender(mid.at[lax.rem(plane + k + 1, planes)], far_in.at[k], other)
        for k, other in enumerate(others)
    ]
    for copy in moves:
        copy.wait_recv()
    keep.wait()
    at = 0
    for ref in (query_ref, key_ref, value_ref):
        part_width = ref.shape[1] // TEAM
        for q in range(TEAM):
            ref[:, q * part_width : (q + 1) * part_width] = landed[q, :, at : at + part_width]
        at += part_width
    for copy in far:
        copy.wait_recv()
    result = mid[plane]
    for k in range(planes - 1):
        result = result + far_in[k]
    gain_ref[...] = result
    sender.finish()


def closing(x, gains, rows, widths, planes, collective):
    links = 2 * (TEAM - 1) + planes - 1
    block = gains.shape[2:]
    vmem = pl.BlockSpec(memory_space=pltpu.VMEM)
    like = jax.ShapeDtypeStruct
    return pl.pallas_call(
        functools.partial(close_kernel, planes),
        out_shape=(*(like((rows, w), bf16) for w in widths), like(block, f32)),
        in_specs=[pl.BlockSpec(memory_space=pl.ANY), vmem],
        out_specs=(vmem,) * 4,
        scratch_shapes=[
            pltpu.VMEM((TEAM, rows, x.shape[1]), x.dtype),
            pltpu.VMEM((TEAM - 1, planes, *block), f32),
            pltpu.VMEM((planes, *block), f32),
            pltpu.VMEM((planes - 1, *block), f32),
            pltpu.SemaphoreType.DMA((links,)),
            pltpu.SemaphoreType.DMA((links,)),
            pltpu.SemaphoreType.DMA((2,)),
        ],
        compiler_params=params(collective, LIMIT),
    )(x, gains)


def visible_and_tables(ids_row, table):
    rows = ids_row.shape[1]
    row_at = lax.broadcasted_iota(jnp.int32, (rows, rows), 0)
    column_at = lax.broadcasted_iota(jnp.int32, (rows, rows), 1)
    ids_column = jnp.sum(jnp.where(row_at == column_at, ids_row, 0.0), axis=1, keepdims=True)
    visible = (ids_column == ids_row) & (column_at <= row_at)
    sequence = table.shape[0]
    place = jnp.sum(visible.astype(f32), axis=1, keepdims=True) - 1.0
    at = lax.broadcasted_iota(jnp.int32, (rows, sequence), 1).astype(f32)
    chosen = (at == place).astype(bf16)
    both = simple_product(chosen, table)
    width = 2 * HEAD_SIZE
    both = (both[:, :width] + both[:, width : 2 * width]) + both[:, 2 * width :]
    return visible, both[:, :HEAD_SIZE], both[:, HEAD_SIZE:]


def softmax(query, key, visible):
    scores = dot_last(query, key) * HEAD_SIZE ** (-0.5)
    scores = jnp.where(visible, scores, -1e30)
    expos = jnp.exp(scores - jnp.max(scores, axis=1, keepdims=True))
    return expos / jnp.sum(expos, axis=1, keepdims=True)


def by_step(*shape):
    return pl.BlockSpec(shape, lambda i: (i, *(0 for _ in shape[1:])))


def fixed(*shape):
    return pl.BlockSpec(shape, lambda i: tuple(0 for _ in shape))


def attend_kernel(
    planes, x_in, gain, weight, ids_row, table, query_gain, key_gain, right_in, tokens, cot_in, live,
    mlp_gain, _, normed_out, raw_out, turned_out, value_out, context_out, out, two, cot, units,
    x_ref, normed_ref, raw_ref, turned_ref, value_ref, context_ref, cot_own,
    mix, from_core, from_x, from_y, right, send, receive, own,
):
    me = lax.axis_index("fsdp")
    loader = Loader(own)
    steps = x_ref.shape[0] // STEP
    for i in range(steps):
        loader(rows_of(x_in, i, STEP), rows_of(x_ref, i, STEP))
    load_right = loader(right_in, right)
    cot_own[...] = cot_in[...] * live[...]
    keep = loader(cot_own, cot.at[lax.rem(me, TEAM)])
    greet(me, (1, 2, 4), line_peers(me, planes))
    sender = Sender(send, receive)
    line = Line(sender, units, planes, me)
    rows_cot = Gather(sender, cot_own, cot, me)
    line.start(0)
    rows_cot.start()
    heads = context_ref.shape[1] // HEAD_SIZE
    homes = []

    def attention(i):
        loader.copies[i].wait()
        here = slice(i * STEP, (i + 1) * STEP)
        x = x_ref[here].astype(f32)
        scale = lax.rsqrt(jnp.mean(x * x, axis=1, keepdims=True) + epsilon)
        normed = (x * scale * gain[...]).astype(bf16)
        normed_ref[here] = normed
        projected = simple_product(normed, weight[...])
        visible, cosine, sine = visible_and_tables(ids_row[i], table[...])
        raw_ref[here] = projected[:, : (heads + 1) * HEAD_SIZE]
        value = projected[:, (heads + 1) * HEAD_SIZE :].astype(bf16)
        value_ref[here] = value
        turned = []
        for h in range(heads + 1):
            at = slice(h * HEAD_SIZE, (h + 1) * HEAD_SIZE)
            raw = projected[:, at]
            head_gain = query_gain if h < heads else key_gain
            scale = lax.rsqrt(jnp.mean(raw * raw, axis=1, keepdims=True) + epsilon)
            y = raw * scale * head_gain[...]
            y = y * cosine + pltpu.roll(y, HEAD_SIZE // 2, 1) * sine
            turned.append(y.astype(bf16))
            turned_ref[here, at] = turned[-1]
        for h in range(heads):
            probs = softmax(turned[h], turned[heads], visible).astype(bf16)
            context = simple_product(probs, value)
            context_ref[here, h * HEAD_SIZE : (h + 1) * HEAD_SIZE] = context.astype(bf16)
        for ref, home in (
            (normed_ref, normed_out), (raw_ref, raw_out), (turned_ref, turned_out),
            (value_ref, value_out), (context_ref, context_out),
        ):
            homes.append(loader(rows_of(ref, i, STEP), rows_of(home, i, STEP)))

    for i in range(steps):
        attention(i)
        if i == steps // 2 - 1:
            rows_cot.forward()
    rows_cot.across()
    line.arrive(0)
    if planes > 2:
        line.start(1)
    load_right.wait()
    buffers = [mix, from_core, from_x, from_y]
    total = TeamSum(sender, me, out, buffers, [context_ref], [right], False)
    total.start()
    rows_cot.diagonal()
    total.own()
    total.relay()
    if planes > 2:
        line.arrive(1)
    if planes > 3:
        line.start(2)
    total.finish()

    @pl.loop(0, out.shape[0] // STRIP)
    def _(i):
        at = pl.ds(i * STRIP, STRIP)
        middle = tokens[at, :].astype(f32) + out[at, :]
        out[at, :] = middle
        scale = lax.rsqrt(jnp.mean(middle * middle, axis=1, keepdims=True) + epsilon)
        two[at, :] = (middle * scale * mlp_gain[...]).astype(bf16)

    rows_cot.arrive()
    if planes > 3:
        line.through(2, planes - 1)
    for step in range(min(2, planes - 1)):
        line.sent(step)
    sender.finish()
    for copy in (keep, *homes):
        copy.wait()


def attend(
    x, gain, weight, ids, table, query_gain, key_gain, right, tokens, cot, live, mlp_gain, units,
    planes, collective,
):
    rows, width = x.shape
    out = weight.shape[1]
    heads = out - 2 * HEAD_SIZE
    own_rows = tokens.shape[0]
    steps = rows // STEP
    like = jax.ShapeDtypeStruct
    anywhere = pl.BlockSpec(memory_space=pl.ANY)
    vmem = pl.BlockSpec(memory_space=pltpu.VMEM)
    kept = (
        like((rows, width), bf16),
        like((rows, heads + HEAD_SIZE), f32),
        like((rows, heads + HEAD_SIZE), bf16),
        like((rows, HEAD_SIZE), bf16),
        like((rows, heads), bf16),
    )
    links = SUM_COPIES + 14 + 2 * (planes - 1)
    return pl.pallas_call(
        functools.partial(attend_kernel, planes),
        out_shape=(
            *kept,
            like((own_rows, width), f32),
            like((own_rows, width), bf16),
            like((TEAM, own_rows, width), bf16),
            like(units.shape, bf16),
        ),
        in_specs=[anywhere] + [vmem] * 6 + [anywhere] + [vmem] * 4 + [anywhere],
        out_specs=(*([anywhere] * 5), vmem, vmem, anywhere, anywhere),
        input_output_aliases={12: 8},
        scratch_shapes=[
            pltpu.VMEM((rows, width), bf16),
            *(pltpu.VMEM(x.shape, x.dtype) for x in kept),
            pltpu.VMEM((own_rows, width), bf16),
            *sum_buffers(own_rows, width),
            pltpu.VMEM(right.shape, bf16),
            pltpu.SemaphoreType.DMA((links,)),
            pltpu.SemaphoreType.DMA((links,)),
            pltpu.SemaphoreType.DMA((6 * steps + 2,)),
        ],
        compiler_params=params(collective, LIMIT),
        cost_estimate=pl.CostEstimate(
            flops=2 * rows * width * (out + heads),
            bytes_accessed=8 * rows * width,
            transcendentals=0,
        ),
    )(
        x, gain, weight, ids, table, query_gain, key_gain, right, tokens, cot, live, mlp_gain, units
    )


def attend_back_kernel(planes, grad_in, out_weight, context, raw_in, turned_in, value_in, normed_in,
    ids_row, table, query_gain, key_gain, grad_raw_ref, weight_out, merged, grad_gains_ref, after,
    mine, there, sems,
    grad_ref, raw_ref, turned_ref, value_ref, normed_ref, out_sum, weight_sum, send, receive, own,
):
    me = lax.axis_index("fsdp")
    place = lax.rem(me, TEAM)
    team = me - place
    loader = Loader(own)
    loader(grad_in, grad_ref)
    for source, target in (
        (raw_in, raw_ref), (turned_in, turned_ref), (value_in, value_ref), (normed_in, normed_ref)
    ):
        loader(source, target)
    greet(me, range(1, TEAM), line_peers(me, planes))
    loader.copies[0].wait()

    total, width = grad_ref.shape
    heads = context.shape[1] // HEAD_SIZE
    out = weight_sum.shape[1]
    rows, block = weight_sum.shape[0] // planes, out_sum.shape[0] // planes
    cuts = width // out

    def source(k, c):
        return out_sum.at[pl.ds(k * block, block), pl.ds(c * out, out)]

    def target(k, c):
        return merged.at[k, pl.ds(c * block, block)]

    def outgoing(k, c):
        number = planes * place + k
        partner, there = lax.rem(number, TEAM), lax.div(number, TEAM)
        s, r = send.at[k * cuts + c], receive.at[there * cuts + c]
        over = remote(source(k, c), target(there, c), s, r, team + partner)
        here = pltpu.make_async_copy(source(k, c), target(there, c), own.at[5 + k * cuts + c])
        return partner, over, here

    def incoming(k, c):
        partner = lax.div(TEAM * k + place, planes)
        s, r = send.at[k * cuts + c], receive.at[k * cuts + c]
        return partner, remote(source(k, c), target(k, c), s, r, team + partner)

    for c in range(cuts):
        at = slice(c * out, (c + 1) * out)
        out_sum[:, at] = dot_first(context[...], grad_ref[:, at]).astype(bf16)
        for k in range(planes):
            partner, over, here = outgoing(k, c)
            pl.when(partner != place)(over.start)
            pl.when(partner == place)(here.start)

    grad_gains_ref[...] = jnp.zeros_like(grad_gains_ref)
    for copy in loader.copies[1:]:
        copy.wait()

    @pl.loop(0, total // STEP)
    def _(i):
        here = pl.ds(pl.multiple_of(i * STEP, STEP), STEP)
        grad_context = dot_last(grad_ref[here, :], out_weight[...]).astype(bf16)
        visible, cosine, sine = visible_and_tables(ids_row[i], table[...])
        value = value_ref[here, :]
        key = turned_ref[here, heads * HEAD_SIZE :]
        grads = []
        grad_value = 0.0
        grad_key = 0.0
        for h in range(heads):
            at = slice(h * HEAD_SIZE, (h + 1) * HEAD_SIZE)
            query = turned_ref[here, at]
            probs = softmax(query, key, visible)
            grad_value = grad_value + dot_first(probs.astype(bf16), grad_context[:, at])
            grad_probs = dot_last(grad_context[:, at], value)
            inner = jnp.sum(probs * grad_probs, axis=1, keepdims=True)
            grad_scores = (probs * (grad_probs - inner)).astype(bf16)
            grads.append(simple_product(grad_scores, key) * HEAD_SIZE ** (-0.5))
            grad_key = grad_key + dot_first(grad_scores, query) * HEAD_SIZE ** (-0.5)
        grads.append(grad_key)
        parts = []
        for h in range(heads + 1):
            raw = raw_ref[here, h * HEAD_SIZE : (h + 1) * HEAD_SIZE]
            head_gain = query_gain[...] if h < heads else key_gain[...]
            scale = lax.rsqrt(jnp.mean(raw * raw, axis=1, keepdims=True) + epsilon)
            turned = grads[h] * cosine + pltpu.roll(grads[h] * sine, HEAD_SIZE // 2, 1)
            row = 0 if h < heads else 1
            grad_gains_ref[row : row + 1, :] += jnp.sum(turned * raw * scale, axis=0, keepdims=True)
            turned = turned * head_gain
            mean = jnp.mean(turned * raw, axis=1, keepdims=True)
            parts.append((turned * scale - raw * (scale * scale * scale * mean)).astype(bf16))
        parts.append(grad_value.astype(bf16))
        grad_raw_ref[here, :] = jnp.concatenate(parts, axis=1)

    for k in range(planes):
        for c in range(cuts):
            partner, over, here = outgoing(k, c)
            pl.when(partner != place)(over.wait_send)
            pl.when(partner == place)(here.wait)
            partner, arriving = incoming(k, c)
            pl.when(partner != place)(arriving.wait_recv)
    sender = Sender(send, receive)
    sender.count = planes * cuts
    line = LineSum(sender, merged, None, after, mine, there, sems, planes, me, 0)
    line.start(0)

    @pl.loop(0, planes)
    def _(g):
        at = pl.ds(pl.multiple_of(g * rows, rows), rows)
        weight_sum[at, :] = dot_first(normed_ref[:, at], grad_raw_ref[...]).astype(bf16)

    homes = []
    for g in range(planes):
        copy = pltpu.make_async_copy(
            weight_sum.at[pl.ds(g * rows, rows)],
            weight_out.at[g],
            own.at[5 + planes * cuts + g],
        )
        copy.start()
        homes.append(copy)
    line.wait(0)
    for copy in homes:
        copy.wait()


def attend_back(
    grad, out_weight, context, raw, turned, value, normed, ids, table, query_gain, key_gain,
    planes, collective,
):
    rows, width = grad.shape
    heads = context.shape[1]
    out = heads + 2 * HEAD_SIZE
    by_plane = (planes, width // planes, out)
    merged = (planes, heads * width // out // planes, out)
    copies = planes * (width // out)
    anywhere = pl.BlockSpec(memory_space=pl.ANY)
    vmem = pl.BlockSpec(memory_space=pltpu.VMEM)
    like = jax.ShapeDtypeStruct
    return pl.pallas_call(
        functools.partial(attend_back_kernel, planes),
        out_shape=(
            like((rows, out), bf16),
            like(by_plane, bf16),
            like(merged, bf16),
            like((8, HEAD_SIZE), f32),
            like((1, 2, *merged[1:]), bf16),
        ),
        in_specs=[anywhere, vmem, vmem] + [anywhere] * 4 + [vmem] * 4,
        out_specs=(vmem, anywhere, anywhere, vmem, anywhere),
        scratch_shapes=[
            *line_scratch(*merged[1:]),
            *(pltpu.VMEM(x.shape, x.dtype) for x in (grad, raw, turned, value, normed)),
            pltpu.VMEM((heads, width), bf16),
            pltpu.VMEM((width, out), bf16),
            pltpu.SemaphoreType.DMA((copies + 2,)),
            pltpu.SemaphoreType.DMA((copies + 2,)),
            pltpu.SemaphoreType.DMA((5 + copies + planes,)),
        ],
        compiler_params=params(collective, LIMIT),
        cost_estimate=pl.CostEstimate(
            flops=2 * rows * width * (out + 2 * heads),
            bytes_accessed=8 * rows * width,
            transcendentals=0,
        ),
    )(grad, out_weight, context, raw, turned, value, normed, ids, table, query_gain, key_gain)


def hidden(two, weight):
    return simple_product(two, weight)


def hidden_grads(both, cot, down):
    units = both.shape[1] // 2
    gate, up = both[:, :units], both[:, units:]
    grad_act = dot_last(cot, down)
    sigma = 1.0 / (1.0 + jnp.exp(-gate))
    silu_gate = gate * sigma
    act = (silu_gate * up).astype(bf16)
    grad_gate = (grad_act * up * (sigma * (1.0 + gate * (1.0 - sigma)))).astype(bf16)
    grad_up = (grad_act * silu_gate).astype(bf16)
    return act, grad_gate, grad_up


def feed_kernel(
    planes, two_in, cot_in, weight_in, down_in, _, two_out, act_out, grad_both_out,
    weight_out, units_ref, two, cot, weight, down, both, weight_sum, act, grad_both, grad_weight,
    send, receive, own,
):
    me = lax.axis_index("fsdp")
    place = lax.rem(me, TEAM)
    loader = Loader(own)
    loader(two_in, two.at[place])
    loader(cot_in, cot)
    loader(weight_in, weight)
    loader(rows_of(down_in, 0, down.shape[0]), down)
    greet(me, (1, 2, 4), line_peers(me, planes))
    sender = Sender(send, receive)
    rows_two = Gather(sender, two_in, two, me)
    line = Line(sender, units_ref, planes, me)
    rows_two.start()
    line.start(0)
    rows, units = act.shape[1:]
    width = two.shape[2]

    crossed = {0: (0, 1), 2: (2, 4), 4: (3, 5), 6: (6, 7)}

    def chip_of(mask):
        return pl.ds(2 * lax.div(flipped(place, mask), 2), 2)

    def work(mask):
        for k in crossed[mask]:
            rows_two.late[k].wait_recv()
        chip = chip_of(mask)
        loader(two.at[chip], two_out.at[chip])
        both[...] = simple_product(two[chip].reshape(2 * rows, width), weight[...])
        flat = cot[chip].reshape(2 * rows, width)
        a, grad_gate, grad_up = hidden_grads(both[...], flat, down[...])
        act[chip] = a.reshape(2, rows, units)
        loader(act.at[chip], act_out.at[chip])
        grads = jnp.concatenate([grad_gate, grad_up], axis=1)
        grad_both[chip] = grads.reshape(2, rows, 2 * units)
        loader(grad_both.at[chip], grad_both_out.at[chip])
        for t in range(width // TILE):
            at = slice(t * TILE, (t + 1) * TILE)
            left = two[chip, :, at].reshape(2 * rows, TILE)
            term = dot_first(left, grads)
            if mask == 0:
                weight_sum[at, :] = term
            elif mask != 6:
                weight_sum[at, :] += term
            else:
                tile = pl.ds(t * TILE, TILE)
                grad_weight[at, :] = (weight_sum[at, :] + term).astype(bf16)
                loader(grad_weight.at[tile], weight_out.at[tile])

    rows_two.forward()
    loader.wait()
    work(0)
    rows_two.across()
    line.arrive(0)
    if planes > 2:
        line.start(1)
    work(2)
    rows_two.diagonal()
    work(4)
    if planes > 2:
        line.arrive(1)
    if planes > 3:
        line.start(2)
    work(6)
    if planes > 3:
        line.through(2, planes - 1)
    for step in range(min(2, planes - 1)):
        line.sent(step)
    sender.finish()
    for copy in loader.copies[4:]:
        copy.wait()


def feed(two, cot, weight, down, next_units, planes, collective):
    rows, width = two.shape
    units = weight.shape[1] // 2
    anywhere = pl.BlockSpec(memory_space=pl.ANY)
    like = jax.ShapeDtypeStruct
    return pl.pallas_call(
        functools.partial(feed_kernel, planes),
        out_shape=(
            like((TEAM, rows, width), bf16),
            like((TEAM, rows, units), bf16),
            like((TEAM, rows, 2 * units), bf16),
            like(weight.shape, bf16),
            like(next_units.shape, bf16),
        ),
        in_specs=[anywhere] * 5,
        out_specs=(anywhere,) * 5,
        input_output_aliases={4: 4},
        scratch_shapes=[
            pltpu.VMEM((TEAM, rows, width), bf16),
            pltpu.VMEM((TEAM, rows, width), bf16),
            pltpu.VMEM(weight.shape, bf16),
            pltpu.VMEM((units, width), bf16),
            pltpu.VMEM((2 * rows, 2 * units), f32),
            pltpu.VMEM(weight.shape, f32),
            pltpu.VMEM((TEAM, rows, units), bf16),
            pltpu.VMEM((TEAM, rows, 2 * units), bf16),
            pltpu.VMEM(weight.shape, bf16),
            pltpu.SemaphoreType.DMA((14 + 2 * (planes - 1),)),
            pltpu.SemaphoreType.DMA((14 + 2 * (planes - 1),)),
            pltpu.SemaphoreType.DMA((16 + width // TILE,)),
        ],
        compiler_params=params(collective, LIMIT),
        cost_estimate=pl.CostEstimate(
            flops=10 * TEAM * rows * width * units,
            bytes_accessed=8 * TEAM * rows * width,
            transcendentals=0,
        ),
    )(two, cot, weight, down, next_units)


def feed_rest_kernel(two, cot, weight, down, act, grad_both):
    blocks, rows, units = act.shape
    both = simple_product(two[...].reshape(blocks * rows, -1), weight[...])
    flat = cot[...].reshape(blocks * rows, -1)
    a, grad_gate, grad_up = hidden_grads(both, flat, down[...])
    act[...] = a.reshape(blocks, rows, units)
    grad_both[:, :, :units] = grad_gate.reshape(blocks, rows, units)
    grad_both[:, :, units:] = grad_up.reshape(blocks, rows, units)


def feed_rest(two, cot, weight, down, part):
    _, rows, width = two.shape
    units = weight.shape[1] // 2
    like = jax.ShapeDtypeStruct
    return pl.pallas_call(
        feed_rest_kernel,
        grid=(TEAM // 2,),
        out_shape=(like((TEAM, rows, units), bf16), like((TEAM, rows, 2 * units), bf16)),
        in_specs=[
            by_step(2, rows, width),
            by_step(2, rows, width),
            fixed(*weight.shape),
            pl.BlockSpec((units, width), lambda i: (part, 0)),
        ],
        out_specs=(by_step(2, rows, units), by_step(2, rows, 2 * units)),
        compiler_params=pltpu.CompilerParams(vmem_limit_bytes=LIMIT),
        cost_estimate=pl.CostEstimate(
            flops=6 * TEAM * rows * width * units,
            bytes_accessed=4 * TEAM * rows * width,
            transcendentals=0,
        ),
    )(two, cot, weight, down)


def local(
    devices,
    tokens,
    segments,
    micro_live,
    cotangent,
    w_query,
    key_weight,
    value_weight,
    w_output,
    attn_gain,
    query_norm_gain,
    key_gain,
    w_gate,
    w_up,
    w_down,
    mlp_gain,
):
    planes = devices // TEAM
    lines = [[place + TEAM * k for k in range(planes)] for place in range(TEAM)]
    slots, sequence = segments.shape
    token_count, width = tokens.shape
    groups = QUERY_HEADS // KEY_VALUE_HEADS
    rows = w_query.shape[0]
    parts = 2
    team_rows = TEAM * token_count
    head_width = groups * HEAD_SIZE
    me = lax.axis_index("fsdp")
    plane = me // TEAM

    def sum_line(x):
        return lax.psum_scatter(
            x, "fsdp", scatter_dimension=0, tiled=True, axis_index_groups=lines
        )

    slot_live = (lax.broadcasted_iota(jnp.int32, (slots, 1), 0) < micro_live[0]).astype(f32)
    row_live = jnp.broadcast_to(slot_live, (slots, sequence)).reshape(token_count, 1)

    smalls = [x[None] for x in (attn_gain, mlp_gain, query_norm_gain, key_gain)] + [segments]
    opened = opening(
        w_query,
        key_weight,
        value_weight,
        w_output,
        tokens,
        w_gate,
        w_up,
        w_down,
        smalls,
        planes,
        parts,
        1,
    )
    unit_slices, opened = opened[:parts], opened[parts:]
    qkv_weight, _, output_weight, team_tokens, down_weight = opened[:5]
    norm_gain, mlp_norm_gain, qgain, kgain, ids = opened[5:]
    mlp_norm_gain = mlp_norm_gain.reshape(width)
    qkv_weight = qkv_weight.reshape(width, -1)
    output_weight = output_weight.reshape(head_width, width)
    down_weight = down_weight.reshape(-1, width)
    table = jnp.asarray(rotation_tables(sequence))

    inputs = tokens.astype(f32)
    first, second = unit_slices
    team_normed, raw, turned, value_b, context_b, middle, normed_two, team_cot, first = attend(
        team_tokens.reshape(team_rows, width),
        norm_gain,
        qkv_weight,
        ids,
        table,
        qgain,
        kgain,
        output_weight,
        tokens,
        cotangent,
        row_live.astype(bf16),
        mlp_norm_gain.reshape(1, width),
        first,
        planes,
        2,
    )

    unit_weights = [first.reshape(width, -1)]
    team_two, act, grad_both, first_units, second = feed(
        normed_two, team_cot, unit_weights[0], down_weight, second, planes, 0
    )
    unit_weights.append(second.reshape(width, -1))
    acts, grads_both, grad_units = [act], [grad_both], [first_units]
    for k in range(1, parts):
        act, grad_both = feed_rest(team_two, team_cot, unit_weights[k], down_weight, k)
        acts.append(act)
        grads_both.append(grad_both)
    grad_normed_two, last_units = feed_back(team_two, grads_both, unit_weights, 4)
    grad_units = [sum_line(g) for g in (*grad_units, last_units)[:parts]]
    _, pull_two = jax.vjp(root_mean_square_norm, middle, mlp_norm_gain)
    middle_part, grad_mgain = pull_two(grad_normed_two)
    grad_middle = (cotangent * row_live.astype(bf16)).astype(f32) + middle_part
    team_grad, grad_down = gather_down(grad_middle.astype(bf16), team_cot, acts, 10)
    team_grad = team_grad.reshape(team_rows, width)
    grad_down = sum_line(grad_down)

    grad_qkv, grad_attention, out_blocks, grad_head_gains, out_line = attend_back(
        team_grad,
        output_weight,
        context_b,
        raw,
        turned,
        value_b,
        team_normed,
        ids,
        table,
        qgain,
        kgain,
        planes,
        6,
    )
    grad_attention = sum_line(grad_attention.reshape(-1, grad_attention.shape[2]))
    grad_normed, summed_out, grad_gate, grad_up, grad_output, _ = last_sums(
        grad_qkv.reshape(TEAM, token_count, -1),
        qkv_weight,
        acts,
        down_weight,
        [g.reshape(TEAM, rows, -1) for g in grad_units],
        out_blocks,
        out_line,
        planes,
        5,
    )
    grad_gate, grad_up = grad_gate.astype(f32), grad_up.astype(f32)
    _, pull_one = jax.vjp(root_mean_square_norm, inputs, norm_gain.reshape(width))
    input_part, grad_again = pull_one(grad_normed)
    grad_tokens = (grad_middle + input_part).astype(bf16)
    layer_out = (row_live * (middle + summed_out)).astype(bf16)

    def by_owner(vector):
        vector = vector.reshape(devices, -1)
        return jnp.pad(vector, ((0, 0), (0, 128 - vector.shape[1])))

    gains = jnp.stack(
        [by_owner(v) for v in (grad_again, grad_mgain, grad_head_gains[0], grad_head_gains[1])], axis=1
    )
    gains = jnp.pad(gains, ((0, 0), (0, 4), (0, 0)))
    gains = gains.reshape(planes, TEAM, 8, 128).transpose(1, 0, 2, 3)

    grad_attention, grad_gate, grad_up, layer_out, grad_tokens = lax.optimization_barrier(
        (grad_attention, grad_gate, grad_up, layer_out, grad_tokens)
    )
    grad_query, grad_key, grad_value_w, gains = closing(
        grad_attention,
        gains,
        rows,
        (w_query.shape[1], key_weight.shape[1], value_weight.shape[1]),
        planes,
        9,
    )
    attention_grads = tuple(
        g.astype(f32) for g in (grad_query, grad_key, grad_value_w, grad_output)
    )
    gains = (
        gains[0, : attn_gain.shape[0]],
        gains[2, : query_norm_gain.shape[0]],
        gains[3, : key_gain.shape[0]],
        gains[1, : mlp_gain.shape[0]],
    )
    grad_down, attention_grads, gains = lax.optimization_barrier(
        (grad_down, attention_grads, gains)
    )
    return (
        layer_out,
        grad_tokens,
        *attention_grads,
        *gains[:3],
        grad_gate,
        grad_up,
        grad_down.astype(f32),
        gains[3],
    )


def solution(mesh):
    by_rows, by_entry = P("fsdp", None), P("fsdp")
    return jax.shard_map(
        functools.partial(local, mesh.shape["fsdp"]),
        mesh=mesh,
        in_specs=(
            by_rows,
            by_rows,
            by_entry,
            by_rows,
            by_rows,
            by_rows,
            by_rows,
            by_rows,
            by_entry,
            by_entry,
            by_entry,
            by_rows,
            by_rows,
            by_rows,
            by_entry,
        ),
        out_specs=(
            by_rows,
            by_rows,
            by_rows,
            by_rows,
            by_rows,
            by_rows,
            by_entry,
            by_entry,
            by_entry,
            by_rows,
            by_rows,
            by_rows,
            by_entry,
        ),
        check_vma=False,
    )
```

```python
import functools

import jax
import jax.numpy as jnp
import numpy as np
from jax import lax
from jax.experimental import pallas as pl
from jax.experimental.pallas import tpu as pltpu
from jax.sharding import PartitionSpec as P

QUERY_HEADS = 16
KEY_VALUE_HEADS = 8
HEAD_SIZE = 128
TEAM = 8
STEP = 256

epsilon = 1e-06
base_theta = 1000000.0
MESH = pl.DeviceIdType.MESH
LIMIT = 60 * 2**20
f32 = jnp.float32
bf16 = jnp.bfloat16


def root_mean_square_norm(values, gain):
    return values * lax.rsqrt(jnp.mean(values * values, axis=-1, keepdims=True) + epsilon) * gain


def rotation_tables(positions):
    half = HEAD_SIZE // 2
    powers = -np.arange(half, dtype=np.float32) * np.float32(2.0) / np.float32(HEAD_SIZE)
    freqs = np.power(np.float32(base_theta), powers).astype(np.float32)
    angles = np.arange(positions, dtype=np.float32)[:, None] * freqs
    cosine, sine = np.cos(angles), np.sin(angles)
    rest = np.concatenate([cosine, cosine, -sine, sine], axis=1).astype(np.float32)
    parts = []
    for _ in range(3):
        parts.append(rest.astype(jnp.bfloat16))
        rest = rest - parts[-1].astype(np.float32)
    return np.concatenate(parts, axis=1)


def dot_last(left, right):
    return lax.dot_general(
        left, right, (((1,), (1,)), ((), ())), preferred_element_type=jnp.float32
    )


def dot_first(left, right):
    return lax.dot_general(
        left, right, (((0,), (0,)), ((), ())), preferred_element_type=jnp.float32
    )


def simple_product(left, right):
    return jnp.dot(left, right, preferred_element_type=jnp.float32)


def flipped(index, mask):
    for bit in (1, 2, 4):
        if mask & bit:
            index = index + bit * (1 - 2 * lax.rem(lax.div(index, bit), 2))
    return index


def greet(me, masks, others=()):
    barrier = pltpu.get_barrier_semaphore()
    for device in (*(flipped(me, mask) for mask in masks), *others):
        pl.semaphore_signal(barrier, inc=1, device_id=(device,), device_id_type=MESH)
    pl.semaphore_wait(barrier, len(masks) + len(others))


def remote(source, target, send, receive, device):
    return pltpu.make_async_remote_copy(
        src_ref=source,
        dst_ref=target,
        send_sem=send,
        recv_sem=receive,
        device_id=(device,),
        device_id_type=MESH,
    )


def params(collective, limit=None):
    if limit is None:
        return pltpu.CompilerParams(collective_id=collective, has_side_effects=True)
    return pltpu.CompilerParams(
        collective_id=collective, has_side_effects=True, vmem_limit_bytes=limit
    )


class Gather:
    def __init__(self, begin, x, o, me):
        self.begin, self.x, self.o, self.me = begin, x, o, me
        self.place = lax.rem(me, TEAM)
        self.half = x.shape[0] // 2

    def part(self, ref, which):
        return ref.at[pl.ds(which * self.half, self.half)]

    def first(self, which, mask):
        target = self.part(self.o.at[self.place], which)
        return self.begin(self.part(self.x, which), target, flipped(self.me, mask))

    def relay(self, origin, which, mask):
        ref = self.part(self.o.at[flipped(self.place, origin)], which)
        return self.begin(ref, ref, flipped(self.me, mask))

    def start(self):
        self.x0, self.y1 = self.first(0, 2), self.first(1, 4)
        self.x1, self.y0 = self.first(1, 2), self.first(0, 4)
        self.late = [self.first(0, 1), self.first(1, 1)]

    def forward(self):
        self.x0.wait_recv()
        self.d0 = self.relay(2, 0, 4)
        self.y1.wait_recv()
        self.d1 = self.relay(4, 1, 2)
        self.late += [self.relay(2, 0, 1), self.relay(4, 1, 1)]

    def across(self):
        self.x1.wait_recv()
        self.late.append(self.relay(2, 1, 1))
        self.y0.wait_recv()
        self.late.append(self.relay(4, 0, 1))

    def diagonal(self):
        self.d0.wait_recv()
        self.late.append(self.relay(6, 0, 1))
        self.d1.wait_recv()
        self.late.append(self.relay(6, 1, 1))

    def arrive(self):
        for copy in self.late:
            copy.wait_recv()


class Sender:
    def __init__(self, send, receive):
        self.send, self.receive, self.count, self.started = send, receive, 0, []

    def take(self):
        self.count += 1
        return self.count - 1

    def __call__(self, source, target, device):
        k = self.take()
        copy = remote(source, target, self.send.at[k], self.receive.at[k], device)
        copy.start()
        self.started.append(copy)
        return copy

    def finish(self):
        for copy in self.started:
            copy.wait_send()


class Line:
    def __init__(self, sender, ref, planes, me):
        self.sender, self.ref, self.planes = sender, ref, planes
        self.plane, self.place = lax.div(me, TEAM), lax.rem(me, TEAM)
        self.flows = [(sign, [sender.take() for _ in range(planes - 1)]) for sign in (1, -1)]

    def passing(self, step, sign, ks, source):
        block = jnp.clip(source, 0, self.planes - 1)
        beyond = jnp.clip(self.plane + sign, 0, self.planes - 1) * TEAM + self.place
        ref, k = self.ref.at[block], ks[step]
        return remote(ref, ref, self.sender.send.at[k], self.sender.receive.at[k], beyond)

    def goes(self, step, sign):
        source, onward = self.plane - sign * step, self.plane + sign
        last = self.planes - 1
        return (source >= 0) & (source <= last) & (onward >= 0) & (onward <= last)

    def start(self, step):
        for sign, ks in self.flows:
            going = self.passing(step, sign, ks, self.plane - sign * step)
            pl.when(self.goes(step, sign))(going.start)

    def arrive(self, step):
        for sign, ks in self.flows:
            source = self.plane - sign * (step + 1)
            coming = self.passing(step, sign, ks, source)
            pl.when((source >= 0) & (source <= self.planes - 1))(coming.wait_recv)

    def sent(self, step):
        for sign, ks in self.flows:
            going = self.passing(step, sign, ks, self.plane - sign * step)
            pl.when(self.goes(step, sign))(going.wait_send)

    def through(self, first, last):
        for step in range(first, last):
            self.arrive(step)
            if step + 1 < last:
                self.start(step + 1)
        for step in range(first, last):
            self.sent(step)


def line_peers(me, planes):
    return [lax.rem(me + TEAM * k, planes * TEAM) for k in range(1, planes)]


TILE = 512
STRIP = 16


class TeamSum:
    def __init__(self, sender, me, out, buffers, lefts, rights, turned):
        self.sender, self.me, self.out = sender, me, out
        self.mix, self.from_core, self.from_x, self.from_y = buffers
        self.lefts, self.rights, self.turned = lefts, rights, turned
        place = lax.rem(me, TEAM)
        self.core = lax.rem(place, 2)
        self.rows, self.width = out.shape
        self.half = self.rows // 2
        self.chips = [lax.div(flipped(place, mask), 2) for mask in (6, 2, 4, 0)]
        self.across = []

    def product(self, j):
        @pl.loop(0, self.width // TILE)
        def _(t):
            at = pl.ds(pl.multiple_of(t * TILE, TILE), TILE)
            value = 0.0
            for left, right in zip(self.lefts, self.rights):
                if len(left.shape) == 2:
                    first = pl.multiple_of(self.chips[j] * 2 * self.rows, 2 * self.rows)
                    both = left[pl.ds(first, 2 * self.rows), :]
                else:
                    both = left[pl.ds(2 * self.chips[j], 2)].reshape(2 * self.rows, left.shape[2])
                if self.turned:
                    value = value + dot_last(both, right[at, :])
                else:
                    value = value + simple_product(both, right[:, at])
            self.mix[j, :, :, at] = value.astype(bf16).reshape(2, self.rows, TILE)

        self.across.append(
            self.sender(self.mix.at[j, 1 - self.core], self.from_core.at[j], flipped(self.me, 1))
        )

    def combine(self, j):
        self.across[j].wait_recv()

        @pl.loop(0, self.rows // STRIP)
        def _(i):
            at = pl.ds(i * STRIP, STRIP)
            self.mix[j, self.core, at, :] = (
                self.mix[j, self.core, at, :].astype(f32) + self.from_core[j, at, :].astype(f32)
            ).astype(bf16)

    def begin(self, j, which, ref, slot, mask):
        source = self.mix.at[j, self.core, pl.ds(which * self.half, self.half)]
        return self.sender(source, ref.at[slot], flipped(self.me, mask))

    def add_relayed(self, j, which, ref):
        @pl.loop(0, self.half // STRIP)
        def _(i):
            at = pl.ds(which * self.half + i * STRIP, STRIP)
            self.mix[j, self.core, at, :] = (
                self.mix[j, self.core, at, :].astype(f32)
                + ref[0, pl.ds(i * STRIP, STRIP), :].astype(f32)
            ).astype(bf16)

    def start(self):
        self.product(0)
        self.product(1)
        self.combine(0)
        self.d_x = self.begin(0, 0, self.from_x, 0, 2)
        self.d_y = self.begin(0, 1, self.from_y, 0, 4)
        self.product(2)
        self.combine(1)
        self.x_0 = self.begin(1, 0, self.from_x, 1, 2)
        self.combine(2)
        self.y_1 = self.begin(2, 1, self.from_y, 1, 4)

    def own(self):
        self.product(3)

    def relay(self):
        self.d_x.wait_recv()
        self.add_relayed(2, 0, self.from_x)
        self.y_0 = self.begin(2, 0, self.from_y, 2, 4)
        self.d_y.wait_recv()
        self.add_relayed(1, 1, self.from_y)
        self.x_1 = self.begin(1, 1, self.from_x, 2, 2)

    def gather_half(self, which, slot_x, slot_y):
        @pl.loop(0, self.half // STRIP)
        def _(i):
            at = pl.ds(which * self.half + i * STRIP, STRIP)
            here = pl.ds(i * STRIP, STRIP)
            self.out[at, :] = (
                self.mix[3, self.core, at, :].astype(f32) + self.from_core[3, at, :].astype(f32)
            ) + (
                self.from_x[slot_x, here, :].astype(f32) + self.from_y[slot_y, here, :].astype(f32)
            )

    def finish(self):
        self.across[3].wait_recv()
        self.x_0.wait_recv()
        self.y_0.wait_recv()
        self.gather_half(0, 1, 2)
        self.y_1.wait_recv()
        self.x_1.wait_recv()
        self.gather_half(1, 2, 1)


SUM_COPIES = 10


def sum_buffers(rows, width):
    return [
        pltpu.VMEM((4, 2, rows, width), bf16),
        pltpu.VMEM((4, rows, width), bf16),
        pltpu.VMEM((3, rows // 2, width), bf16),
        pltpu.VMEM((3, rows // 2, width), bf16),
    ]


class Loader:
    def __init__(self, sems):
        self.sems, self.copies = sems, []

    def __call__(self, source, target):
        copy = pltpu.make_async_copy(source, target, self.sems.at[len(self.copies)])
        copy.start()
        self.copies.append(copy)
        return copy

    def wait(self):
        for copy in self.copies:
            copy.wait()


def rows_of(ref, k, rows):
    return ref.at[pl.ds(k * rows, rows)]


def turned_product(left, right, out, part, parts):
    blocks, rows, units = left.shape
    width = right.shape[2]
    tiles = width // TILE
    flat = left[...].reshape(blocks * rows, units)

    @pl.loop(part * tiles // parts, (part + 1) * tiles // parts)
    def _(t):
        at = pl.ds(pl.multiple_of(t * TILE, TILE), TILE)
        value = dot_first(flat, right[:, :, at].reshape(blocks * rows, TILE))
        out[:, at] = value.astype(bf16)


def turned_rows(left, right, out, part, parts):
    blocks, rows, width = left.shape
    tiles = width // TILE
    flat = right[...].reshape(blocks * rows, right.shape[2])

    @pl.loop(part * tiles // parts, (part + 1) * tiles // parts)
    def _(t):
        at = pl.ds(pl.multiple_of(t * TILE, TILE), TILE)
        value = dot_first(left[:, :, at].reshape(blocks * rows, TILE), flat)
        out[at, :] = value.astype(bf16)


def feed_back_kernel(parts, two, *refs):
    grads, weights, refs = refs[:parts], refs[parts : 2 * parts], refs[2 * parts :]
    out, weight_out, buffers, refs = refs[0], refs[1], refs[2:6], refs[6:]
    grads_here, weights_here = refs[:parts], refs[parts : 2 * parts]
    two_here, send, receive, own = refs[2 * parts :]
    me = lax.axis_index("fsdp")
    loader = Loader(own)
    for source, target in zip((*grads, *weights), (*grads_here, *weights_here)):
        loader(source, target)
    greet(me, (1, 2, 4))
    loader.wait()
    loader(two, two_here)
    sender = Sender(send, receive)
    total = TeamSum(sender, me, out, buffers, grads_here, weights_here, True)
    total.start()
    loader.copies[-1].wait()
    total.relay()
    total.own()
    turned_rows(two_here, grads_here[-1], weight_out, 0, 1)
    total.finish()
    sender.finish()


def feed_back(two, grads, weights, collective):
    _, rows, width = two.shape
    parts, units = len(grads), grads[0].shape[2]
    anywhere = pl.BlockSpec(memory_space=pl.ANY)
    vmem = pl.BlockSpec(memory_space=pltpu.VMEM)
    like = jax.ShapeDtypeStruct
    return pl.pallas_call(
        functools.partial(feed_back_kernel, parts),
        out_shape=(like((rows, width), f32), like((width, units), bf16)),
        in_specs=[anywhere] * (1 + 2 * parts),
        out_specs=(vmem, vmem),
        scratch_shapes=[
            *sum_buffers(rows, width),
            *(pltpu.VMEM(x.shape, bf16) for x in (*grads, *weights, two)),
            pltpu.SemaphoreType.DMA((SUM_COPIES,)),
            pltpu.SemaphoreType.DMA((SUM_COPIES,)),
            pltpu.SemaphoreType.DMA((2 * parts + 1,)),
        ],
        compiler_params=params(collective, LIMIT),
        cost_estimate=pl.CostEstimate(
            flops=2 * TEAM * rows * units * width * (parts + 1),
            bytes_accessed=2 * TEAM * rows * (units * parts + width),
            transcendentals=0,
        ),
    )(two, *grads, *weights)


def gather_down_kernel(parts, x, cot, *refs):
    acts, refs = refs[:parts], refs[parts:]
    o_ref, down_out, refs = refs[0], refs[1], refs[2:]
    acts_here, (cot_here, send, receive, own) = refs[:parts], refs[parts:]
    me = lax.axis_index("fsdp")
    loader = Loader(own)
    loader(x, o_ref.at[lax.rem(me, TEAM)])
    loader(cot, cot_here)
    for source, target in zip(acts, acts_here):
        loader(source, target)
    greet(me, (1, 2, 4))
    sender = Sender(send, receive)
    moves = Gather(sender, x, o_ref, me)
    units = acts_here[0].shape[2]

    def work(k):
        turned_product(
            acts_here[k // 2], cot_here, rows_of(down_out, k // 2, units), k % 2, 2
        )

    moves.start()
    loader.wait()
    work(0)
    moves.forward()
    work(1)
    moves.across()
    if parts > 1:
        work(2)
    moves.diagonal()
    if parts > 1:
        work(3)
    moves.arrive()
    sender.finish()


def gather_down(x, cot, acts, collective):
    rows, width = x.shape
    parts, units = len(acts), acts[0].shape[2]
    anywhere = pl.BlockSpec(memory_space=pl.ANY)
    vmem = pl.BlockSpec(memory_space=pltpu.VMEM)
    like = jax.ShapeDtypeStruct
    return pl.pallas_call(
        functools.partial(gather_down_kernel, parts),
        out_shape=(like((TEAM, rows, width), x.dtype), like((parts * units, width), bf16)),
        in_specs=[vmem, anywhere] + [anywhere] * parts,
        out_specs=(anywhere, vmem),
        scratch_shapes=[
            *(pltpu.VMEM(a.shape, bf16) for a in acts),
            pltpu.VMEM(cot.shape, bf16),
            pltpu.SemaphoreType.DMA((14,)),
            pltpu.SemaphoreType.DMA((14,)),
            pltpu.SemaphoreType.DMA((2 + parts,)),
        ],
        compiler_params=params(collective, LIMIT),
        cost_estimate=pl.CostEstimate(
            flops=2 * TEAM * rows * width * units * parts,
            bytes_accessed=6 * TEAM * rows * width,
            transcendentals=0,
        ),
    )(x, cot, *acts)


def last_sums_kernel(planes, parts, grad_qkv, qkv_weight, down, out_blocks, before, *refs):
    acts, units, refs = refs[:parts], refs[parts : 2 * parts], refs[2 * parts :]
    grad_normed, layer, gate, up, output, after, *refs = refs
    first, second, refs = refs[:4], refs[4:8], refs[8:]
    acts_here, downs_here, refs = refs[:parts], refs[parts : 2 * parts], refs[2 * parts :]
    grad_here, weight_here, landed, mine, there, sems, out_sum, send, receive, own = refs
    me = lax.axis_index("fsdp")
    place = lax.rem(me, TEAM)
    loader = Loader(own)
    loader(grad_qkv, grad_here)
    loader(qkv_weight, weight_here)
    for k in range(parts):
        loader(units[k].at[place], landed.at[k, place])
        loader(acts[k], acts_here[k])
        loader(rows_of(down, k, downs_here[k].shape[0]), downs_here[k])
    greet(me, range(1, TEAM), line_peers(me, planes))
    sender = Sender(send, receive)
    line = LineSum(sender, out_blocks, before.at[0], after, mine, there, sems, planes, me, 1)
    line.start(0)
    moves = [
        sender(units[k].at[flipped(place, m)], landed.at[k, place], flipped(me, m))
        for k in range(parts)
        for m in SWAP_ORDER
    ]
    loader.wait()
    one = TeamSum(sender, me, grad_normed, first, [grad_here], [weight_here], True)
    two = TeamSum(sender, me, layer, second, acts_here, downs_here, False)
    one.start()
    one.own()
    two.start()
    one.relay()
    two.own()
    line.wait(0)
    if planes > 3:
        line.start(1)
    two.relay()
    for copy in moves:
        copy.wait_recv()
    block = gate.shape[1] // (planes * TEAM)
    some = planes // parts
    span = TEAM * block
    for j, ref in enumerate((gate, up)):
        for g in range(planes):
            at = (j * some + g % some) * block
            ref[:, g * span : (g + 1) * span] = jnp.concatenate(
                [landed[g // some, q, :, at : at + block] for q in range(TEAM)], axis=1
            )
    one.finish()
    two.finish()
    for k in range(1, planes - 2):
        if k > 1:
            line.start(k)
        line.wait(k)
    line.total(out_sum)
    width, rows = out_sum.shape[1], output.shape[0]
    for c in range(output.shape[1] // width):
        output[:, c * width : (c + 1) * width] = out_sum[c * rows : (c + 1) * rows]
    sender.finish()


def last_sums(grad_qkv, qkv_weight, acts, down, units, out_blocks, before, planes, collective):
    _, rows, depth = grad_qkv.shape
    width = qkv_weight.shape[0]
    parts = len(acts)
    anywhere = pl.BlockSpec(memory_space=pl.ANY)
    vmem = pl.BlockSpec(memory_space=pltpu.VMEM)
    like = jax.ShapeDtypeStruct
    _, own_rows, some = units[0].shape
    steps = planes - 2
    links = 2 * SUM_COPIES + (TEAM - 1) * parts + 2 * steps
    _, block, block_width = out_blocks.shape
    home = like((own_rows, TEAM * parts * some // 2), bf16)
    return pl.pallas_call(
        functools.partial(last_sums_kernel, planes, parts),
        out_shape=(like((rows, width), f32),) * 2
        + (home,) * 2
        + (like((own_rows, width), f32), like((steps, 2, block, block_width), bf16),),
        in_specs=[anywhere] * (5 + 2 * parts),
        out_specs=(vmem,) * 5 + (anywhere,),
        scratch_shapes=[
            *sum_buffers(rows, width),
            *sum_buffers(rows, width),
            *(pltpu.VMEM(a.shape, bf16) for a in acts),
            *(pltpu.VMEM((a.shape[2], width), bf16) for a in acts),
            pltpu.VMEM(grad_qkv.shape, bf16),
            pltpu.VMEM(qkv_weight.shape, bf16),
            pltpu.VMEM((parts, *units[0].shape), bf16),
            *line_scratch(block, block_width),
            pltpu.VMEM((block, block_width), f32),
            pltpu.SemaphoreType.DMA((links,)),
            pltpu.SemaphoreType.DMA((links,)),
            pltpu.SemaphoreType.DMA((2 + 3 * parts,)),
        ],
        compiler_params=params(collective, LIMIT),
        cost_estimate=pl.CostEstimate(
            flops=2 * TEAM * rows * width * (depth + sum(a.shape[2] for a in acts)),
            bytes_accessed=4 * TEAM * rows * depth,
            transcendentals=0,
        ),
    )(grad_qkv, qkv_weight, down, out_blocks, before, *acts, *units)


class LineSum:
    def __init__(self, sender, own, before, after, mine, there, sems, planes, me, first):
        self.sender, self.own, self.before, self.after = sender, own, before, after
        self.mine, self.there, self.sems = mine, there, sems
        self.planes, self.me, self.first = planes, me, first
        self.plane = lax.div(me, TEAM)
        self.flows = [(sign, [sender.take() for _ in range(after.shape[0])]) for sign in (1, -1)]

    def rank(self, sign):
        return self.plane if sign > 0 else self.planes - 1 - self.plane

    def block(self, sign, step):
        rank = jnp.clip(self.planes - 1 - (step - self.rank(sign)), 0, self.planes - 1)
        return rank if sign > 0 else self.planes - 1 - rank

    def sends(self, sign, step):
        rank = self.rank(sign)
        return (rank <= step) & (rank < self.planes - 1)

    def comes(self, sign, step):
        rank = self.rank(sign)
        return (rank >= 1) & (rank - 1 <= step)

    def copy(self, sign, k):
        d = 0 if sign > 0 else 1
        beyond = jnp.clip(self.plane + sign, 0, self.planes - 1) * TEAM + lax.rem(self.me, TEAM)
        sem = dict((sign, ks[k]) for sign, ks in self.flows)[sign]
        target = self.after.at[k, d]
        send, receive = self.sender.send.at[sem], self.sender.receive.at[sem]
        return remote(self.mine.at[d], target, send, receive, beyond)

    def start(self, k):
        step = self.first + k
        for d, (sign, _) in enumerate(self.flows):

            @pl.when(self.sends(sign, step))
            def _():
                load = pltpu.make_async_copy(
                    self.own.at[self.block(sign, step)], self.mine.at[d], self.sems.at[0]
                )
                load.start()
                load.wait()
                if step > 0:

                    @pl.when(self.rank(sign) >= 1)
                    def _():
                        source = self.after.at[k - 1, d] if k else self.before.at[d]
                        load = pltpu.make_async_copy(source, self.there, self.sems.at[1])
                        load.start()
                        load.wait()
                        self.add(d)

                self.copy(sign, k).start()

    def add(self, d):
        @pl.loop(0, self.there.shape[0] // STRIP)
        def _(i):
            at = pl.ds(i * STRIP, STRIP)
            self.mine[d, at, :] = (
                self.mine[d, at, :].astype(f32) + self.there[at, :].astype(f32)
            ).astype(bf16)

    def wait(self, k):
        step = self.first + k
        for sign, _ in self.flows:
            copy = self.copy(sign, k)
            pl.when(self.sends(sign, step))(copy.wait_send)
            pl.when(self.comes(sign, step))(copy.wait_recv)

    def rest(self):
        for k in range(self.after.shape[0]):
            if k:
                self.start(k)
            self.wait(k)

    def total(self, out):
        load = pltpu.make_async_copy(self.own.at[self.plane], self.mine.at[0], self.sems.at[0])
        load.start()
        load.wait()

        @pl.loop(0, out.shape[0] // STRIP)
        def _(i):
            at = pl.ds(i * STRIP, STRIP)
            out[at, :] = self.mine[0, at, :].astype(f32)

        for d, (sign, _) in enumerate(self.flows):

            @pl.when(self.rank(sign) >= 1)
            def _():
                load = pltpu.make_async_copy(
                    self.after.at[self.after.shape[0] - 1, d], self.there, self.sems.at[1]
                )
                load.start()
                load.wait()

                @pl.loop(0, out.shape[0] // STRIP)
                def _(i):
                    at = pl.ds(i * STRIP, STRIP)
                    out[at, :] = out[at, :] + self.there[at, :].astype(f32)


def line_scratch(rows, width):
    return [
        pltpu.VMEM((2, rows, width), bf16),
        pltpu.VMEM((rows, width), bf16),
        pltpu.SemaphoreType.DMA((2,)),
    ]


SWAP_ORDER = (6, 7, 2, 3, 4, 5, 1)


def open_kernel(
    planes, parts, query_in, key_in, value_in, output_in, tokens_in, gate_in, up_in, down_in, *refs
):
    smalls, refs = refs[:5], refs[5:]
    gate_up, refs = refs[:parts], refs[parts:]
    qkv, output_raw, output, tokens, down, *gain_refs, numbers = refs[:10]
    small_in, small, sorted_units, send, receive, own = refs[10:]
    slots, sequence = smalls[4].shape
    small_in[...] = jnp.zeros_like(small_in)
    for k, ref in enumerate(smalls):
        small_in[k : k + ref.shape[0], : ref.shape[1]] = ref[...].astype(f32)
    me = lax.axis_index("fsdp")
    place = lax.rem(me, TEAM)
    plane = lax.div(me, TEAM)
    team = me - place
    others = [lax.rem(me + TEAM * k, planes * TEAM) for k in range(1, planes)]
    sender = Sender(send, receive)
    keeps = []

    def keep(source, target):
        copy = pltpu.make_async_copy(source, target, own.at[len(keeps)])
        copy.start()
        keeps.append(copy)

    qkv_parts, at = [], 0
    for ref in (query_in, key_in, value_in):
        part = ref.shape[1] // TEAM
        qkv_parts.append((ref, part, qkv.at[plane, place, :, pl.ds(at, part)]))
        at += part

    def columns(ref, part, target):
        return ref.at[:, pl.ds(pl.multiple_of(target * part, part), part)]

    for ref, part, target in qkv_parts:
        keep(columns(ref, part, place), target)
    keep(small_in, small.at[me])
    keep(tokens_in, tokens.at[place])
    keep(down_in, down.at[plane])
    keep(output_in, output_raw.at[plane])
    greet(me, range(1, TEAM), others)

    qkv_line = Line(sender, qkv, planes, me)
    out_line = Line(sender, output_raw, planes, me)
    down_line = Line(sender, down, planes, me)
    rows_tokens = Gather(sender, tokens_in, tokens, me)
    spread_send = [sender.take() for _ in range(planes)]
    spread_own = len(keeps)

    def outgoing(k):
        number = TEAM * k + place
        partner, there = lax.div(number, planes), lax.rem(number, planes)
        s, r = send.at[spread_send[0] + k], receive.at[spread_send[0] + there]
        over = remote(output_raw.at[k], output.at[there], s, r, team + partner)
        here = pltpu.make_async_copy(output_raw.at[k], output.at[there], own.at[spread_own + k])
        return partner, over, here

    def incoming(k):
        partner = lax.rem(planes * place + k, TEAM)
        s, r = send.at[spread_send[k]], receive.at[spread_send[k]]
        return partner, remote(output_raw.at[k], output.at[k], s, r, team + partner)

    def spread_one(k, inside):
        partner, over, here = outgoing(jnp.clip(k, 0, planes - 1))
        pl.when(inside & (partner != place))(over.start)
        pl.when(inside & (partner == place))(here.start)

    def step_out(step):
        out_line.arrive(step)
        if step < planes - 2:
            out_line.start(step + 1)
        spread_one(plane - step - 1, plane - step - 1 >= 0)
        spread_one(plane + step + 1, plane + step + 1 <= planes - 1)

    keeps[-1].wait()
    out_line.start(0)
    keeps[-2].wait()
    down_line.start(0)
    swaps = [
        sender(columns(ref, part, flipped(place, m)), target, flipped(me, m))
        for m in SWAP_ORDER
        for ref, part, target in qkv_parts
    ]
    near = [sender(small_in, small.at[me], flipped(me, m)) for m in SWAP_ORDER]
    block = gate_in.shape[1] // (planes * TEAM)
    some = planes // parts
    units = some * block
    for k in range(parts):
        for q in range(TEAM):
            for j, ref in enumerate((gate_in, up_in)):
                starts = [(TEAM * g + q) * block for g in range(k * some, (k + 1) * some)]
                sorted_units[k, q, :, j * units : (j + 1) * units] = jnp.concatenate(
                    [ref[:, at : at + block] for at in starts], axis=1
                )
    for copy in swaps:
        copy.wait_recv()
    for copy in keeps[:3]:
        copy.wait()
    qkv_line.start(0)
    rows_tokens.start()
    kept_units = [
        pltpu.make_async_copy(
            sorted_units.at[k, place], gate_up[k].at[plane, place], own.at[spread_own + planes + k]
        )
        for k in range(parts)
    ]
    for copy in kept_units:
        copy.start()
    step_out(0)
    rows_tokens.forward()
    spread_one(plane, True)
    for copy in near:
        copy.wait_recv()
    keeps[3].wait()
    shared = small.at[pl.ds(team, TEAM)]
    far = [sender(shared, shared, other) for other in others]
    for step in range(planes - 1):
        down_line.arrive(step)
        if step < planes - 2:
            down_line.start(step + 1)
        qkv_line.arrive(step)
        if step < planes - 2:
            qkv_line.start(step + 1)
            step_out(step + 1)
        if step == 0:
            rows_tokens.across()
            moves = [
                sender(
                    sorted_units.at[k, flipped(place, m)],
                    gate_up[k].at[plane, place],
                    flipped(me, m),
                )
                for k in range(parts)
                for m in SWAP_ORDER
            ]
            rows_tokens.diagonal()
            for copy in far:
                copy.wait_recv()
            for k, ref in enumerate(gain_refs):
                part = smalls[k].shape[1]
                ref[...] = jnp.concatenate(
                    [small[i, k : k + 1, :part] for i in range(planes * TEAM)], axis=1
                )
            per_step = STEP // sequence
            for i in range(numbers.shape[0]):
                pieces = []
                for m in range(i * per_step, (i + 1) * per_step):
                    row = 4 + m % slots
                    pieces.append(small[team + m // slots, row : row + 1, :sequence] + 64.0 * m)
                numbers[i] = jnp.concatenate(pieces, axis=1)
    rows_tokens.arrive()
    for copy in moves:
        copy.wait_recv()
    for copy in kept_units:
        copy.wait()
    for k in range(planes):
        partner, over, here = outgoing(k)
        pl.when(partner != place)(over.wait_send)
        pl.when(partner == place)(here.wait)
        partner, arriving = incoming(k)
        pl.when(partner != place)(arriving.wait_recv)
    for step in range(planes - 1):
        qkv_line.sent(step)
        out_line.sent(step)
        down_line.sent(step)
    sender.finish()
    for copy in keeps[4:-2]:
        copy.wait()


def opening(query, key, value, output, tokens, gate, up, down, smalls, planes, parts, collective):
    links = 28 + 6 * (planes - 1) + 14 + planes - 1 + planes + parts * (TEAM - 1)
    anywhere = pl.BlockSpec(memory_space=pl.ANY)
    vmem = pl.BlockSpec(memory_space=pltpu.VMEM)
    like = jax.ShapeDtypeStruct
    rows = query.shape[0]
    width = (query.shape[1] + key.shape[1] + value.shape[1]) // TEAM
    units = (TEAM, rows, 2 * gate.shape[1] // TEAM // parts)
    devices = planes * TEAM
    return pl.pallas_call(
        functools.partial(open_kernel, planes, parts),
        out_shape=(
            *((like((planes, *units), bf16),) * parts),
            like((planes, TEAM, rows, width), bf16),
            like((planes, *output.shape), bf16),
            like((planes, *output.shape), bf16),
            like((TEAM, *tokens.shape), bf16),
            like((planes, *down.shape), bf16),
            *(like((1, devices * x.shape[1]), f32) for x in smalls[:4]),
            like((TEAM * tokens.shape[0] // STEP, 1, STEP), f32),
        ),
        in_specs=[vmem] * 13,
        out_specs=(anywhere,) * (5 + parts) + (vmem,) * 5,
        scratch_shapes=[
            pltpu.VMEM((8, 128), f32),
            pltpu.VMEM((devices, 8, 128), f32),
            pltpu.VMEM((parts, *units), bf16),
            pltpu.SemaphoreType.DMA((links,)),
            pltpu.SemaphoreType.DMA((links,)),
            pltpu.SemaphoreType.DMA((7 + planes + parts,)),
        ],
        compiler_params=params(collective, LIMIT),
    )(query, key, value, output, tokens, gate, up, down, *smalls)


def close_kernel(planes, x_ref, gains, *refs):
    query_ref, key_ref, value_ref, gain_ref, *refs = refs
    landed, near_in, mid, far_in, send, receive, own = refs
    me = lax.axis_index("fsdp")
    place = lax.rem(me, TEAM)
    plane = lax.div(me, TEAM)
    others = [lax.rem(me + TEAM * k, planes * TEAM) for k in range(1, planes)]
    rows = landed.shape[1]

    def part(target):
        return x_ref.at[pl.ds(pl.multiple_of(target * rows, rows), rows)]

    keep = pltpu.make_async_copy(part(place), landed.at[place], own.at[0])
    keep.start()
    greet(me, range(1, TEAM), others)
    sender = Sender(send, receive)
    near = [
        sender(gains.at[flipped(place, m)], near_in.at[m - 1], flipped(me, m)) for m in SWAP_ORDER
    ]
    moves = [
        sender(part(flipped(place, m)), landed.at[place], flipped(me, m)) for m in SWAP_ORDER
    ]
    for copy in near:
        copy.wait_recv()
    summed = gains[place]
    for mask in range(1, TEAM):
        summed = summed + near_in[mask - 1]
    mid[...] = summed
    far = [
        sender(mid.at[lax.rem(plane + k + 1, planes)], far_in.at[k], other)
        for k, other in enumerate(others)
    ]
    for copy in moves:
        copy.wait_recv()
    keep.wait()
    at = 0
    for ref in (query_ref, key_ref, value_ref):
        part_width = ref.shape[1] // TEAM
        for q in range(TEAM):
            ref[:, q * part_width : (q + 1) * part_width] = landed[q, :, at : at + part_width]
        at += part_width
    for copy in far:
        copy.wait_recv()
    result = mid[plane]
    for k in range(planes - 1):
        result = result + far_in[k]
    gain_ref[...] = result
    sender.finish()


def closing(x, gains, rows, widths, planes, collective):
    links = 2 * (TEAM - 1) + planes - 1
    block = gains.shape[2:]
    vmem = pl.BlockSpec(memory_space=pltpu.VMEM)
    like = jax.ShapeDtypeStruct
    return pl.pallas_call(
        functools.partial(close_kernel, planes),
        out_shape=(*(like((rows, w), bf16) for w in widths), like(block, f32)),
        in_specs=[pl.BlockSpec(memory_space=pl.ANY), vmem],
        out_specs=(vmem,) * 4,
        scratch_shapes=[
            pltpu.VMEM((TEAM, rows, x.shape[1]), x.dtype),
            pltpu.VMEM((TEAM - 1, planes, *block), f32),
            pltpu.VMEM((planes, *block), f32),
            pltpu.VMEM((planes - 1, *block), f32),
            pltpu.SemaphoreType.DMA((links,)),
            pltpu.SemaphoreType.DMA((links,)),
            pltpu.SemaphoreType.DMA((2,)),
        ],
        compiler_params=params(collective, LIMIT),
    )(x, gains)


def visible_and_tables(ids_row, table):
    rows = ids_row.shape[1]
    row_at = lax.broadcasted_iota(jnp.int32, (rows, rows), 0)
    column_at = lax.broadcasted_iota(jnp.int32, (rows, rows), 1)
    ids_column = jnp.sum(jnp.where(row_at == column_at, ids_row, 0.0), axis=1, keepdims=True)
    visible = (ids_column == ids_row) & (column_at <= row_at)
    sequence = table.shape[0]
    place = jnp.sum(visible.astype(f32), axis=1, keepdims=True) - 1.0
    at = lax.broadcasted_iota(jnp.int32, (rows, sequence), 1).astype(f32)
    chosen = (at == place).astype(bf16)
    both = simple_product(chosen, table)
    width = 2 * HEAD_SIZE
    both = (both[:, :width] + both[:, width : 2 * width]) + both[:, 2 * width :]
    return visible, both[:, :HEAD_SIZE], both[:, HEAD_SIZE:]


def softmax(query, key, visible):
    scores = dot_last(query, key) * HEAD_SIZE ** (-0.5)
    scores = jnp.where(visible, scores, -1e30)
    expos = jnp.exp(scores - jnp.max(scores, axis=1, keepdims=True))
    return expos / jnp.sum(expos, axis=1, keepdims=True)


def by_step(*shape):
    return pl.BlockSpec(shape, lambda i: (i, *(0 for _ in shape[1:])))


def fixed(*shape):
    return pl.BlockSpec(shape, lambda i: tuple(0 for _ in shape))


def attend_kernel(
    planes, x_in, gain, weight, ids_row, table, query_gain, key_gain, right_in, tokens, cot_in, live,
    mlp_gain, _, normed_out, raw_out, turned_out, value_out, context_out, out, two, cot, units,
    x_ref, normed_ref, raw_ref, turned_ref, value_ref, context_ref, cot_own,
    mix, from_core, from_x, from_y, right, send, receive, own,
):
    me = lax.axis_index("fsdp")
    loader = Loader(own)
    steps = x_ref.shape[0] // STEP
    for i in range(steps):
        loader(rows_of(x_in, i, STEP), rows_of(x_ref, i, STEP))
    load_right = loader(right_in, right)
    cot_own[...] = cot_in[...] * live[...]
    keep = loader(cot_own, cot.at[lax.rem(me, TEAM)])
    greet(me, (1, 2, 4), line_peers(me, planes))
    sender = Sender(send, receive)
    line = Line(sender, units, planes, me)
    rows_cot = Gather(sender, cot_own, cot, me)
    line.start(0)
    rows_cot.start()
    heads = context_ref.shape[1] // HEAD_SIZE
    homes = []

    def attention(i):
        loader.copies[i].wait()
        here = slice(i * STEP, (i + 1) * STEP)
        x = x_ref[here].astype(f32)
        scale = lax.rsqrt(jnp.mean(x * x, axis=1, keepdims=True) + epsilon)
        normed = (x * scale * gain[...]).astype(bf16)
        normed_ref[here] = normed
        projected = simple_product(normed, weight[...])
        visible, cosine, sine = visible_and_tables(ids_row[i], table[...])
        raw_ref[here] = projected[:, : (heads + 1) * HEAD_SIZE]
        value = projected[:, (heads + 1) * HEAD_SIZE :].astype(bf16)
        value_ref[here] = value
        turned = []
        for h in range(heads + 1):
            at = slice(h * HEAD_SIZE, (h + 1) * HEAD_SIZE)
            raw = projected[:, at]
            head_gain = query_gain if h < heads else key_gain
            scale = lax.rsqrt(jnp.mean(raw * raw, axis=1, keepdims=True) + epsilon)
            y = raw * scale * head_gain[...]
            y = y * cosine + pltpu.roll(y, HEAD_SIZE // 2, 1) * sine
            turned.append(y.astype(bf16))
            turned_ref[here, at] = turned[-1]
        for h in range(heads):
            probs = softmax(turned[h], turned[heads], visible).astype(bf16)
            context = simple_product(probs, value)
            context_ref[here, h * HEAD_SIZE : (h + 1) * HEAD_SIZE] = context.astype(bf16)
        for ref, home in (
            (normed_ref, normed_out), (raw_ref, raw_out), (turned_ref, turned_out),
            (value_ref, value_out), (context_ref, context_out),
        ):
            homes.append(loader(rows_of(ref, i, STEP), rows_of(home, i, STEP)))

    for i in range(steps):
        attention(i)
        if i == steps // 2 - 1:
            rows_cot.forward()
    rows_cot.across()
    line.arrive(0)
    if planes > 2:
        line.start(1)
    load_right.wait()
    buffers = [mix, from_core, from_x, from_y]
    total = TeamSum(sender, me, out, buffers, [context_ref], [right], False)
    total.start()
    rows_cot.diagonal()
    total.own()
    total.relay()
    if planes > 2:
        line.arrive(1)
    if planes > 3:
        line.start(2)
    total.finish()

    @pl.loop(0, out.shape[0] // STRIP)
    def _(i):
        at = pl.ds(i * STRIP, STRIP)
        middle = tokens[at, :].astype(f32) + out[at, :]
        out[at, :] = middle
        scale = lax.rsqrt(jnp.mean(middle * middle, axis=1, keepdims=True) + epsilon)
        two[at, :] = (middle * scale * mlp_gain[...]).astype(bf16)

    rows_cot.arrive()
    if planes > 3:
        line.through(2, planes - 1)
    for step in range(min(2, planes - 1)):
        line.sent(step)
    sender.finish()
    for copy in (keep, *homes):
        copy.wait()


def attend(
    x, gain, weight, ids, table, query_gain, key_gain, right, tokens, cot, live, mlp_gain, units,
    planes, collective,
):
    rows, width = x.shape
    out = weight.shape[1]
    heads = out - 2 * HEAD_SIZE
    own_rows = tokens.shape[0]
    steps = rows // STEP
    like = jax.ShapeDtypeStruct
    anywhere = pl.BlockSpec(memory_space=pl.ANY)
    vmem = pl.BlockSpec(memory_space=pltpu.VMEM)
    kept = (
        like((rows, width), bf16),
        like((rows, heads + HEAD_SIZE), f32),
        like((rows, heads + HEAD_SIZE), bf16),
        like((rows, HEAD_SIZE), bf16),
        like((rows, heads), bf16),
    )
    links = SUM_COPIES + 14 + 2 * (planes - 1)
    return pl.pallas_call(
        functools.partial(attend_kernel, planes),
        out_shape=(
            *kept,
            like((own_rows, width), f32),
            like((own_rows, width), bf16),
            like((TEAM, own_rows, width), bf16),
            like(units.shape, bf16),
        ),
        in_specs=[anywhere] + [vmem] * 6 + [anywhere] + [vmem] * 4 + [anywhere],
        out_specs=(*([anywhere] * 5), vmem, vmem, anywhere, anywhere),
        input_output_aliases={12: 8},
        scratch_shapes=[
            pltpu.VMEM((rows, width), bf16),
            *(pltpu.VMEM(x.shape, x.dtype) for x in kept),
            pltpu.VMEM((own_rows, width), bf16),
            *sum_buffers(own_rows, width),
            pltpu.VMEM(right.shape, bf16),
            pltpu.SemaphoreType.DMA((links,)),
            pltpu.SemaphoreType.DMA((links,)),
            pltpu.SemaphoreType.DMA((6 * steps + 2,)),
        ],
        compiler_params=params(collective, LIMIT),
        cost_estimate=pl.CostEstimate(
            flops=2 * rows * width * (out + heads),
            bytes_accessed=8 * rows * width,
            transcendentals=0,
        ),
    )(
        x, gain, weight, ids, table, query_gain, key_gain, right, tokens, cot, live, mlp_gain, units
    )


def attend_back_kernel(planes, grad_in, out_weight, context, raw_in, turned_in, value_in, normed_in,
    ids_row, table, query_gain, key_gain, grad_raw_ref, weight_out, merged, grad_gains_ref, after,
    mine, there, sems,
    grad_ref, raw_ref, turned_ref, value_ref, normed_ref, out_sum, weight_sum, send, receive, own,
):
    me = lax.axis_index("fsdp")
    place = lax.rem(me, TEAM)
    team = me - place
    loader = Loader(own)
    loader(grad_in, grad_ref)
    for source, target in (
        (raw_in, raw_ref), (turned_in, turned_ref), (value_in, value_ref), (normed_in, normed_ref)
    ):
        loader(source, target)
    greet(me, range(1, TEAM), line_peers(me, planes))
    loader.copies[0].wait()

    total, width = grad_ref.shape
    heads = context.shape[1] // HEAD_SIZE
    out = weight_sum.shape[1]
    rows, block = weight_sum.shape[0] // planes, out_sum.shape[0] // planes
    cuts = width // out

    def source(k, c):
        return out_sum.at[pl.ds(k * block, block), pl.ds(c * out, out)]

    def target(k, c):
        return merged.at[k, pl.ds(c * block, block)]

    def outgoing(k, c):
        number = planes * place + k
        partner, there = lax.rem(number, TEAM), lax.div(number, TEAM)
        s, r = send.at[k * cuts + c], receive.at[there * cuts + c]
        over = remote(source(k, c), target(there, c), s, r, team + partner)
        here = pltpu.make_async_copy(source(k, c), target(there, c), own.at[5 + k * cuts + c])
        return partner, over, here

    def incoming(k, c):
        partner = lax.div(TEAM * k + place, planes)
        s, r = send.at[k * cuts + c], receive.at[k * cuts + c]
        return partner, remote(source(k, c), target(k, c), s, r, team + partner)

    for c in range(cuts):
        at = slice(c * out, (c + 1) * out)
        out_sum[:, at] = dot_first(context[...], grad_ref[:, at]).astype(bf16)
        for k in range(planes):
            partner, over, here = outgoing(k, c)
            pl.when(partner != place)(over.start)
            pl.when(partner == place)(here.start)

    grad_gains_ref[...] = jnp.zeros_like(grad_gains_ref)
    for copy in loader.copies[1:]:
        copy.wait()

    @pl.loop(0, total // STEP)
    def _(i):
        here = pl.ds(pl.multiple_of(i * STEP, STEP), STEP)
        grad_context = dot_last(grad_ref[here, :], out_weight[...]).astype(bf16)
        visible, cosine, sine = visible_and_tables(ids_row[i], table[...])
        value = value_ref[here, :]
        key = turned_ref[here, heads * HEAD_SIZE :]
        grads = []
        grad_value = 0.0
        grad_key = 0.0
        for h in range(heads):
            at = slice(h * HEAD_SIZE, (h + 1) * HEAD_SIZE)
            query = turned_ref[here, at]
            probs = softmax(query, key, visible)
            grad_value = grad_value + dot_first(probs.astype(bf16), grad_context[:, at])
            grad_probs = dot_last(grad_context[:, at], value)
            inner = jnp.sum(probs * grad_probs, axis=1, keepdims=True)
            grad_scores = (probs * (grad_probs - inner)).astype(bf16)
            grads.append(simple_product(grad_scores, key) * HEAD_SIZE ** (-0.5))
            grad_key = grad_key + dot_first(grad_scores, query) * HEAD_SIZE ** (-0.5)
        grads.append(grad_key)
        parts = []
        for h in range(heads + 1):
            raw = raw_ref[here, h * HEAD_SIZE : (h + 1) * HEAD_SIZE]
            head_gain = query_gain[...] if h < heads else key_gain[...]
            scale = lax.rsqrt(jnp.mean(raw * raw, axis=1, keepdims=True) + epsilon)
            turned = grads[h] * cosine + pltpu.roll(grads[h] * sine, HEAD_SIZE // 2, 1)
            row = 0 if h < heads else 1
            grad_gains_ref[row : row + 1, :] += jnp.sum(turned * raw * scale, axis=0, keepdims=True)
            turned = turned * head_gain
            mean = jnp.mean(turned * raw, axis=1, keepdims=True)
            parts.append((turned * scale - raw * (scale * scale * scale * mean)).astype(bf16))
        parts.append(grad_value.astype(bf16))
        grad_raw_ref[here, :] = jnp.concatenate(parts, axis=1)

    for k in range(planes):
        for c in range(cuts):
            partner, over, here = outgoing(k, c)
            pl.when(partner != place)(over.wait_send)
            pl.when(partner == place)(here.wait)
            partner, arriving = incoming(k, c)
            pl.when(partner != place)(arriving.wait_recv)
    sender = Sender(send, receive)
    sender.count = planes * cuts
    line = LineSum(sender, merged, None, after, mine, there, sems, planes, me, 0)
    line.start(0)

    @pl.loop(0, planes)
    def _(g):
        at = pl.ds(pl.multiple_of(g * rows, rows), rows)
        weight_sum[at, :] = dot_first(normed_ref[:, at], grad_raw_ref[...]).astype(bf16)

    homes = []
    for g in range(planes):
        copy = pltpu.make_async_copy(
            weight_sum.at[pl.ds(g * rows, rows)],
            weight_out.at[g],
            own.at[5 + planes * cuts + g],
        )
        copy.start()
        homes.append(copy)
    line.wait(0)
    for copy in homes:
        copy.wait()


def attend_back(
    grad, out_weight, context, raw, turned, value, normed, ids, table, query_gain, key_gain,
    planes, collective,
):
    rows, width = grad.shape
    heads = context.shape[1]
    out = heads + 2 * HEAD_SIZE
    by_plane = (planes, width // planes, out)
    merged = (planes, heads * width // out // planes, out)
    copies = planes * (width // out)
    anywhere = pl.BlockSpec(memory_space=pl.ANY)
    vmem = pl.BlockSpec(memory_space=pltpu.VMEM)
    like = jax.ShapeDtypeStruct
    return pl.pallas_call(
        functools.partial(attend_back_kernel, planes),
        out_shape=(
            like((rows, out), bf16),
            like(by_plane, bf16),
            like(merged, bf16),
            like((8, HEAD_SIZE), f32),
            like((1, 2, *merged[1:]), bf16),
        ),
        in_specs=[anywhere, vmem, vmem] + [anywhere] * 4 + [vmem] * 4,
        out_specs=(vmem, anywhere, anywhere, vmem, anywhere),
        scratch_shapes=[
            *line_scratch(*merged[1:]),
            *(pltpu.VMEM(x.shape, x.dtype) for x in (grad, raw, turned, value, normed)),
            pltpu.VMEM((heads, width), bf16),
            pltpu.VMEM((width, out), bf16),
            pltpu.SemaphoreType.DMA((copies + 2,)),
            pltpu.SemaphoreType.DMA((copies + 2,)),
            pltpu.SemaphoreType.DMA((5 + copies + planes,)),
        ],
        compiler_params=params(collective, LIMIT),
        cost_estimate=pl.CostEstimate(
            flops=2 * rows * width * (out + 2 * heads),
            bytes_accessed=8 * rows * width,
            transcendentals=0,
        ),
    )(grad, out_weight, context, raw, turned, value, normed, ids, table, query_gain, key_gain)


def hidden(two, weight):
    return simple_product(two, weight)


def hidden_grads(both, cot, down):
    units = both.shape[1] // 2
    gate, up = both[:, :units], both[:, units:]
    grad_act = dot_last(cot, down)
    sigma = 1.0 / (1.0 + jnp.exp(-gate))
    silu_gate = gate * sigma
    act = (silu_gate * up).astype(bf16)
    grad_gate = (grad_act * up * (sigma * (1.0 + gate * (1.0 - sigma)))).astype(bf16)
    grad_up = (grad_act * silu_gate).astype(bf16)
    return act, grad_gate, grad_up


def feed_kernel(
    planes, two_in, cot_in, weight_in, down_in, _, two_out, act_out, grad_both_out,
    weight_out, units_ref, two, cot, weight, down, both, weight_sum, act, grad_both, grad_weight,
    send, receive, own,
):
    me = lax.axis_index("fsdp")
    place = lax.rem(me, TEAM)
    loader = Loader(own)
    loader(two_in, two.at[place])
    loader(cot_in, cot)
    loader(weight_in, weight)
    loader(rows_of(down_in, 0, down.shape[0]), down)
    greet(me, (1, 2, 4), line_peers(me, planes))
    sender = Sender(send, receive)
    rows_two = Gather(sender, two_in, two, me)
    line = Line(sender, units_ref, planes, me)
    rows_two.start()
    line.start(0)
    rows, units = act.shape[1:]
    width = two.shape[2]

    crossed = {0: (0, 1), 2: (2, 4), 4: (3, 5), 6: (6, 7)}

    def chip_of(mask):
        return pl.ds(2 * lax.div(flipped(place, mask), 2), 2)

    def work(mask):
        for k in crossed[mask]:
            rows_two.late[k].wait_recv()
        chip = chip_of(mask)
        loader(two.at[chip], two_out.at[chip])
        both[...] = simple_product(two[chip].reshape(2 * rows, width), weight[...])
        flat = cot[chip].reshape(2 * rows, width)
        a, grad_gate, grad_up = hidden_grads(both[...], flat, down[...])
        act[chip] = a.reshape(2, rows, units)
        loader(act.at[chip], act_out.at[chip])
        grads = jnp.concatenate([grad_gate, grad_up], axis=1)
        grad_both[chip] = grads.reshape(2, rows, 2 * units)
        loader(grad_both.at[chip], grad_both_out.at[chip])
        for t in range(width // TILE):
            at = slice(t * TILE, (t + 1) * TILE)
            left = two[chip, :, at].reshape(2 * rows, TILE)
            term = dot_first(left, grads)
            if mask == 0:
                weight_sum[at, :] = term
            elif mask != 6:
                weight_sum[at, :] += term
            else:
                tile = pl.ds(t * TILE, TILE)
                grad_weight[at, :] = (weight_sum[at, :] + term).astype(bf16)
                loader(grad_weight.at[tile], weight_out.at[tile])

    rows_two.forward()
    loader.wait()
    work(0)
    rows_two.across()
    line.arrive(0)
    if planes > 2:
        line.start(1)
    work(2)
    rows_two.diagonal()
    work(4)
    if planes > 2:
        line.arrive(1)
    if planes > 3:
        line.start(2)
    work(6)
    if planes > 3:
        line.through(2, planes - 1)
    for step in range(min(2, planes - 1)):
        line.sent(step)
    sender.finish()
    for copy in loader.copies[4:]:
        copy.wait()


def feed(two, cot, weight, down, next_units, planes, collective):
    rows, width = two.shape
    units = weight.shape[1] // 2
    anywhere = pl.BlockSpec(memory_space=pl.ANY)
    like = jax.ShapeDtypeStruct
    return pl.pallas_call(
        functools.partial(feed_kernel, planes),
        out_shape=(
            like((TEAM, rows, width), bf16),
            like((TEAM, rows, units), bf16),
            like((TEAM, rows, 2 * units), bf16),
            like(weight.shape, bf16),
            like(next_units.shape, bf16),
        ),
        in_specs=[anywhere] * 5,
        out_specs=(anywhere,) * 5,
        input_output_aliases={4: 4},
        scratch_shapes=[
            pltpu.VMEM((TEAM, rows, width), bf16),
            pltpu.VMEM((TEAM, rows, width), bf16),
            pltpu.VMEM(weight.shape, bf16),
            pltpu.VMEM((units, width), bf16),
            pltpu.VMEM((2 * rows, 2 * units), f32),
            pltpu.VMEM(weight.shape, f32),
            pltpu.VMEM((TEAM, rows, units), bf16),
            pltpu.VMEM((TEAM, rows, 2 * units), bf16),
            pltpu.VMEM(weight.shape, bf16),
            pltpu.SemaphoreType.DMA((14 + 2 * (planes - 1),)),
            pltpu.SemaphoreType.DMA((14 + 2 * (planes - 1),)),
            pltpu.SemaphoreType.DMA((16 + width // TILE,)),
        ],
        compiler_params=params(collective, LIMIT),
        cost_estimate=pl.CostEstimate(
            flops=10 * TEAM * rows * width * units,
            bytes_accessed=8 * TEAM * rows * width,
            transcendentals=0,
        ),
    )(two, cot, weight, down, next_units)


def feed_rest_kernel(two, cot, weight, down, act, grad_both):
    blocks, rows, units = act.shape
    both = simple_product(two[...].reshape(blocks * rows, -1), weight[...])
    flat = cot[...].reshape(blocks * rows, -1)
    a, grad_gate, grad_up = hidden_grads(both, flat, down[...])
    act[...] = a.reshape(blocks, rows, units)
    grad_both[:, :, :units] = grad_gate.reshape(blocks, rows, units)
    grad_both[:, :, units:] = grad_up.reshape(blocks, rows, units)


def feed_rest(two, cot, weight, down, part):
    _, rows, width = two.shape
    units = weight.shape[1] // 2
    like = jax.ShapeDtypeStruct
    return pl.pallas_call(
        feed_rest_kernel,
        grid=(TEAM // 2,),
        out_shape=(like((TEAM, rows, units), bf16), like((TEAM, rows, 2 * units), bf16)),
        in_specs=[
            by_step(2, rows, width),
            by_step(2, rows, width),
            fixed(*weight.shape),
            pl.BlockSpec((units, width), lambda i: (part, 0)),
        ],
        out_specs=(by_step(2, rows, units), by_step(2, rows, 2 * units)),
        compiler_params=pltpu.CompilerParams(vmem_limit_bytes=LIMIT),
        cost_estimate=pl.CostEstimate(
            flops=6 * TEAM * rows * width * units,
            bytes_accessed=4 * TEAM * rows * width,
            transcendentals=0,
        ),
    )(two, cot, weight, down)


def local(
    devices,
    tokens,
    segments,
    micro_live,
    cotangent,
    w_query,
    key_weight,
    value_weight,
    w_output,
    attn_gain,
    query_norm_gain,
    key_gain,
    w_gate,
    w_up,
    w_down,
    mlp_gain,
):
    planes = devices // TEAM
    lines = [[place + TEAM * k for k in range(planes)] for place in range(TEAM)]
    slots, sequence = segments.shape
    token_count, width = tokens.shape
    groups = QUERY_HEADS // KEY_VALUE_HEADS
    rows = w_query.shape[0]
    parts = 2
    team_rows = TEAM * token_count
    head_width = groups * HEAD_SIZE
    me = lax.axis_index("fsdp")
    plane = me // TEAM

    def sum_line(x):
        return lax.psum_scatter(
            x, "fsdp", scatter_dimension=0, tiled=True, axis_index_groups=lines
        )

    slot_live = (lax.broadcasted_iota(jnp.int32, (slots, 1), 0) < micro_live[0]).astype(f32)
    row_live = jnp.broadcast_to(slot_live, (slots, sequence)).reshape(token_count, 1)

    smalls = [x[None] for x in (attn_gain, mlp_gain, query_norm_gain, key_gain)] + [segments]
    opened = opening(
        w_query,
        key_weight,
        value_weight,
        w_output,
        tokens,
        w_gate,
        w_up,
        w_down,
        smalls,
        planes,
        parts,
        1,
    )
    unit_slices, opened = opened[:parts], opened[parts:]
    qkv_weight, _, output_weight, team_tokens, down_weight = opened[:5]
    norm_gain, mlp_norm_gain, qgain, kgain, ids = opened[5:]
    mlp_norm_gain = mlp_norm_gain.reshape(width)
    qkv_weight = qkv_weight.reshape(width, -1)
    output_weight = output_weight.reshape(head_width, width)
    down_weight = down_weight.reshape(-1, width)
    table = jnp.asarray(rotation_tables(sequence))

    inputs = tokens.astype(f32)
    first, second = unit_slices
    team_normed, raw, turned, value_b, context_b, middle, normed_two, team_cot, first = attend(
        team_tokens.reshape(team_rows, width),
        norm_gain,
        qkv_weight,
        ids,
        table,
        qgain,
        kgain,
        output_weight,
        tokens,
        cotangent,
        row_live.astype(bf16),
        mlp_norm_gain.reshape(1, width),
        first,
        planes,
        2,
    )

    unit_weights = [first.reshape(width, -1)]
    team_two, act, grad_both, first_units, second = feed(
        normed_two, team_cot, unit_weights[0], down_weight, second, planes, 0
    )
    unit_weights.append(second.reshape(width, -1))
    acts, grads_both, grad_units = [act], [grad_both], [first_units]
    for k in range(1, parts):
        act, grad_both = feed_rest(team_two, team_cot, unit_weights[k], down_weight, k)
        acts.append(act)
        grads_both.append(grad_both)
    grad_normed_two, last_units = feed_back(team_two, grads_both, unit_weights, 4)
    grad_units = [sum_line(g) for g in (*grad_units, last_units)[:parts]]
    _, pull_two = jax.vjp(root_mean_square_norm, middle, mlp_norm_gain)
    middle_part, grad_mgain = pull_two(grad_normed_two)
    grad_middle = (cotangent * row_live.astype(bf16)).astype(f32) + middle_part
    team_grad, grad_down = gather_down(grad_middle.astype(bf16), team_cot, acts, 10)
    team_grad = team_grad.reshape(team_rows, width)
    grad_down = sum_line(grad_down)

    grad_qkv, grad_attention, out_blocks, grad_head_gains, out_line = attend_back(
        team_grad,
        output_weight,
        context_b,
        raw,
        turned,
        value_b,
        team_normed,
        ids,
        table,
        qgain,
        kgain,
        planes,
        6,
    )
    grad_attention = sum_line(grad_attention.reshape(-1, grad_attention.shape[2]))
    grad_normed, summed_out, grad_gate, grad_up, grad_output, _ = last_sums(
        grad_qkv.reshape(TEAM, token_count, -1),
        qkv_weight,
        acts,
        down_weight,
        [g.reshape(TEAM, rows, -1) for g in grad_units],
        out_blocks,
        out_line,
        planes,
        5,
    )
    grad_gate, grad_up = grad_gate.astype(f32), grad_up.astype(f32)
    _, pull_one = jax.vjp(root_mean_square_norm, inputs, norm_gain.reshape(width))
    input_part, grad_again = pull_one(grad_normed)
    grad_tokens = (grad_middle + input_part).astype(bf16)
    layer_out = (row_live * (middle + summed_out)).astype(bf16)

    def by_owner(vector):
        vector = vector.reshape(devices, -1)
        return jnp.pad(vector, ((0, 0), (0, 128 - vector.shape[1])))

    gains = jnp.stack(
        [by_owner(v) for v in (grad_again, grad_mgain, grad_head_gains[0], grad_head_gains[1])], axis=1
    )
    gains = jnp.pad(gains, ((0, 0), (0, 4), (0, 0)))
    gains = gains.reshape(planes, TEAM, 8, 128).transpose(1, 0, 2, 3)

    grad_attention, grad_gate, grad_up, layer_out, grad_tokens = lax.optimization_barrier(
        (grad_attention, grad_gate, grad_up, layer_out, grad_tokens)
    )
    grad_query, grad_key, grad_value_w, gains = closing(
        grad_attention,
        gains,
        rows,
        (w_query.shape[1], key_weight.shape[1], value_weight.shape[1]),
        planes,
        9,
    )
    attention_grads = tuple(
        g.astype(f32) for g in (grad_query, grad_key, grad_value_w, grad_output)
    )
    gains = (
        gains[0, : attn_gain.shape[0]],
        gains[2, : query_norm_gain.shape[0]],
        gains[3, : key_gain.shape[0]],
        gains[1, : mlp_gain.shape[0]],
    )
    grad_down, attention_grads, gains = lax.optimization_barrier(
        (grad_down, attention_grads, gains)
    )
    return (
        layer_out,
        grad_tokens,
        *attention_grads,
        *gains[:3],
        grad_gate,
        grad_up,
        grad_down.astype(f32),
        gains[3],
    )


def solution(mesh):
    by_rows, by_entry = P("fsdp", None), P("fsdp")
    return jax.shard_map(
        functools.partial(local, mesh.shape["fsdp"]),
        mesh=mesh,
        in_specs=(
            by_rows,
            by_rows,
            by_entry,
            by_rows,
            by_rows,
            by_rows,
            by_rows,
            by_rows,
            by_entry,
            by_entry,
            by_entry,
            by_rows,
            by_rows,
            by_rows,
            by_entry,
        ),
        out_specs=(
            by_rows,
            by_rows,
            by_rows,
            by_rows,
            by_rows,
            by_rows,
            by_entry,
            by_entry,
            by_entry,
            by_rows,
            by_rows,
            by_rows,
            by_entry,
        ),
        check_vma=False,
    )
```
